32 devices in a mesh: rep: 2 (over y), fsdp: 8 (over z, x), mp: 2 (over core).
Axes of the slice: x: 2, y: 2, z: 4, core: 2. Of those that a mesh axis runs over, the one named last changes fastest.
Arguments:
- noise_in: bfloat16 [1024, 3072], P(('rep', 'fsdp'), 'mp'), parts along dimension 0, may hold values from -6 to 6
- renoise: bfloat16 [1024, 3072], P(('rep', 'fsdp'), 'mp'), parts along dimension 0, may hold values from -6 to 6
- gen_step: int32 [16], P('rep'), parts along dimension 0, may hold values from 0 to 999
- noise_step: int32 [16], P('rep'), parts along dimension 0, may hold values from 0 to 999
- gen_weight: bfloat16 [3072, 3072], P('fsdp', 'mp'), may hold values from -0.109375 to 0.109375
- real_weight: bfloat16 [3072, 3072], P('fsdp', 'mp'), may hold values from -0.109375 to 0.109375
- fake_weight: bfloat16 [3072, 3072], P('fsdp', 'mp'), may hold values from -0.109375 to 0.109375
- gen_embed: bfloat16 [128, 3072], replicated, may hold values from -0.5 to 0.5
- real_embed: bfloat16 [128, 3072], replicated, may hold values from -0.5 to 0.5
- fake_embed: bfloat16 [128, 3072], replicated, may hold values from -0.5 to 0.5
- gen_gain: float32 [3072], replicated, may hold values from 0.1 to 1.9
- real_gain: float32 [3072], replicated, may hold values from 0.1 to 1.9
- fake_gain: float32 [3072], replicated, may hold values from 0.1 to 1.9
Outputs:
- noised: bfloat16 [1024, 3072], P(('rep', 'fsdp'), 'mp'), parts along dimension 0
- latent_grad: bfloat16 [1024, 3072], P(('rep', 'fsdp'), 'mp'), parts along dimension 0
- gain_grad: float32 [6144], P(('rep', 'fsdp', 'mp')), parts along dimension 0
The draws below stay inside these ranges and needn't reach their ends.
There are 2 independent parts, one for each index of `rep`. The reference program is written for one: setup_inputs(seed, part) draws one part's arguments, and reference() takes and returns one part's arrays. A program takes and returns all parts, laid end to end along the dimension named above; an argument that names none is the same for every part. Nothing has to cross between parts.
All inputs are finite; a program needn't handle non-finite values.
Results may differ from the reference program's by a relative error of at most 0.0066.
Values may be sent and summed in bfloat16 or wider, within the bound.
No kernel may reach another device: no remote copies, remote signals or barrier semaphores. Data moves between devices by JAX's collectives and lax.ppermute only.
A program may use at most 128 MiB of HBM per device.

```python
import math
import jax
import jax.numpy as jnp
from jax import lax

D = 3072
TF = 128
NT = 1000
TOK_DEV = 64
NBLK = 8
TOKENS = 512


def with_ends(array, rng, smallest, top_value):
    longest = array.shape.index(max(array.shape))
    spots = []
    for shift in (0, 1):
        where = [jax.random.randint(jax.random.fold_in(rng, axis), (), 0, length) for axis, length in enumerate(array.shape)]
        where[longest] = (where[longest] + shift) % array.shape[longest]
        spots.append(tuple(where))
    return array.at[spots[0]].set(smallest).at[spots[1]].set(top_value)


def steps_of(stream_key, extent, split, low, top_value):
    def one(position, shards_of):
        steps = jax.random.uniform(jax.random.fold_in(jax.random.fold_in(stream_key, 6), position), (shards_of,), jnp.float32, low / len(split), top_value / len(split))
        return jnp.repeat(jnp.exp(steps), extent[position] // shards_of).reshape((-1,) + (1,) * (len(extent) - position - 1))

    gain = one(*split[0])
    for cut in split[1:]:
        gain = gain * one(*cut)
    return gain


def noise(own_key, extent, scale, limit, shards=(), held_as=jnp.bfloat16):
    gain = steps_of(own_key, extent, shards, -0.22, 0.18) if shards else 1.0
    result = jax.random.normal(own_key, extent, jnp.float32) * scale * gain
    return jnp.minimum(jnp.maximum(result, -limit), limit).astype(held_as)


def setup_inputs(seed: int = 0, part: int = 0) -> dict:
    splits = jax.random.split(jax.random.key(seed), 14)
    part_splits = jax.random.split(jax.random.fold_in(splits[13], part), 14)
    return {
        "noise_in": noise(part_splits[0], (TOKENS, D), 1.0, 6.0, ((0, 8), (1, 2))),
        "renoise": noise(part_splits[1], (TOKENS, D), 1.0, 6.0, ((0, 8), (1, 2))),
        "gen_step": with_ends(jax.random.randint(part_splits[2], (NBLK,), 0, NT), jax.random.fold_in(part_splits[2], 1), 0, NT - 1).astype(jnp.int32),
        "noise_step": with_ends(jax.random.randint(part_splits[3], (NBLK,), 0, NT), jax.random.fold_in(part_splits[3], 1), 0, NT - 1).astype(jnp.int32),
        "gen_weight": noise(splits[4], (D, D), D ** -0.5, 0.109375, ((0, 8), (1, 2))),
        "real_weight": noise(splits[5], (D, D), D ** -0.5, 0.109375, ((0, 8), (1, 2))),
        "fake_weight": noise(splits[6], (D, D), D ** -0.5, 0.109375, ((0, 8), (1, 2))),
        "gen_embed": noise(splits[7], (TF, D), TF ** -0.5, 0.5),
        "real_embed": noise(splits[8], (TF, D), TF ** -0.5, 0.5),
        "fake_embed": noise(splits[9], (TF, D), TF ** -0.5, 0.5),
        "gen_gain": jnp.clip(1.0 + 0.18 * jax.random.normal(splits[10], (D,), jnp.float32), 0.1, 1.9),
        "real_gain": jnp.clip(1.0 + 0.18 * jax.random.normal(splits[11], (D,), jnp.float32), 0.1, 1.9),
        "fake_gain": jnp.clip(1.0 + 0.18 * jax.random.normal(splits[12], (D,), jnp.float32), 0.1, 1.9),
    }


def step_features(step_ids):
    half_width = TF // 2
    frequency = jnp.exp(-math.log(10000.0) * jnp.arange(half_width, dtype=jnp.float32) / half_width)
    angles = step_ids.astype(jnp.float32)[:, None] * frequency[None, :]
    return jnp.concatenate([jnp.cos(angles), jnp.sin(angles)], axis=1).astype(jnp.bfloat16)

def modulate(full_rows, gain_vec, modulation):
    values = full_rows.astype(jnp.float32)
    normed = values * lax.rsqrt(lax.optimization_barrier(jnp.mean(values * values, axis=1, keepdims=True)) + 1e-06)
    lifted = normed.reshape(NBLK, TOK_DEV, D) * gain_vec * (1.0 + modulation[:, None, :])
    return (normed, lifted.reshape(TOKENS, D).astype(jnp.bfloat16))

def reference(noise_in, renoise, gen_step, noise_step, gen_weight, real_weight, fake_weight, gen_embed, real_embed, fake_embed, gen_gain, real_gain, fake_gain):
    gen_mod = jnp.dot(step_features(gen_step), gen_embed, preferred_element_type=jnp.float32)
    noise_feat = step_features(noise_step)
    real_mod = jnp.dot(noise_feat, real_embed, preferred_element_type=jnp.float32)
    fake_mod = jnp.dot(noise_feat, fake_embed, preferred_element_type=jnp.float32)
    shares = ((noise_step.astype(jnp.float32) + 1.0) / (NT + 1.0))[:, None, None]
    normed, lifted = modulate(noise_in, gen_gain, gen_mod)
    generated = noise_in.astype(jnp.float32) + jnp.dot(lifted, gen_weight, preferred_element_type=jnp.float32)
    blended = (1.0 - shares) * generated.reshape(NBLK, TOK_DEV, D) + shares * renoise.astype(jnp.float32).reshape(NBLK, TOK_DEV, D)
    noised = blended.reshape(TOKENS, D).astype(jnp.bfloat16)
    real_normed, real_lift = modulate(noised, real_gain, real_mod)
    real_pred = jnp.dot(real_lift, real_weight, preferred_element_type=jnp.float32).astype(jnp.bfloat16)
    fake_normed, fake_lift = modulate(noised, fake_gain, fake_mod)
    fake_pred = jnp.dot(fake_lift, fake_weight, preferred_element_type=jnp.float32).astype(jnp.bfloat16)
    difference = real_pred.astype(jnp.float32) - fake_pred.astype(jnp.float32)
    latent_grad = (shares * difference.reshape(NBLK, TOK_DEV, D)).reshape(TOKENS, D).astype(jnp.bfloat16)
    backward = jnp.dot(latent_grad, gen_weight.T, preferred_element_type=jnp.float32)
    scaled = (backward.reshape(NBLK, TOK_DEV, D) * (1.0 + gen_mod[:, None, :])).reshape(TOKENS, D)
    gain_grad = lax.optimization_barrier(jnp.sum(scaled * normed, axis=0)) / TOK_DEV
    return (noised, latent_grad, gain_grad)
```

```python
import math

import jax
import jax.numpy as jnp
from jax import lax
from jax.sharding import PartitionSpec as P

NT = 1000


norm_epsilon = 1e-06


def from_behind(value, axis, by):
    size = lax.axis_size(axis)
    pairs = [(i, i + by) for i in range(size) if 0 <= i + by < size]
    return lax.ppermute(value, axis, pairs)


def shifted(value, axis, by):
    size = lax.axis_size(axis)
    return lax.ppermute(value, axis, [(i, (i + by) % size) for i in range(size)])


def step_features(step_ids, feature_width):
    half_width = feature_width // 2
    frequency = jnp.exp(-math.log(10000.0) * jnp.arange(half_width, dtype=jnp.float32) / half_width)
    angles = step_ids.astype(jnp.float32)[:, None] * frequency[None, :]
    return jnp.concatenate([jnp.cos(angles), jnp.sin(angles)], axis=1).astype(jnp.bfloat16)


def lookup(step_table, block_ids):
    matches = block_ids[:, None] == jnp.arange(step_table.shape[0], dtype=jnp.int32)[None, :]
    return jnp.sum(jnp.where(matches, step_table[None, :], 0), axis=1)


def block_shares(step_ids):
    return ((step_ids.astype(jnp.float32) + 1.0) / (NT + 1.0))[:, None, None]


def modulate(full_rows, gain_vec, modulation):
    blocks = modulation.shape[0]
    values = full_rows.astype(jnp.float32)
    normed = values * lax.rsqrt(jnp.mean(values * values, axis=1, keepdims=True) + norm_epsilon)
    lifted = normed.reshape(blocks, -1, values.shape[1]) * gain_vec * (1.0 + modulation[:, None, :])
    return (normed, lifted.reshape(values.shape).astype(jnp.bfloat16))


def on_groups(
    noise_in,
    renoise,
    gen_step,
    noise_step,
    gen_weight,
    real_weight,
    fake_weight,
    gen_embed,
    real_embed,
    fake_embed,
    gen_gain,
    real_gain,
    fake_gain,
):
    devices = lax.axis_size("fsdp")
    quarter = devices // 4
    half = 2 * quarter
    position = lax.axis_index("fsdp")
    block_rows = noise_in.shape[0]
    half_width = noise_in.shape[1]
    model_width = gen_gain.shape[0]
    feature_width = gen_embed.shape[0]
    slice_rows = 4 * block_rows // devices
    group_role = (position >= quarter).astype(jnp.int32) + (position >= half).astype(jnp.int32)
    in_generator = group_role == 2
    slot_ids = jnp.arange(devices, dtype=jnp.int32)
    slot_role = (
        (slot_ids >= quarter).astype(jnp.int32) + (slot_ids >= half).astype(jnp.int32)
    ).reshape(devices, 1, 1)
    outgoing = jnp.where(
        slot_role == 2,
        gen_weight[None],
        jnp.where(slot_role == 0, real_weight[None], fake_weight[None]),
    )
    received = lax.all_to_all(outgoing, "fsdp", split_axis=0, concat_axis=0, tiled=True)
    weight_mine = received.reshape(model_width, half_width)
    embed_mine = jnp.where(
        group_role == 2, gen_embed, jnp.where(group_role == 0, real_embed, fake_embed)
    )
    gain_mine = jnp.where(
        group_role == 2, gen_gain, jnp.where(group_role == 0, real_gain, fake_gain)
    )
    partner_noise, partner_renoise = from_behind((noise_in, renoise), "fsdp", half)
    gen_ids = jnp.stack([position, (position + half) % devices])
    gen_mod = jnp.dot(
        step_features(lookup(gen_step, gen_ids), feature_width),
        embed_mine,
        preferred_element_type=jnp.float32,
    )
    gen_shares = block_shares(lookup(noise_step, gen_ids))
    gen_rows = jnp.concatenate([noise_in, partner_noise], axis=0)
    gen_noise = jnp.concatenate([renoise, partner_renoise], axis=0)
    gen_full = lax.all_gather(gen_rows, "mp", axis=1, tiled=True)

    def generate(operands):
        full_rows, own_rows, fresh_noise = operands
        normed, lifted = modulate(full_rows, gain_mine, gen_mod)
        latents = own_rows.astype(jnp.float32) + jnp.dot(
            lifted, weight_mine, preferred_element_type=jnp.float32
        )
        blended = (1.0 - gen_shares) * latents.reshape(
            2, block_rows, half_width
        ) + gen_shares * fresh_noise.astype(jnp.float32).reshape(2, block_rows, half_width)
        return (blended.reshape(2 * block_rows, half_width).astype(jnp.bfloat16), normed)

    def skip_generate(operands):
        return (
            jnp.zeros((2 * block_rows, half_width), jnp.bfloat16),
            jnp.zeros((2 * block_rows, model_width), jnp.float32),
        )

    gen_noised, gen_normed = lax.cond(
        in_generator, generate, skip_generate, (gen_full, gen_rows, gen_noise)
    )
    width_now = gen_noised.shape[1]
    pieces = (
        gen_noised.reshape(2, quarter, slice_rows, width_now)
        .transpose(1, 0, 2, 3)
        .reshape(quarter, 2 * slice_rows, width_now)
    )
    send_rows = jnp.concatenate(
        [pieces, pieces, jnp.zeros((half, 2 * slice_rows, width_now), jnp.bfloat16)], axis=0
    )
    arrived = lax.all_to_all(send_rows, "fsdp", split_axis=0, concat_axis=0, tiled=True)
    score_rows = arrived[half:].reshape(2 * half * slice_rows, width_now)
    gen_slots = jnp.arange(half, dtype=jnp.int32)
    score_ids = jnp.stack([gen_slots + half, gen_slots], axis=1).reshape(2 * half)
    score_mod = jnp.dot(
        step_features(lookup(noise_step, score_ids), feature_width),
        embed_mine,
        preferred_element_type=jnp.float32,
    )
    score_full = lax.all_gather(score_rows, "mp", axis=1, tiled=True)

    def assess(full_rows):
        normed, lifted = modulate(full_rows, gain_mine, score_mod)
        return jnp.dot(lifted, weight_mine, preferred_element_type=jnp.float32).astype(jnp.bfloat16)

    def skip_assess(full_rows):
        return jnp.zeros((2 * half * slice_rows, half_width), jnp.bfloat16)

    prediction = lax.cond(in_generator, skip_assess, assess, score_full)
    grouped = prediction.reshape(half, 2, slice_rows, half_width)
    by_owner = jnp.concatenate([grouped[:, 1], grouped[:, 0]], axis=0)
    returned = lax.all_to_all(by_owner, "fsdp", split_axis=0, concat_axis=0, tiled=True)
    real_block = returned[:quarter].reshape(block_rows, half_width).astype(jnp.float32)
    fake_block = returned[quarter:half].reshape(block_rows, half_width).astype(jnp.float32)
    own_share = block_shares(lookup(noise_step, position[None]))[0]
    own_grad = (own_share * (real_block - fake_block)).astype(jnp.bfloat16)
    handed = jnp.where(in_generator, gen_noised[block_rows:], own_grad)
    taken = shifted(handed, "fsdp", half)

    def reverse(operands):
        grad_rows, normed = operands
        backward = lax.dot_general(
            grad_rows, weight_mine, (((1,), (1,)), ((), ())), preferred_element_type=jnp.float32
        )
        scaled = backward.reshape(2, block_rows, model_width) * (1.0 + gen_mod[:, None, :])
        return jnp.sum(scaled.reshape(2 * block_rows, model_width) * normed, axis=0) / block_rows

    def skip_reverse(operands):
        return jnp.zeros((model_width,), jnp.float32)

    grad_rows = jnp.concatenate([own_grad, taken], axis=0)
    gain_term = lax.cond(in_generator, reverse, skip_reverse, (grad_rows, gen_normed))
    gain_grad = lax.psum_scatter(gain_term, ("fsdp", "mp"), scatter_dimension=0, tiled=True)
    noised_out = jnp.where(in_generator, gen_noised[:block_rows], taken)
    return (noised_out, own_grad, gain_grad)


def on_tiles(
    noise_in,
    renoise,
    gen_step,
    noise_step,
    gen_weight,
    real_weight,
    fake_weight,
    gen_embed,
    real_embed,
    fake_embed,
    gen_gain,
    real_gain,
    fake_gain,
):
    g = lax.axis_size("fsdp") // 2
    position, c = lax.axis_index("fsdp"), lax.axis_index("mp")
    s, q = position // g, position % g
    r, h = noise_in.shape
    d = 2 * h
    w = h // g
    feature_width = gen_embed.shape[0]
    f32, bf16 = jnp.float32, jnp.bfloat16
    both = ("fsdp", "mp")
    near = [q ^ k for k in range(g)]

    def flat(s_, q_, c_):
        return (s_ * g + q_) * 2 + c_

    every = [(s_, q_, c_) for s_ in (0, 1) for q_ in range(g) for c_ in (0, 1)]

    def in_square(value, k):
        return lax.ppermute(value, "fsdp", [(i, i ^ k) for i in range(2 * g)])

    def across(value):
        return lax.ppermute(value, "fsdp", [(i, i ^ g) for i in range(2 * g)])

    def cores(value):
        return lax.ppermute(value, "mp", [(0, 1), (1, 0)])

    def turned(value):
        moved = lax.ppermute(value, both, [(flat(*i), flat(i[2], i[1], i[0])) for i in every if i[0] != i[2]])
        return jnp.where(s == c, value, moved)

    def piece(array, k):
        return lax.dynamic_slice_in_dim(array, near[k] * w, w, 1)

    def relative(array):
        return jnp.concatenate([piece(array, k) for k in range(g)], axis=1)

    def regroup(array, k, axis):
        parts = jnp.split(array, g, axis)
        return jnp.concatenate([parts[j ^ k] for j in range(g)], axis)

    def mine(vector):
        half = lax.dynamic_slice_in_dim(vector, s * h, h, vector.ndim - 1)
        return relative(half.reshape(-1, h))

    def spread(weight):
        return jnp.concatenate([piece(weight, 0)] + [in_square(piece(weight, k), k) for k in range(1, g)], axis=0)

    ids = c * g + jnp.stack(near)

    def modulation(steps, embed):
        return 1.0 + jnp.dot(step_features(lookup(steps, ids), feature_width), mine(embed), preferred_element_type=f32)

    def lifted(values, scale):
        return (values.astype(f32).reshape(g, r, -1) * scale[:, None, :]).astype(bf16).reshape(g * r, -1)

    shares = jnp.repeat(block_shares(lookup(noise_step, ids)).reshape(g, 1), r, axis=0)

    gen_own = spread(gen_weight)
    x_turned = turned(relative(noise_in))
    fresh_turned = turned(relative(renoise))
    x = jnp.concatenate([x_turned] + [regroup(in_square(x_turned, k), k, 1) for k in range(1, g)], axis=0)
    fresh = jnp.concatenate(
        [fresh_turned[:, :w]] + [in_square(fresh_turned[:, k * w : (k + 1) * w], k) for k in range(1, g)], axis=0
    )
    gen_other = cores(gen_own)
    gen_tile = jnp.concatenate([gen_own, gen_other], axis=1)

    def row_sums(values):
        wide = values.astype(f32)
        return jnp.sum(wide * wide, axis=1, keepdims=True)

    def row_scale(partial):
        total = partial + across(partial.reshape(g, r)).reshape(g * r, 1)
        return lax.rsqrt(total / d + norm_epsilon)

    gen_scale = modulation(gen_step, gen_embed)
    x_scale = row_scale(row_sums(x))
    product = jnp.dot(lifted(x, gen_scale * mine(gen_gain)), gen_tile, preferred_element_type=f32)
    keep = jnp.where(s == c, product[:, :w], product[:, w:])
    away = jnp.where(s == c, product[:, w:], product[:, :w]).astype(bf16)
    latents = x[:, :w].astype(f32) + x_scale * (keep + across(away).astype(f32))
    noised_piece = ((1.0 - shares) * latents + shares * fresh.astype(f32)).astype(bf16)

    real_own, fake_own = spread(real_weight), spread(fake_weight)
    score_tile = jnp.concatenate([real_own, fake_own], axis=0)
    score_other = cores(score_tile)
    noised = jnp.concatenate(
        [noised_piece] + [regroup(in_square(noised_piece, k), k, 0) for k in range(1, g)], axis=1
    )
    noised_scale = row_scale(row_sums(noised))
    lifts = jnp.concatenate(
        [
            lifted(noised, modulation(noise_step, real_embed) * mine(real_gain)),
            lifted(noised, -(modulation(noise_step, fake_embed) * mine(fake_gain))),
        ],
        axis=1,
    )
    gap = jnp.concatenate(
        [
            jnp.dot(lifts, score_tile, preferred_element_type=f32),
            jnp.dot(lifts, score_other, preferred_element_type=f32),
        ],
        axis=1,
    )
    gap = gap + across(gap.astype(bf16)).astype(f32)
    grad = (shares * noised_scale * gap).astype(bf16)

    def absolute(array):
        return relative(array)

    def owners(value, k):
        return lax.ppermute(value, both, [(flat(a, q_, a), flat(a, q_ ^ k, a)) for a in (0, 1) for q_ in range(g)])

    owned = [grad[:r]] + [owners(grad[k * r : (k + 1) * r], k) for k in range(1, g)]
    owned_here = jnp.concatenate([o[:, :w] for o in owned], axis=1)
    owned_there = jnp.concatenate([o[:, w:] for o in owned], axis=1)
    latent_grad = absolute(jnp.where(s == c, owned_here, cores(owned_there)))
    noised_out = absolute(turned(noised[:r]))

    backward = lax.dot_general(grad, gen_tile, (((1,), (1,)), ((), ())), preferred_element_type=f32)
    terms = (backward.reshape(g, r, h) * gen_scale[:, None, :]).reshape(g * r, h) * (x.astype(f32) * x_scale)
    sums = (jnp.sum(terms, axis=0) / r).reshape(g, 2, w // 2)
    here = lax.dynamic_index_in_dim(sums, c, 1, False)
    there = lax.dynamic_index_in_dim(sums, 1 - c, 1, False)
    here = here + cores(there)
    gain_grad = here[0]
    for k in range(1, g):
        gain_grad = gain_grad + in_square(here[k], k)
    return (noised_out, latent_grad, gain_grad)


def solution(mesh):
    positions = mesh.shape["fsdp"]
    on_device = on_tiles if positions in (4, 8, 16) and mesh.shape["mp"] == 2 else on_groups
    return jax.shard_map(
        on_device,
        mesh=mesh,
        in_specs=(
            P(("rep", "fsdp"), "mp"),
            P(("rep", "fsdp"), "mp"),
            P("rep"),
            P("rep"),
            P("fsdp", "mp"),
            P("fsdp", "mp"),
            P("fsdp", "mp"),
            P(),
            P(),
            P(),
            P(),
            P(),
            P(),
        ),
        out_specs=(P(("rep", "fsdp"), "mp"), P(("rep", "fsdp"), "mp"), P(("rep", "fsdp", "mp"))),
        check_vma=False,
    )
```

```python
import math

import jax
import jax.numpy as jnp
from jax import lax
from jax.experimental import pallas as pl
from jax.experimental.pallas import tpu as pltpu
from jax.sharding import PartitionSpec as P

NT = 1000


norm_epsilon = 1e-06


def from_behind(value, axis, by):
    size = lax.axis_size(axis)
    pairs = [(i, i + by) for i in range(size) if 0 <= i + by < size]
    return lax.ppermute(value, axis, pairs)


def shifted(value, axis, by):
    size = lax.axis_size(axis)
    return lax.ppermute(value, axis, [(i, (i + by) % size) for i in range(size)])


def step_features(step_ids, feature_width):
    half_width = feature_width // 2
    frequency = jnp.exp(-math.log(10000.0) * jnp.arange(half_width, dtype=jnp.float32) / half_width)
    angles = step_ids.astype(jnp.float32)[:, None] * frequency[None, :]
    return jnp.concatenate([jnp.cos(angles), jnp.sin(angles)], axis=1).astype(jnp.bfloat16)


def lookup(step_table, block_ids):
    matches = block_ids[:, None] == jnp.arange(step_table.shape[0], dtype=jnp.int32)[None, :]
    return jnp.sum(jnp.where(matches, step_table[None, :], 0), axis=1)


def block_shares(step_ids):
    return ((step_ids.astype(jnp.float32) + 1.0) / (NT + 1.0))[:, None, None]


def modulate(full_rows, gain_vec, modulation):
    blocks = modulation.shape[0]
    values = full_rows.astype(jnp.float32)
    normed = values * lax.rsqrt(jnp.mean(values * values, axis=1, keepdims=True) + norm_epsilon)
    lifted = normed.reshape(blocks, -1, values.shape[1]) * gain_vec * (1.0 + modulation[:, None, :])
    return (normed, lifted.reshape(values.shape).astype(jnp.bfloat16))


def on_groups(
    noise_in,
    renoise,
    gen_step,
    noise_step,
    gen_weight,
    real_weight,
    fake_weight,
    gen_embed,
    real_embed,
    fake_embed,
    gen_gain,
    real_gain,
    fake_gain,
):
    devices = lax.axis_size("fsdp")
    quarter = devices // 4
    half = 2 * quarter
    position = lax.axis_index("fsdp")
    block_rows = noise_in.shape[0]
    half_width = noise_in.shape[1]
    model_width = gen_gain.shape[0]
    feature_width = gen_embed.shape[0]
    slice_rows = 4 * block_rows // devices
    group_role = (position >= quarter).astype(jnp.int32) + (position >= half).astype(jnp.int32)
    in_generator = group_role == 2
    slot_ids = jnp.arange(devices, dtype=jnp.int32)
    slot_role = (
        (slot_ids >= quarter).astype(jnp.int32) + (slot_ids >= half).astype(jnp.int32)
    ).reshape(devices, 1, 1)
    outgoing = jnp.where(
        slot_role == 2,
        gen_weight[None],
        jnp.where(slot_role == 0, real_weight[None], fake_weight[None]),
    )
    received = lax.all_to_all(outgoing, "fsdp", split_axis=0, concat_axis=0, tiled=True)
    weight_mine = received.reshape(model_width, half_width)
    embed_mine = jnp.where(
        group_role == 2, gen_embed, jnp.where(group_role == 0, real_embed, fake_embed)
    )
    gain_mine = jnp.where(
        group_role == 2, gen_gain, jnp.where(group_role == 0, real_gain, fake_gain)
    )
    partner_noise, partner_renoise = from_behind((noise_in, renoise), "fsdp", half)
    gen_ids = jnp.stack([position, (position + half) % devices])
    gen_mod = jnp.dot(
        step_features(lookup(gen_step, gen_ids), feature_width),
        embed_mine,
        preferred_element_type=jnp.float32,
    )
    gen_shares = block_shares(lookup(noise_step, gen_ids))
    gen_rows = jnp.concatenate([noise_in, partner_noise], axis=0)
    gen_noise = jnp.concatenate([renoise, partner_renoise], axis=0)
    gen_full = lax.all_gather(gen_rows, "mp", axis=1, tiled=True)

    def generate(operands):
        full_rows, own_rows, fresh_noise = operands
        normed, lifted = modulate(full_rows, gain_mine, gen_mod)
        latents = own_rows.astype(jnp.float32) + jnp.dot(
            lifted, weight_mine, preferred_element_type=jnp.float32
        )
        blended = (1.0 - gen_shares) * latents.reshape(
            2, block_rows, half_width
        ) + gen_shares * fresh_noise.astype(jnp.float32).reshape(2, block_rows, half_width)
        return (blended.reshape(2 * block_rows, half_width).astype(jnp.bfloat16), normed)

    def skip_generate(operands):
        return (
            jnp.zeros((2 * block_rows, half_width), jnp.bfloat16),
            jnp.zeros((2 * block_rows, model_width), jnp.float32),
        )

    gen_noised, gen_normed = lax.cond(
        in_generator, generate, skip_generate, (gen_full, gen_rows, gen_noise)
    )
    width_now = gen_noised.shape[1]
    pieces = (
        gen_noised.reshape(2, quarter, slice_rows, width_now)
        .transpose(1, 0, 2, 3)
        .reshape(quarter, 2 * slice_rows, width_now)
    )
    send_rows = jnp.concatenate(
        [pieces, pieces, jnp.zeros((half, 2 * slice_rows, width_now), jnp.bfloat16)], axis=0
    )
    arrived = lax.all_to_all(send_rows, "fsdp", split_axis=0, concat_axis=0, tiled=True)
    score_rows = arrived[half:].reshape(2 * half * slice_rows, width_now)
    gen_slots = jnp.arange(half, dtype=jnp.int32)
    score_ids = jnp.stack([gen_slots + half, gen_slots], axis=1).reshape(2 * half)
    score_mod = jnp.dot(
        step_features(lookup(noise_step, score_ids), feature_width),
        embed_mine,
        preferred_element_type=jnp.float32,
    )
    score_full = lax.all_gather(score_rows, "mp", axis=1, tiled=True)

    def assess(full_rows):
        normed, lifted = modulate(full_rows, gain_mine, score_mod)
        return jnp.dot(lifted, weight_mine, preferred_element_type=jnp.float32).astype(jnp.bfloat16)

    def skip_assess(full_rows):
        return jnp.zeros((2 * half * slice_rows, half_width), jnp.bfloat16)

    prediction = lax.cond(in_generator, skip_assess, assess, score_full)
    grouped = prediction.reshape(half, 2, slice_rows, half_width)
    by_owner = jnp.concatenate([grouped[:, 1], grouped[:, 0]], axis=0)
    returned = lax.all_to_all(by_owner, "fsdp", split_axis=0, concat_axis=0, tiled=True)
    real_block = returned[:quarter].reshape(block_rows, half_width).astype(jnp.float32)
    fake_block = returned[quarter:half].reshape(block_rows, half_width).astype(jnp.float32)
    own_share = block_shares(lookup(noise_step, position[None]))[0]
    own_grad = (own_share * (real_block - fake_block)).astype(jnp.bfloat16)
    handed = jnp.where(in_generator, gen_noised[block_rows:], own_grad)
    taken = shifted(handed, "fsdp", half)

    def reverse(operands):
        grad_rows, normed = operands
        backward = lax.dot_general(
            grad_rows, weight_mine, (((1,), (1,)), ((), ())), preferred_element_type=jnp.float32
        )
        scaled = backward.reshape(2, block_rows, model_width) * (1.0 + gen_mod[:, None, :])
        return jnp.sum(scaled.reshape(2 * block_rows, model_width) * normed, axis=0) / block_rows

    def skip_reverse(operands):
        return jnp.zeros((model_width,), jnp.float32)

    grad_rows = jnp.concatenate([own_grad, taken], axis=0)
    gain_term = lax.cond(in_generator, reverse, skip_reverse, (grad_rows, gen_normed))
    gain_grad = lax.psum_scatter(gain_term, ("fsdp", "mp"), scatter_dimension=0, tiled=True)
    noised_out = jnp.where(in_generator, gen_noised[:block_rows], taken)
    return (noised_out, own_grad, gain_grad)


def on_tiles(
    noise_in,
    renoise,
    gen_step,
    noise_step,
    gen_weight,
    real_weight,
    fake_weight,
    gen_embed,
    real_embed,
    fake_embed,
    gen_gain,
    real_gain,
    fake_gain,
):
    g = lax.axis_size("fsdp") // 2
    r, h = noise_in.shape
    d = 2 * h
    w = h // g
    t = g * r
    blocks = gen_step.shape[0]
    f32, bf16 = jnp.float32, jnp.bfloat16
    tail = 16
    span = range(g)

    def place():
        position, c = lax.axis_index("fsdp"), lax.axis_index("mp")
        return lax.div(position, g), lax.rem(position, g), c

    def flat(s_, q_, c_):
        return (s_ * g + q_) * 2 + c_

    every = [(s_, q_, c_) for s_ in (0, 1) for q_ in span for c_ in (0, 1)]

    def in_square(value, k):
        return lax.ppermute(value, "fsdp", [(i, i ^ k) for i in range(2 * g)])

    def across(value):
        return lax.ppermute(value, "fsdp", [(i, i ^ g) for i in range(2 * g)])

    def cores(value):
        return lax.ppermute(value, "mp", [(0, 1), (1, 0)])

    def turned(value):
        return lax.ppermute(value, ("fsdp", "mp"), [(flat(*i), flat(i[2], i[1], i[0])) for i in every])

    s, q, c = place()

    def piece(array, k):
        return lax.dynamic_slice_in_dim(array, (q ^ k) * w, w, 1)

    whole = pl.BlockSpec(memory_space=pltpu.VMEM)
    scalars = pl.BlockSpec(memory_space=pltpu.SMEM)

    def call(kernel, operands, outs, flops, scratch=(), in_scalars=0):
        moved = sum(o.size * o.dtype.itemsize for o in operands)
        return pl.pallas_call(
            kernel,
            in_specs=[scalars] * in_scalars + [whole] * (len(operands) - in_scalars),
            out_specs=[whole] * len(outs),
            out_shape=[jax.ShapeDtypeStruct(*o) for o in outs],
            scratch_shapes=list(scratch),
            compiler_params=pltpu.CompilerParams(vmem_limit_bytes=40 * 1024 * 1024),
            cost_estimate=pl.CostEstimate(flops=flops, bytes_accessed=moved, transcendentals=0),
        )(*operands)

    def rows_of(columns):
        return jnp.broadcast_to(columns, (t, 128)).T[:8]

    def columns_of(rows):
        return rows.T[:, :1]

    def pack(rows, store):
        high = rows.astype(bf16)
        rest = rows - high.astype(f32)
        middle = rest.astype(bf16)
        low = (rest - middle.astype(f32)).astype(bf16)
        line = lax.broadcasted_iota(jnp.int32, rows.shape, 0)
        mixed = jnp.where(line == 0, high.astype(f32), jnp.where(line == 1, middle.astype(f32), low.astype(f32)))
        mixed = jnp.where(line < 3, mixed, 0.0)
        store(jnp.concatenate([mixed, jnp.zeros_like(mixed)], axis=0).astype(bf16))

    def unpack(block):
        return jnp.sum(block.astype(f32), axis=0, keepdims=True)

    def share(steps, block):
        return (steps[block].astype(f32) + 1.0) / (NT + 1.0)

    def band(j):
        return slice(j * r, (j + 1) * r)

    def lanes(k):
        return pl.ds(pl.multiple_of(k * w, w), w)

    def scales_kernel(features, gen_e, real_e, fake_e, gen_g, real_g, fake_g, out):
        s, _, _ = place()
        mine = pl.ds(pl.multiple_of(s * h, h), h)
        per = h // 128

        def gain(ref):
            return jnp.concatenate([ref[pl.ds(s * per + i, 1), :] for i in range(per)], axis=1)

        for n, (embed, gains) in enumerate(((gen_e, gen_g), (real_e, real_g), (fake_e, fake_g))):
            part = 0 if n == 0 else 1
            mod = 1.0 + jnp.dot(
                features[part], embed[:, mine], preferred_element_type=f32
            )
            if n == 0:
                out[3] = mod
            scale = mod * gain(gains)
            out[n] = -scale if n == 2 else scale

    features = jnp.stack(
        [step_features(gen_step, gen_embed.shape[0]), step_features(noise_step, gen_embed.shape[0])]
    )
    (scales,) = call(
        scales_kernel,
        [features, gen_embed, real_embed, fake_embed]
        + [v.reshape(-1, 128) for v in (gen_gain, real_gain, fake_gain)],
        [((4, blocks, h), f32)],
        2 * 3 * blocks * 128 * h,
    )

    x = [turned(noise_in)]
    gen_mine = [piece(gen_weight, 0)] + [in_square(piece(gen_weight, k), k) for k in range(1, g)]
    gen_other = [cores(v) for v in gen_mine]
    fresh_turned = turned(renoise)
    x = x + [in_square(x[0], k) for k in range(1, g)]
    fresh = [piece(fresh_turned, 0)] + [in_square(piece(fresh_turned, k), k) for k in range(1, g)]
    real_weight, fake_weight, _ = lax.optimization_barrier((real_weight, fake_weight, x[0]))
    score_send = [jnp.stack([piece(real_weight, k), piece(fake_weight, k)]) for k in span]
    score_mine = [score_send[0]] + [in_square(score_send[k], k) for k in range(1, g)]
    score_other = [cores(v) for v in score_mine]

    def generate_kernel(*refs):
        xs, scale, own, other = refs[:g], refs[g], refs[g + 1 : 2 * g + 1], refs[2 * g + 1 : 3 * g + 1]
        keep, away, sums, x_mine, lift = refs[3 * g + 1 :]
        s, q, c = place()
        totals = []
        for j in span:
            wide = xs[j][...].astype(f32)
            totals.append(jnp.sum(wide * wide, axis=1, keepdims=True))
            lift[band(j), :] = (wide * scale[0, pl.ds(c * g + (q ^ j), 1), :]).astype(bf16)
            x_mine[band(j), :] = xs[j][:, lanes(q)]
        here = jnp.zeros((t, w), f32)
        there = jnp.zeros((t, w), f32)
        for k in span:
            part = lift[:, lanes(q ^ k)]
            here = here + jnp.dot(part, own[k][...], preferred_element_type=f32)
            there = there + jnp.dot(part, other[k][...], preferred_element_type=f32)
        stays = s == c
        keep[...] = jnp.where(stays, here, there)
        away[0:t, :] = jnp.where(stays, there, here).astype(bf16)
        rows = rows_of(jnp.concatenate(totals, axis=0))
        sums[...] = rows

        def store(value):
            away[t : t + tail, 0:t] = value

        if w > t:
            away[t : t + tail, t:] = jnp.zeros((tail, w - t), bf16)
        pack(rows, store)

    keep, away, x_sums, x_mine = call(
        generate_kernel,
        x + [scales] + gen_mine + gen_other,
        [((t, w), f32), ((t + tail, w), bf16), ((8, t), f32), ((t, w), bf16)],
        4 * t * h * w,
        [pltpu.VMEM((t, h), bf16)],
    )

    def inverse_rms(sums, came):
        total = sums[...] + unpack(came[t : t + tail, 0:t])
        return columns_of(lax.rsqrt(total / d + norm_epsilon))

    def blend_kernel(steps, keep, came, sums, x_mine, *refs):
        fresh, (noised, root) = refs[:g], refs[g:]
        _, q, c = place()
        inverse = inverse_rms(sums, came)
        root[...] = jnp.broadcast_to(inverse, (t, 128))
        for j in span:
            part = share(steps, c * g + (q ^ j))
            made = x_mine[band(j), :].astype(f32) + inverse[band(j), :] * (
                keep[band(j), :] + came[band(j), :].astype(f32)
            )
            noised[band(j), :] = ((1.0 - part) * made + part * fresh[j][...].astype(f32)).astype(bf16)

    noised_mine, x_root = call(
        blend_kernel,
        [noise_step, keep, across(away), x_sums, x_mine] + fresh,
        [((t, w), bf16), ((t, 128), f32)],
        10 * t * w,
        in_scalars=1,
    )
    noised = [noised_mine] + [in_square(noised_mine, k) for k in range(1, g)]

    def score_kernel(*refs):
        ns, scale, own, other = refs[:g], refs[g], refs[g + 1 : 2 * g + 1], refs[2 * g + 1 : 3 * g + 1]
        gap, away, sums, full, real_lift, fake_lift = refs[3 * g + 1 :]
        _, q, c = place()
        totals = [jnp.zeros((r, 1), f32) for _ in span]
        here = jnp.zeros((t, w), f32)
        there = jnp.zeros((t, w), f32)
        for k in span:
            for j in span:
                block = pl.ds(c * g + (q ^ j), 1)
                wide = ns[k][band(j ^ k), :].astype(f32)
                totals[j] = totals[j] + jnp.sum(wide * wide, axis=1, keepdims=True)
                real_lift[band(j), :] = (wide * scale[1, block, lanes(q ^ k)]).astype(bf16)
                fake_lift[band(j), :] = (wide * scale[2, block, lanes(q ^ k)]).astype(bf16)
            full[:, lanes(q ^ k)] = ns[k][band(k), :]
            for n, lift in enumerate((real_lift, fake_lift)):
                here = here + jnp.dot(lift[...], own[k][n], preferred_element_type=f32)
                there = there + jnp.dot(lift[...], other[k][n], preferred_element_type=f32)
        gap[:, :w] = here
        gap[:, w:] = there
        away[0:t, :w] = here.astype(bf16)
        away[0:t, w:] = there.astype(bf16)
        rows = rows_of(jnp.concatenate(totals, axis=0))
        sums[...] = rows
        away[t : t + tail, t:] = jnp.zeros((tail, 2 * w - t), bf16)

        def store(value):
            away[t : t + tail, 0:t] = value

        pack(rows, store)

    gap, gap_away, noised_sums, noised_full = call(
        score_kernel,
        noised + [scales] + score_mine + score_other,
        [((t, 2 * w), f32), ((t + tail, 2 * w), bf16), ((8, t), f32), ((r, h), bf16)],
        8 * t * h * w,
        [pltpu.VMEM((t, w), bf16), pltpu.VMEM((t, w), bf16)],
    )
    gap_came = across(gap_away)
    noised_out = turned(noised_full)

    def backward_kernel(steps, gap, came, sums, root, scale, *refs):
        xs, own, other = refs[:g], refs[g : 2 * g], refs[2 * g : 3 * g]
        outs, grad = refs[3 * g : 4 * g], refs[4 * g]
        _, q, c = place()
        inverse = inverse_rms(sums, came)
        for j in span:
            part = share(steps, c * g + (q ^ j))
            value = (part * inverse[band(j), :]) * (gap[band(j), :] + came[band(j), :].astype(f32))
            grad[band(j), :] = value.astype(bf16)
            outs[j][0:r, :] = value.astype(bf16)
        contract = (((1,), (1,)), ((), ()))
        for k in span:
            back = lax.dot_general(grad[:, :w], own[k][...], contract, preferred_element_type=f32)
            back = back + lax.dot_general(grad[:, w:], other[k][...], contract, preferred_element_type=f32)
            total = jnp.zeros((1, w), f32)
            for j in span:
                normed = xs[j][:, lanes(q ^ k)].astype(f32) * root[band(j), :1]
                summed = jnp.sum(back[band(j), :] * normed, axis=0, keepdims=True)
                total = total + summed * scale[3, pl.ds(c * g + (q ^ j), 1), lanes(q ^ k)]

            def store(value):
                outs[k][r : r + tail, :w] = value

            pack(jnp.broadcast_to(total / r, (8, w)), store)
            outs[k][r : r + tail, w:] = jnp.zeros((tail, w), bf16)

    sent = call(
        backward_kernel,
        [noise_step, gap, gap_came, noised_sums, x_root, scales] + x + gen_mine + gen_other,
        [((r + tail, 2 * w), bf16)] * g,
        4 * t * h * w,
        [pltpu.VMEM((t, 2 * w), bf16)],
        in_scalars=1,
    )
    arrived = [sent[0]] + [in_square(sent[k], k) for k in range(1, g)]

    def gather_kernel(*refs):
        parts, (here, there) = refs[:g], refs[g:]
        _, q, _ = place()
        total = jnp.zeros((1, w), f32)
        for k in span:
            here[0:r, lanes(q ^ k)] = parts[k][0:r, :w]
            there[0:r, lanes(q ^ k)] = parts[k][0:r, w:]
            total = total + unpack(parts[k][r : r + tail, :w])

        for ref in (here, there):

            def store(value):
                ref[r : r + tail, :w] = value

            pack(jnp.broadcast_to(total, (8, w)), store)
            ref[r : r + tail, w:] = jnp.zeros((tail, h - w), bf16)

    here, there = call(gather_kernel, arrived, [((r + tail, h), bf16)] * 2, t * h)
    other_core = cores(there)

    def finish_kernel(here, came, grad, gain):
        s, _, c = place()
        grad[...] = jnp.where(s == c, here[0:r, :], came[0:r, :])
        gain[...] = unpack(here[r : r + tail, :w]) + unpack(came[r : r + tail, :w])

    latent_grad, gain = call(finish_kernel, [here, other_core], [((r, h), bf16), ((1, w), f32)], r * h)
    gain_grad = lax.dynamic_slice_in_dim(gain[0], c * (w // 2), w // 2, 0)
    return (noised_out, latent_grad, gain_grad)


def solution(mesh):
    positions = mesh.shape["fsdp"]
    on_device = on_tiles if positions in (4, 8) and mesh.shape["mp"] == 2 else on_groups
    return jax.shard_map(
        on_device,
        mesh=mesh,
        in_specs=(
            P(("rep", "fsdp"), "mp"),
            P(("rep", "fsdp"), "mp"),
            P("rep"),
            P("rep"),
            P("fsdp", "mp"),
            P("fsdp", "mp"),
            P("fsdp", "mp"),
            P(),
            P(),
            P(),
            P(),
            P(),
            P(),
        ),
        out_specs=(P(("rep", "fsdp"), "mp"), P(("rep", "fsdp"), "mp"), P(("rep", "fsdp", "mp"))),
        check_vma=False,
    )
```

```python
import math

import jax
import jax.numpy as jnp
from jax import lax
from jax.experimental import pallas as pl
from jax.experimental.pallas import tpu as pltpu
from jax.sharding import PartitionSpec as P

NT = 1000


norm_epsilon = 1e-06


def from_behind(value, axis, by):
    size = lax.axis_size(axis)
    pairs = [(i, i + by) for i in range(size) if 0 <= i + by < size]
    return lax.ppermute(value, axis, pairs)


def shifted(value, axis, by):
    size = lax.axis_size(axis)
    return lax.ppermute(value, axis, [(i, (i + by) % size) for i in range(size)])


def step_features(step_ids, feature_width):
    half_width = feature_width // 2
    frequency = jnp.exp(-math.log(10000.0) * jnp.arange(half_width, dtype=jnp.float32) / half_width)
    angles = step_ids.astype(jnp.float32)[:, None] * frequency[None, :]
    return jnp.concatenate([jnp.cos(angles), jnp.sin(angles)], axis=1).astype(jnp.bfloat16)


def lookup(step_table, block_ids):
    matches = block_ids[:, None] == jnp.arange(step_table.shape[0], dtype=jnp.int32)[None, :]
    return jnp.sum(jnp.where(matches, step_table[None, :], 0), axis=1)


def block_shares(step_ids):
    return ((step_ids.astype(jnp.float32) + 1.0) / (NT + 1.0))[:, None, None]


def modulate(full_rows, gain_vec, modulation):
    blocks = modulation.shape[0]
    values = full_rows.astype(jnp.float32)
    normed = values * lax.rsqrt(jnp.mean(values * values, axis=1, keepdims=True) + norm_epsilon)
    lifted = normed.reshape(blocks, -1, values.shape[1]) * gain_vec * (1.0 + modulation[:, None, :])
    return (normed, lifted.reshape(values.shape).astype(jnp.bfloat16))


def on_groups(
    noise_in,
    renoise,
    gen_step,
    noise_step,
    gen_weight,
    real_weight,
    fake_weight,
    gen_embed,
    real_embed,
    fake_embed,
    gen_gain,
    real_gain,
    fake_gain,
):
    devices = lax.axis_size("fsdp")
    quarter = devices // 4
    half = 2 * quarter
    position = lax.axis_index("fsdp")
    block_rows = noise_in.shape[0]
    half_width = noise_in.shape[1]
    model_width = gen_gain.shape[0]
    feature_width = gen_embed.shape[0]
    slice_rows = 4 * block_rows // devices
    group_role = (position >= quarter).astype(jnp.int32) + (position >= half).astype(jnp.int32)
    in_generator = group_role == 2
    slot_ids = jnp.arange(devices, dtype=jnp.int32)
    slot_role = (
        (slot_ids >= quarter).astype(jnp.int32) + (slot_ids >= half).astype(jnp.int32)
    ).reshape(devices, 1, 1)
    outgoing = jnp.where(
        slot_role == 2,
        gen_weight[None],
        jnp.where(slot_role == 0, real_weight[None], fake_weight[None]),
    )
    received = lax.all_to_all(outgoing, "fsdp", split_axis=0, concat_axis=0, tiled=True)
    weight_mine = received.reshape(model_width, half_width)
    embed_mine = jnp.where(
        group_role == 2, gen_embed, jnp.where(group_role == 0, real_embed, fake_embed)
    )
    gain_mine = jnp.where(
        group_role == 2, gen_gain, jnp.where(group_role == 0, real_gain, fake_gain)
    )
    partner_noise, partner_renoise = from_behind((noise_in, renoise), "fsdp", half)
    gen_ids = jnp.stack([position, (position + half) % devices])
    gen_mod = jnp.dot(
        step_features(lookup(gen_step, gen_ids), feature_width),
        embed_mine,
        preferred_element_type=jnp.float32,
    )
    gen_shares = block_shares(lookup(noise_step, gen_ids))
    gen_rows = jnp.concatenate([noise_in, partner_noise], axis=0)
    gen_noise = jnp.concatenate([renoise, partner_renoise], axis=0)
    gen_full = lax.all_gather(gen_rows, "mp", axis=1, tiled=True)

    def generate(operands):
        full_rows, own_rows, fresh_noise = operands
        normed, lifted = modulate(full_rows, gain_mine, gen_mod)
        latents = own_rows.astype(jnp.float32) + jnp.dot(
            lifted, weight_mine, preferred_element_type=jnp.float32
        )
        blended = (1.0 - gen_shares) * latents.reshape(
            2, block_rows, half_width
        ) + gen_shares * fresh_noise.astype(jnp.float32).reshape(2, block_rows, half_width)
        return (blended.reshape(2 * block_rows, half_width).astype(jnp.bfloat16), normed)

    def skip_generate(operands):
        return (
            jnp.zeros((2 * block_rows, half_width), jnp.bfloat16),
            jnp.zeros((2 * block_rows, model_width), jnp.float32),
        )

    gen_noised, gen_normed = lax.cond(
        in_generator, generate, skip_generate, (gen_full, gen_rows, gen_noise)
    )
    width_now = gen_noised.shape[1]
    pieces = (
        gen_noised.reshape(2, quarter, slice_rows, width_now)
        .transpose(1, 0, 2, 3)
        .reshape(quarter, 2 * slice_rows, width_now)
    )
    send_rows = jnp.concatenate(
        [pieces, pieces, jnp.zeros((half, 2 * slice_rows, width_now), jnp.bfloat16)], axis=0
    )
    arrived = lax.all_to_all(send_rows, "fsdp", split_axis=0, concat_axis=0, tiled=True)
    score_rows = arrived[half:].reshape(2 * half * slice_rows, width_now)
    gen_slots = jnp.arange(half, dtype=jnp.int32)
    score_ids = jnp.stack([gen_slots + half, gen_slots], axis=1).reshape(2 * half)
    score_mod = jnp.dot(
        step_features(lookup(noise_step, score_ids), feature_width),
        embed_mine,
        preferred_element_type=jnp.float32,
    )
    score_full = lax.all_gather(score_rows, "mp", axis=1, tiled=True)

    def assess(full_rows):
        normed, lifted = modulate(full_rows, gain_mine, score_mod)
        return jnp.dot(lifted, weight_mine, preferred_element_type=jnp.float32).astype(jnp.bfloat16)

    def skip_assess(full_rows):
        return jnp.zeros((2 * half * slice_rows, half_width), jnp.bfloat16)

    prediction = lax.cond(in_generator, skip_assess, assess, score_full)
    grouped = prediction.reshape(half, 2, slice_rows, half_width)
    by_owner = jnp.concatenate([grouped[:, 1], grouped[:, 0]], axis=0)
    returned = lax.all_to_all(by_owner, "fsdp", split_axis=0, concat_axis=0, tiled=True)
    real_block = returned[:quarter].reshape(block_rows, half_width).astype(jnp.float32)
    fake_block = returned[quarter:half].reshape(block_rows, half_width).astype(jnp.float32)
    own_share = block_shares(lookup(noise_step, position[None]))[0]
    own_grad = (own_share * (real_block - fake_block)).astype(jnp.bfloat16)
    handed = jnp.where(in_generator, gen_noised[block_rows:], own_grad)
    taken = shifted(handed, "fsdp", half)

    def reverse(operands):
        grad_rows, normed = operands
        backward = lax.dot_general(
            grad_rows, weight_mine, (((1,), (1,)), ((), ())), preferred_element_type=jnp.float32
        )
        scaled = backward.reshape(2, block_rows, model_width) * (1.0 + gen_mod[:, None, :])
        return jnp.sum(scaled.reshape(2 * block_rows, model_width) * normed, axis=0) / block_rows

    def skip_reverse(operands):
        return jnp.zeros((model_width,), jnp.float32)

    grad_rows = jnp.concatenate([own_grad, taken], axis=0)
    gain_term = lax.cond(in_generator, reverse, skip_reverse, (grad_rows, gen_normed))
    gain_grad = lax.psum_scatter(gain_term, ("fsdp", "mp"), scatter_dimension=0, tiled=True)
    noised_out = jnp.where(in_generator, gen_noised[:block_rows], taken)
    return (noised_out, own_grad, gain_grad)


def on_tiles(
    noise_in,
    renoise,
    gen_step,
    noise_step,
    gen_weight,
    real_weight,
    fake_weight,
    gen_embed,
    real_embed,
    fake_embed,
    gen_gain,
    real_gain,
    fake_gain,
):
    g = lax.axis_size("fsdp") // 2
    r, h = noise_in.shape
    d = 2 * h
    w = h // g
    t = g * r
    blocks = gen_step.shape[0]
    f32, bf16 = jnp.float32, jnp.bfloat16
    tail = 16
    span = range(g)

    def place():
        position, c = lax.axis_index("fsdp"), lax.axis_index("mp")
        return lax.div(position, g), lax.rem(position, g), c

    def flat(s_, q_, c_):
        return (s_ * g + q_) * 2 + c_

    every = [(s_, q_, c_) for s_ in (0, 1) for q_ in span for c_ in (0, 1)]

    def in_square(value, k):
        return lax.ppermute(value, "fsdp", [(i, i ^ k) for i in range(2 * g)])

    def across(value):
        return lax.ppermute(value, "fsdp", [(i, i ^ g) for i in range(2 * g)])

    def cores(value):
        return lax.ppermute(value, "mp", [(0, 1), (1, 0)])

    def turned(value):
        return lax.ppermute(value, ("fsdp", "mp"), [(flat(*i), flat(i[2], i[1], i[0])) for i in every])

    whole = pl.BlockSpec(memory_space=pltpu.VMEM)
    scalars = pl.BlockSpec(memory_space=pltpu.SMEM)

    def call(kernel, operands, outs, flops, scratch=(), in_scalars=0):
        moved = sum(o.size * o.dtype.itemsize for o in operands)
        return pl.pallas_call(
            kernel,
            in_specs=[scalars] * in_scalars + [whole] * (len(operands) - in_scalars),
            out_specs=[whole] * len(outs),
            out_shape=[jax.ShapeDtypeStruct(*o) for o in outs],
            scratch_shapes=list(scratch),
            compiler_params=pltpu.CompilerParams(vmem_limit_bytes=40 * 1024 * 1024),
            cost_estimate=pl.CostEstimate(flops=flops, bytes_accessed=moved, transcendentals=0),
        )(*operands)

    def rows_of(columns):
        return jnp.broadcast_to(columns, (t, 128)).T[:8]

    def columns_of(rows):
        return rows.T[:, :1]

    def pack(rows, store):
        high = rows.astype(bf16)
        rest = rows - high.astype(f32)
        middle = rest.astype(bf16)
        low = (rest - middle.astype(f32)).astype(bf16)
        line = lax.broadcasted_iota(jnp.int32, rows.shape, 0)
        mixed = jnp.where(line == 0, high.astype(f32), jnp.where(line == 1, middle.astype(f32), low.astype(f32)))
        mixed = jnp.where(line < 3, mixed, 0.0)
        store(jnp.concatenate([mixed, jnp.zeros_like(mixed)], axis=0).astype(bf16))

    def unpack(block):
        return jnp.sum(block.astype(f32), axis=0, keepdims=True)

    def share(steps, block):
        return (steps[block].astype(f32) + 1.0) / (NT + 1.0)

    def band(j):
        return slice(j * r, (j + 1) * r)

    def lanes(k):
        return pl.ds(pl.multiple_of(k * w, w), w)

    def scales_kernel(features, gen_e, real_e, fake_e, gen_g, real_g, fake_g, out):
        s, _, _ = place()
        mine = pl.ds(pl.multiple_of(s * h, h), h)
        per = h // 128

        def gain(ref):
            return jnp.concatenate([ref[pl.ds(s * per + i, 1), :] for i in range(per)], axis=1)

        for n, (embed, gains) in enumerate(((gen_e, gen_g), (real_e, real_g), (fake_e, fake_g))):
            part = 0 if n == 0 else 1
            mod = 1.0 + jnp.dot(
                features[part], embed[:, mine], preferred_element_type=f32
            )
            if n == 0:
                out[3] = mod
            scale = mod * gain(gains)
            out[n] = -scale if n == 2 else scale

    features = jnp.stack(
        [step_features(gen_step, gen_embed.shape[0]), step_features(noise_step, gen_embed.shape[0])]
    )
    (scales,) = call(
        scales_kernel,
        [features, gen_embed, real_embed, fake_embed]
        + [v.reshape(-1, 128) for v in (gen_gain, real_gain, fake_gain)],
        [((4, blocks, h), f32)],
        2 * 3 * blocks * 128 * h,
    )

    depth = gen_weight.shape[0]

    def cut_gen_kernel(weight, fresh, *outs):
        _, q, _ = place()
        for k in span:
            outs[k][0:depth, :] = weight[:, lanes(q ^ k)]
            outs[k][depth : depth + r, :] = fresh[:, lanes(q ^ k)]

    def cut_score_kernel(real, fake, *outs):
        _, q, _ = place()
        for k in span:
            outs[k][0] = real[:, lanes(q ^ k)]
            outs[k][1] = fake[:, lanes(q ^ k)]

    x = [turned(noise_in)]
    gen_sent = call(cut_gen_kernel, [gen_weight, renoise], [((depth + r, w), bf16)] * g, depth * h)
    gen_mine = [gen_sent[0]] + [in_square(gen_sent[k], k) for k in range(1, g)]
    gen_other = [cores(v) for v in gen_mine]
    x[0], scales = lax.optimization_barrier((x[0], scales))
    x = x + [in_square(x[0], k) for k in range(1, g)]
    fresh = turned(jnp.concatenate([v[depth:] for v in gen_mine], axis=0))
    real_weight, fake_weight, _ = lax.optimization_barrier((real_weight, fake_weight, x[0]))
    score_sent = call(cut_score_kernel, [real_weight, fake_weight], [((2, depth, w), bf16)] * g, 2 * depth * h)
    score_mine = [score_sent[0]] + [in_square(score_sent[k], k) for k in range(1, g)]
    score_other = [cores(v) for v in score_mine]

    def generate_kernel(*refs):
        xs, scale, own, other = refs[:g], refs[g], refs[g + 1 : 2 * g + 1], refs[2 * g + 1 : 3 * g + 1]
        keep, away, sums, x_mine, lift = refs[3 * g + 1 :]
        s, q, c = place()
        totals = []
        for j in span:
            wide = xs[j][...].astype(f32)
            totals.append(jnp.sum(wide * wide, axis=1, keepdims=True))
            lift[band(j), :] = (wide * scale[0, pl.ds(c * g + (q ^ j), 1), :]).astype(bf16)
            x_mine[band(j), :] = xs[j][:, lanes(q)]
        here = jnp.zeros((t, w), f32)
        there = jnp.zeros((t, w), f32)
        for k in span:
            part = lift[:, lanes(q ^ k)]
            here = here + jnp.dot(part, own[k][0:depth, :], preferred_element_type=f32)
            there = there + jnp.dot(part, other[k][0:depth, :], preferred_element_type=f32)
        stays = s == c
        keep[...] = jnp.where(stays, here, there)
        away[0:t, :] = jnp.where(stays, there, here).astype(bf16)
        rows = rows_of(jnp.concatenate(totals, axis=0))
        sums[...] = rows

        def store(value):
            away[t : t + tail, 0:t] = value

        if w > t:
            away[t : t + tail, t:] = jnp.zeros((tail, w - t), bf16)
        pack(rows, store)

    keep, away, x_sums, x_mine = call(
        generate_kernel,
        x + [scales] + gen_mine + gen_other,
        [((t, w), f32), ((t + tail, w), bf16), ((8, t), f32), ((t, w), bf16)],
        4 * t * h * w,
        [pltpu.VMEM((t, h), bf16)],
    )

    def inverse_rms(sums, came):
        total = sums[...] + unpack(came[t : t + tail, 0:t])
        return columns_of(lax.rsqrt(total / d + norm_epsilon))

    def blend_kernel(steps, keep, came, sums, x_mine, fresh, noised, root):
        _, q, c = place()
        inverse = inverse_rms(sums, came)
        root[...] = jnp.broadcast_to(inverse, (t, 128))
        for j in span:
            part = share(steps, c * g + (q ^ j))
            made = x_mine[band(j), :].astype(f32) + inverse[band(j), :] * (
                keep[band(j), :] + came[band(j), :].astype(f32)
            )
            noised[band(j), :] = ((1.0 - part) * made + part * fresh[band(j), :].astype(f32)).astype(bf16)

    noised_mine, x_root = call(
        blend_kernel,
        [noise_step, keep, across(away), x_sums, x_mine, fresh],
        [((t, w), bf16), ((t, 128), f32)],
        10 * t * w,
        in_scalars=1,
    )
    noised_owned = turned(noised_mine)
    noised = [noised_mine] + [in_square(noised_mine, k) for k in range(1, g)]

    def score_kernel(*refs):
        ns, scale, own, other = refs[:g], refs[g], refs[g + 1 : 2 * g + 1], refs[2 * g + 1 : 3 * g + 1]
        gap, away, sums, real_lift, fake_lift = refs[3 * g + 1 :]
        _, q, c = place()
        totals = [jnp.zeros((r, 1), f32) for _ in span]
        here = jnp.zeros((t, w), f32)
        there = jnp.zeros((t, w), f32)
        for k in span:
            for j in span:
                block = pl.ds(c * g + (q ^ j), 1)
                wide = ns[k][band(j ^ k), :].astype(f32)
                totals[j] = totals[j] + jnp.sum(wide * wide, axis=1, keepdims=True)
                real_lift[band(j), :] = (wide * scale[1, block, lanes(q ^ k)]).astype(bf16)
                fake_lift[band(j), :] = (wide * scale[2, block, lanes(q ^ k)]).astype(bf16)
            for n, lift in enumerate((real_lift, fake_lift)):
                here = here + jnp.dot(lift[...], own[k][n], preferred_element_type=f32)
                there = there + jnp.dot(lift[...], other[k][n], preferred_element_type=f32)
        gap[:, :w] = here
        gap[:, w:] = there
        away[0:t, :w] = here.astype(bf16)
        away[0:t, w:] = there.astype(bf16)
        rows = rows_of(jnp.concatenate(totals, axis=0))
        sums[...] = rows
        away[t : t + tail, t:] = jnp.zeros((tail, 2 * w - t), bf16)

        def store(value):
            away[t : t + tail, 0:t] = value

        pack(rows, store)

    gap, gap_away, noised_sums = call(
        score_kernel,
        noised + [scales] + score_mine + score_other,
        [((t, 2 * w), f32), ((t + tail, 2 * w), bf16), ((8, t), f32)],
        8 * t * h * w,
        [pltpu.VMEM((t, w), bf16), pltpu.VMEM((t, w), bf16)],
    )
    gap_came = across(gap_away)

    def backward_kernel(steps, gap, came, sums, root, scale, owned, *refs):
        xs, own, other = refs[:g], refs[g : 2 * g], refs[2 * g : 3 * g]
        outs, grad = refs[3 * g : 4 * g], refs[4 * g]
        _, q, c = place()
        inverse = inverse_rms(sums, came)
        for j in span:
            part = share(steps, c * g + (q ^ j))
            value = (part * inverse[band(j), :]) * (gap[band(j), :] + came[band(j), :].astype(f32))
            grad[band(j), :] = value.astype(bf16)
            outs[j][0:r, :] = value.astype(bf16)
            for n in (0, 1):
                half = slice(j * r + n * (r // 2), j * r + (n + 1) * (r // 2))
                outs[j][r + tail : r + tail + r // 2, n * w : (n + 1) * w] = owned[half, :]
        contract = (((1,), (1,)), ((), ()))
        for k in span:
            back = lax.dot_general(grad[:, :w], own[k][0:depth, :], contract, preferred_element_type=f32)
            back = back + lax.dot_general(grad[:, w:], other[k][0:depth, :], contract, preferred_element_type=f32)
            total = jnp.zeros((1, w), f32)
            for j in span:
                normed = xs[j][:, lanes(q ^ k)].astype(f32) * root[band(j), :1]
                summed = jnp.sum(back[band(j), :] * normed, axis=0, keepdims=True)
                total = total + summed * scale[3, pl.ds(c * g + (q ^ j), 1), lanes(q ^ k)]

            def store(value):
                outs[k][r : r + tail, :w] = value

            pack(jnp.broadcast_to(total / r, (8, w)), store)
            outs[k][r : r + tail, w:] = jnp.zeros((tail, w), bf16)

    sent = call(
        backward_kernel,
        [noise_step, gap, gap_came, noised_sums, x_root, scales, noised_owned] + x + gen_mine + gen_other,
        [((r + tail + r // 2, 2 * w), bf16)] * g,
        4 * t * h * w,
        [pltpu.VMEM((t, 2 * w), bf16)],
        in_scalars=1,
    )
    arrived = [sent[0]] + [in_square(sent[k], k) for k in range(1, g)]

    def gather_kernel(*refs):
        parts, (here, there, noised) = refs[:g], refs[g:]
        _, q, _ = place()
        total = jnp.zeros((1, w), f32)
        for k in span:
            here[0:r, lanes(q ^ k)] = parts[k][0:r, :w]
            there[0:r, lanes(q ^ k)] = parts[k][0:r, w:]
            total = total + unpack(parts[k][r : r + tail, :w])
            for n in (0, 1):
                noised[n * (r // 2) : (n + 1) * (r // 2), lanes(q ^ k)] = parts[k][r + tail :, n * w : (n + 1) * w]

        for ref in (here, there):

            def store(value):
                ref[r : r + tail, :w] = value

            pack(jnp.broadcast_to(total, (8, w)), store)
            ref[r : r + tail, w:] = jnp.zeros((tail, h - w), bf16)

    here, there, noised_out = call(
        gather_kernel, arrived, [((r + tail, h), bf16)] * 2 + [((r, h), bf16)], t * h
    )
    other_core = cores(there)

    def finish_kernel(here, came, grad, gain):
        s, _, c = place()
        grad[...] = jnp.where(s == c, here[0:r, :], came[0:r, :])
        both = unpack(here[r : r + tail, :w]) + unpack(came[r : r + tail, :w])
        gain[...] = jnp.where(c == 0, both[:, : w // 2], both[:, w // 2 :])

    latent_grad, gain = call(finish_kernel, [here, other_core], [((r, h), bf16), ((1, w // 2), f32)], r * h)
    return (noised_out, latent_grad, gain[0])


def solution(mesh):
    positions = mesh.shape["fsdp"]
    on_device = on_tiles if positions in (4, 8) and mesh.shape["mp"] == 2 else on_groups
    return jax.shard_map(
        on_device,
        mesh=mesh,
        in_specs=(
            P(("rep", "fsdp"), "mp"),
            P(("rep", "fsdp"), "mp"),
            P("rep"),
            P("rep"),
            P("fsdp", "mp"),
            P("fsdp", "mp"),
            P("fsdp", "mp"),
            P(),
            P(),
            P(),
            P(),
            P(),
            P(),
        ),
        out_specs=(P(("rep", "fsdp"), "mp"), P(("rep", "fsdp"), "mp"), P(("rep", "fsdp", "mp"))),
        check_vma=False,
    )
```

```python
import math

import jax
import jax.numpy as jnp
from jax import lax
from jax.experimental import pallas as pl
from jax.experimental.pallas import tpu as pltpu
from jax.sharding import PartitionSpec as P

NT = 1000


norm_epsilon = 1e-06


def from_behind(value, axis, by):
    size = lax.axis_size(axis)
    pairs = [(i, i + by) for i in range(size) if 0 <= i + by < size]
    return lax.ppermute(value, axis, pairs)


def shifted(value, axis, by):
    size = lax.axis_size(axis)
    return lax.ppermute(value, axis, [(i, (i + by) % size) for i in range(size)])


def step_features(step_ids, feature_width):
    half_width = feature_width // 2
    frequency = jnp.exp(-math.log(10000.0) * jnp.arange(half_width, dtype=jnp.float32) / half_width)
    angles = step_ids.astype(jnp.float32)[:, None] * frequency[None, :]
    return jnp.concatenate([jnp.cos(angles), jnp.sin(angles)], axis=1).astype(jnp.bfloat16)


def lookup(step_table, block_ids):
    matches = block_ids[:, None] == jnp.arange(step_table.shape[0], dtype=jnp.int32)[None, :]
    return jnp.sum(jnp.where(matches, step_table[None, :], 0), axis=1)


def block_shares(step_ids):
    return ((step_ids.astype(jnp.float32) + 1.0) / (NT + 1.0))[:, None, None]


def modulate(full_rows, gain_vec, modulation):
    blocks = modulation.shape[0]
    values = full_rows.astype(jnp.float32)
    normed = values * lax.rsqrt(jnp.mean(values * values, axis=1, keepdims=True) + norm_epsilon)
    lifted = normed.reshape(blocks, -1, values.shape[1]) * gain_vec * (1.0 + modulation[:, None, :])
    return (normed, lifted.reshape(values.shape).astype(jnp.bfloat16))


def on_groups(
    noise_in,
    renoise,
    gen_step,
    noise_step,
    gen_weight,
    real_weight,
    fake_weight,
    gen_embed,
    real_embed,
    fake_embed,
    gen_gain,
    real_gain,
    fake_gain,
):
    devices = lax.axis_size("fsdp")
    quarter = devices // 4
    half = 2 * quarter
    position = lax.axis_index("fsdp")
    block_rows = noise_in.shape[0]
    half_width = noise_in.shape[1]
    model_width = gen_gain.shape[0]
    feature_width = gen_embed.shape[0]
    slice_rows = 4 * block_rows // devices
    group_role = (position >= quarter).astype(jnp.int32) + (position >= half).astype(jnp.int32)
    in_generator = group_role == 2
    slot_ids = jnp.arange(devices, dtype=jnp.int32)
    slot_role = (
        (slot_ids >= quarter).astype(jnp.int32) + (slot_ids >= half).astype(jnp.int32)
    ).reshape(devices, 1, 1)
    outgoing = jnp.where(
        slot_role == 2,
        gen_weight[None],
        jnp.where(slot_role == 0, real_weight[None], fake_weight[None]),
    )
    received = lax.all_to_all(outgoing, "fsdp", split_axis=0, concat_axis=0, tiled=True)
    weight_mine = received.reshape(model_width, half_width)
    embed_mine = jnp.where(
        group_role == 2, gen_embed, jnp.where(group_role == 0, real_embed, fake_embed)
    )
    gain_mine = jnp.where(
        group_role == 2, gen_gain, jnp.where(group_role == 0, real_gain, fake_gain)
    )
    partner_noise, partner_renoise = from_behind((noise_in, renoise), "fsdp", half)
    gen_ids = jnp.stack([position, (position + half) % devices])
    gen_mod = jnp.dot(
        step_features(lookup(gen_step, gen_ids), feature_width),
        embed_mine,
        preferred_element_type=jnp.float32,
    )
    gen_shares = block_shares(lookup(noise_step, gen_ids))
    gen_rows = jnp.concatenate([noise_in, partner_noise], axis=0)
    gen_noise = jnp.concatenate([renoise, partner_renoise], axis=0)
    gen_full = lax.all_gather(gen_rows, "mp", axis=1, tiled=True)

    def generate(operands):
        full_rows, own_rows, fresh_noise = operands
        normed, lifted = modulate(full_rows, gain_mine, gen_mod)
        latents = own_rows.astype(jnp.float32) + jnp.dot(
            lifted, weight_mine, preferred_element_type=jnp.float32
        )
        blended = (1.0 - gen_shares) * latents.reshape(
            2, block_rows, half_width
        ) + gen_shares * fresh_noise.astype(jnp.float32).reshape(2, block_rows, half_width)
        return (blended.reshape(2 * block_rows, half_width).astype(jnp.bfloat16), normed)

    def skip_generate(operands):
        return (
            jnp.zeros((2 * block_rows, half_width), jnp.bfloat16),
            jnp.zeros((2 * block_rows, model_width), jnp.float32),
        )

    gen_noised, gen_normed = lax.cond(
        in_generator, generate, skip_generate, (gen_full, gen_rows, gen_noise)
    )
    width_now = gen_noised.shape[1]
    pieces = (
        gen_noised.reshape(2, quarter, slice_rows, width_now)
        .transpose(1, 0, 2, 3)
        .reshape(quarter, 2 * slice_rows, width_now)
    )
    send_rows = jnp.concatenate(
        [pieces, pieces, jnp.zeros((half, 2 * slice_rows, width_now), jnp.bfloat16)], axis=0
    )
    arrived = lax.all_to_all(send_rows, "fsdp", split_axis=0, concat_axis=0, tiled=True)
    score_rows = arrived[half:].reshape(2 * half * slice_rows, width_now)
    gen_slots = jnp.arange(half, dtype=jnp.int32)
    score_ids = jnp.stack([gen_slots + half, gen_slots], axis=1).reshape(2 * half)
    score_mod = jnp.dot(
        step_features(lookup(noise_step, score_ids), feature_width),
        embed_mine,
        preferred_element_type=jnp.float32,
    )
    score_full = lax.all_gather(score_rows, "mp", axis=1, tiled=True)

    def assess(full_rows):
        normed, lifted = modulate(full_rows, gain_mine, score_mod)
        return jnp.dot(lifted, weight_mine, preferred_element_type=jnp.float32).astype(jnp.bfloat16)

    def skip_assess(full_rows):
        return jnp.zeros((2 * half * slice_rows, half_width), jnp.bfloat16)

    prediction = lax.cond(in_generator, skip_assess, assess, score_full)
    grouped = prediction.reshape(half, 2, slice_rows, half_width)
    by_owner = jnp.concatenate([grouped[:, 1], grouped[:, 0]], axis=0)
    returned = lax.all_to_all(by_owner, "fsdp", split_axis=0, concat_axis=0, tiled=True)
    real_block = returned[:quarter].reshape(block_rows, half_width).astype(jnp.float32)
    fake_block = returned[quarter:half].reshape(block_rows, half_width).astype(jnp.float32)
    own_share = block_shares(lookup(noise_step, position[None]))[0]
    own_grad = (own_share * (real_block - fake_block)).astype(jnp.bfloat16)
    handed = jnp.where(in_generator, gen_noised[block_rows:], own_grad)
    taken = shifted(handed, "fsdp", half)

    def reverse(operands):
        grad_rows, normed = operands
        backward = lax.dot_general(
            grad_rows, weight_mine, (((1,), (1,)), ((), ())), preferred_element_type=jnp.float32
        )
        scaled = backward.reshape(2, block_rows, model_width) * (1.0 + gen_mod[:, None, :])
        return jnp.sum(scaled.reshape(2 * block_rows, model_width) * normed, axis=0) / block_rows

    def skip_reverse(operands):
        return jnp.zeros((model_width,), jnp.float32)

    grad_rows = jnp.concatenate([own_grad, taken], axis=0)
    gain_term = lax.cond(in_generator, reverse, skip_reverse, (grad_rows, gen_normed))
    gain_grad = lax.psum_scatter(gain_term, ("fsdp", "mp"), scatter_dimension=0, tiled=True)
    noised_out = jnp.where(in_generator, gen_noised[:block_rows], taken)
    return (noised_out, own_grad, gain_grad)


def on_tiles(
    noise_in,
    renoise,
    gen_step,
    noise_step,
    gen_weight,
    real_weight,
    fake_weight,
    gen_embed,
    real_embed,
    fake_embed,
    gen_gain,
    real_gain,
    fake_gain,
):
    g = lax.axis_size("fsdp") // 2
    r, h = noise_in.shape
    d = 2 * h
    w = h // g
    t = g * r
    blocks = gen_step.shape[0]
    f32, bf16 = jnp.float32, jnp.bfloat16
    tail = 16
    span = range(g)

    def place():
        position, c = lax.axis_index("fsdp"), lax.axis_index("mp")
        return lax.div(position, g), lax.rem(position, g), c

    def flat(s_, q_, c_):
        return (s_ * g + q_) * 2 + c_

    every = [(s_, q_, c_) for s_ in (0, 1) for q_ in span for c_ in (0, 1)]

    def in_square(value, k):
        return lax.ppermute(value, "fsdp", [(i, i ^ k) for i in range(2 * g)])

    def across(value):
        return lax.ppermute(value, "fsdp", [(i, i ^ g) for i in range(2 * g)])

    def cores(value):
        return lax.ppermute(value, "mp", [(0, 1), (1, 0)])

    def turned(value):
        return lax.ppermute(value, ("fsdp", "mp"), [(flat(*i), flat(i[2], i[1], i[0])) for i in every])

    whole = pl.BlockSpec(memory_space=pltpu.VMEM)
    scalars = pl.BlockSpec(memory_space=pltpu.SMEM)

    def call(kernel, operands, outs, flops, scratch=(), in_scalars=0):
        moved = sum(o.size * o.dtype.itemsize for o in operands)
        return pl.pallas_call(
            kernel,
            in_specs=[scalars] * in_scalars + [whole] * (len(operands) - in_scalars),
            out_specs=[whole] * len(outs),
            out_shape=[jax.ShapeDtypeStruct(*o) for o in outs],
            scratch_shapes=list(scratch),
            compiler_params=pltpu.CompilerParams(vmem_limit_bytes=40 * 1024 * 1024),
            cost_estimate=pl.CostEstimate(flops=flops, bytes_accessed=moved, transcendentals=0),
        )(*operands)

    def rows_of(columns):
        return jnp.broadcast_to(columns, (t, 128)).T[:8]

    def columns_of(rows):
        return rows.T[:, :1]

    def pack(rows, store):
        high = rows.astype(bf16)
        rest = rows - high.astype(f32)
        middle = rest.astype(bf16)
        low = (rest - middle.astype(f32)).astype(bf16)
        line = lax.broadcasted_iota(jnp.int32, rows.shape, 0)
        mixed = jnp.where(line == 0, high.astype(f32), jnp.where(line == 1, middle.astype(f32), low.astype(f32)))
        mixed = jnp.where(line < 3, mixed, 0.0)
        store(jnp.concatenate([mixed, jnp.zeros_like(mixed)], axis=0).astype(bf16))

    def unpack(block):
        return jnp.sum(block.astype(f32), axis=0, keepdims=True)

    def share(steps, block):
        return (steps[block].astype(f32) + 1.0) / (NT + 1.0)

    def band(j):
        return slice(j * r, (j + 1) * r)

    def lanes(k):
        return pl.ds(pl.multiple_of(k * w, w), w)

    def scales_kernel(features, gen_e, real_e, fake_e, gen_g, real_g, fake_g, out):
        s, _, _ = place()
        mine = pl.ds(pl.multiple_of(s * h, h), h)
        per = h // 128

        def gain(ref):
            return jnp.concatenate([ref[pl.ds(s * per + i, 1), :] for i in range(per)], axis=1)

        for n, (embed, gains) in enumerate(((gen_e, gen_g), (real_e, real_g), (fake_e, fake_g))):
            part = 0 if n == 0 else 1
            mod = 1.0 + jnp.dot(
                features[part], embed[:, mine], preferred_element_type=f32
            )
            if n == 0:
                out[3] = mod
            scale = mod * gain(gains)
            out[n] = -scale if n == 2 else scale

    features = jnp.stack(
        [step_features(gen_step, gen_embed.shape[0]), step_features(noise_step, gen_embed.shape[0])]
    )
    (scales,) = call(
        scales_kernel,
        [features, gen_embed, real_embed, fake_embed]
        + [v.reshape(-1, 128) for v in (gen_gain, real_gain, fake_gain)],
        [((4, blocks, h), f32)],
        2 * 3 * blocks * 128 * h,
    )

    depth = gen_weight.shape[0]
    fold = r // g

    def cut_gen_kernel(weight, *outs):
        _, q, _ = place()
        for k in span:
            outs[k][...] = weight[:, lanes(q ^ k)]

    def cut_score_kernel(real, fake, *outs):
        _, q, _ = place()
        for k in span:
            outs[k][0] = real[:, lanes(q ^ k)]
            outs[k][1] = fake[:, lanes(q ^ k)]

    def cut_rows_kernel(rows, fresh, *outs):
        _, q, _ = place()
        for k in span:
            outs[k][0:r, :] = rows[...]
            for i in span:
                outs[k][r : r + fold, i * w : (i + 1) * w] = fresh[i * fold : (i + 1) * fold, lanes(q ^ k)]

    x_turned, fresh_turned = turned(noise_in), turned(renoise)
    gen_sent = call(cut_gen_kernel, [gen_weight], [((depth, w), bf16)] * g, depth * h)
    gen_mine = [gen_sent[0]] + [in_square(gen_sent[k], k) for k in range(1, g)]
    gen_other = [cores(v) for v in gen_mine]
    x_turned, scales = lax.optimization_barrier((x_turned, scales))
    x_sent = call(cut_rows_kernel, [x_turned, fresh_turned], [((r + fold, h), bf16)] * g, r * h)
    x = [x_sent[0]] + [in_square(x_sent[k], k) for k in range(1, g)]
    real_weight, fake_weight, _ = lax.optimization_barrier((real_weight, fake_weight, x_turned))
    score_sent = call(cut_score_kernel, [real_weight, fake_weight], [((2, depth, w), bf16)] * g, 2 * depth * h)
    score_mine = [score_sent[0]] + [in_square(score_sent[k], k) for k in range(1, g)]
    score_other = [cores(v) for v in score_mine]

    def generate_kernel(steps, *refs):
        xs, scale, own, other = refs[:g], refs[g], refs[g + 1 : 2 * g + 1], refs[2 * g + 1 : 3 * g + 1]
        keep, away, sums, base, lift = refs[3 * g + 1 :]
        s, q, c = place()
        totals = []
        for j in span:
            wide = xs[j][0:r, :].astype(f32)
            totals.append(jnp.sum(wide * wide, axis=1, keepdims=True))
            lift[band(j), :] = (wide * scale[0, pl.ds(c * g + (q ^ j), 1), :]).astype(bf16)
            part = share(steps, c * g + (q ^ j))
            for i in span:
                some = slice(i * fold, (i + 1) * fold)
                base[j * r + i * fold : j * r + (i + 1) * fold, :] = (1.0 - part) * xs[j][some, lanes(q)].astype(
                    f32
                ) + part * xs[j][r : r + fold, i * w : (i + 1) * w].astype(f32)
        here = jnp.zeros((t, w), f32)
        there = jnp.zeros((t, w), f32)
        for k in span:
            part = lift[:, lanes(q ^ k)]
            here = here + jnp.dot(part, own[k][...], preferred_element_type=f32)
            there = there + jnp.dot(part, other[k][...], preferred_element_type=f32)
        stays = s == c
        keep[...] = jnp.where(stays, here, there)
        away[0:t, :] = jnp.where(stays, there, here).astype(bf16)
        rows = rows_of(jnp.concatenate(totals, axis=0))
        sums[...] = rows

        def store(value):
            away[t : t + tail, 0:t] = value

        if w > t:
            away[t : t + tail, t:] = jnp.zeros((tail, w - t), bf16)
        pack(rows, store)

    keep, away, x_sums, base = call(
        generate_kernel,
        [noise_step] + x + [scales] + gen_mine + gen_other,
        [((t, w), f32), ((t + tail, w), bf16), ((8, t), f32), ((t, w), f32)],
        4 * t * h * w,
        [pltpu.VMEM((t, h), bf16)],
        in_scalars=1,
    )

    def inverse_rms(sums, came):
        total = sums[...] + unpack(came[t : t + tail, 0:t])
        return columns_of(lax.rsqrt(total / d + norm_epsilon))

    def blend_kernel(steps, keep, came, sums, base, noised, root):
        _, q, c = place()
        inverse = inverse_rms(sums, came)
        root[...] = jnp.broadcast_to(inverse, (t, 128))
        for j in span:
            stay = 1.0 - share(steps, c * g + (q ^ j))
            made = keep[band(j), :] + came[band(j), :].astype(f32)
            noised[band(j), :] = (base[band(j), :] + (stay * inverse[band(j), :]) * made).astype(bf16)

    noised_mine, x_root = call(
        blend_kernel,
        [noise_step, keep, across(away), x_sums, base],
        [((t, w), bf16), ((t, 128), f32)],
        10 * t * w,
        in_scalars=1,
    )
    noised_owned = turned(noised_mine)
    noised = [noised_mine] + [in_square(noised_mine, k) for k in range(1, g)]
    noised_owned, score_scales = lax.optimization_barrier((noised_owned, scales))

    def score_kernel(*refs):
        ns, scale, own, other = refs[:g], refs[g], refs[g + 1 : 2 * g + 1], refs[2 * g + 1 : 3 * g + 1]
        gap, away, sums, real_lift, fake_lift = refs[3 * g + 1 :]
        _, q, c = place()
        totals = [jnp.zeros((r, 1), f32) for _ in span]
        here = jnp.zeros((t, w), f32)
        there = jnp.zeros((t, w), f32)
        for k in span:
            for j in span:
                block = pl.ds(c * g + (q ^ j), 1)
                wide = ns[k][band(j ^ k), :].astype(f32)
                totals[j] = totals[j] + jnp.sum(wide * wide, axis=1, keepdims=True)
                real_lift[band(j), :] = (wide * scale[1, block, lanes(q ^ k)]).astype(bf16)
                fake_lift[band(j), :] = (wide * scale[2, block, lanes(q ^ k)]).astype(bf16)
            for n, lift in enumerate((real_lift, fake_lift)):
                here = here + jnp.dot(lift[...], own[k][n], preferred_element_type=f32)
                there = there + jnp.dot(lift[...], other[k][n], preferred_element_type=f32)
        gap[:, :w] = here
        gap[:, w:] = there
        away[0:t, :w] = here.astype(bf16)
        away[0:t, w:] = there.astype(bf16)
        rows = rows_of(jnp.concatenate(totals, axis=0))
        sums[...] = rows
        away[t : t + tail, t:] = jnp.zeros((tail, 2 * w - t), bf16)

        def store(value):
            away[t : t + tail, 0:t] = value

        pack(rows, store)

    gap, gap_away, noised_sums = call(
        score_kernel,
        noised + [score_scales] + score_mine + score_other,
        [((t, 2 * w), f32), ((t + tail, 2 * w), bf16), ((8, t), f32)],
        8 * t * h * w,
        [pltpu.VMEM((t, w), bf16), pltpu.VMEM((t, w), bf16)],
    )
    gap_came = across(gap_away)

    def backward_kernel(steps, gap, came, sums, root, scale, owned, *refs):
        xs, own, other = refs[:g], refs[g : 2 * g], refs[2 * g : 3 * g]
        outs, grad = refs[3 * g : 4 * g], refs[4 * g]
        _, q, c = place()
        inverse = inverse_rms(sums, came)
        for j in span:
            part = share(steps, c * g + (q ^ j))
            value = (part * inverse[band(j), :]) * (gap[band(j), :] + came[band(j), :].astype(f32))
            grad[band(j), :] = value.astype(bf16)
            outs[j][0:r, :] = value.astype(bf16)
            for n in (0, 1):
                half = slice(j * r + n * (r // 2), j * r + (n + 1) * (r // 2))
                outs[j][r + tail : r + tail + r // 2, n * w : (n + 1) * w] = owned[half, :]
        contract = (((1,), (1,)), ((), ()))
        for k in span:
            back = lax.dot_general(grad[:, :w], own[k][...], contract, preferred_element_type=f32)
            back = back + lax.dot_general(grad[:, w:], other[k][...], contract, preferred_element_type=f32)
            total = jnp.zeros((1, w), f32)
            for j in span:
                normed = xs[j][0:r, lanes(q ^ k)].astype(f32) * root[band(j), :1]
                summed = jnp.sum(back[band(j), :] * normed, axis=0, keepdims=True)
                total = total + summed * scale[3, pl.ds(c * g + (q ^ j), 1), lanes(q ^ k)]

            def store(value):
                outs[k][r : r + tail, :w] = value

            pack(jnp.broadcast_to(total / r, (8, w)), store)
            outs[k][r : r + tail, w:] = jnp.zeros((tail, w), bf16)

    sent = call(
        backward_kernel,
        [noise_step, gap, gap_came, noised_sums, x_root, scales, noised_owned] + x + gen_mine + gen_other,
        [((r + tail + r // 2, 2 * w), bf16)] * g,
        4 * t * h * w,
        [pltpu.VMEM((t, 2 * w), bf16)],
        in_scalars=1,
    )
    arrived = [sent[0]] + [in_square(sent[k], k) for k in range(1, g)]

    def gather_kernel(*refs):
        parts, (here, there, noised) = refs[:g], refs[g:]
        _, q, _ = place()
        total = jnp.zeros((1, w), f32)
        for k in span:
            here[0:r, lanes(q ^ k)] = parts[k][0:r, :w]
            there[0:r, lanes(q ^ k)] = parts[k][0:r, w:]
            total = total + unpack(parts[k][r : r + tail, :w])
            for n in (0, 1):
                noised[n * (r // 2) : (n + 1) * (r // 2), lanes(q ^ k)] = parts[k][r + tail :, n * w : (n + 1) * w]

        for ref in (here, there):

            def store(value):
                ref[r : r + tail, :w] = value

            pack(jnp.broadcast_to(total, (8, w)), store)
            ref[r : r + tail, w:] = jnp.zeros((tail, h - w), bf16)

    here, there, noised_out = call(
        gather_kernel, arrived, [((r + tail, h), bf16)] * 2 + [((r, h), bf16)], t * h
    )
    other_core = cores(there)

    def finish_kernel(here, came, grad, gain):
        s, _, c = place()
        grad[...] = jnp.where(s == c, here[0:r, :], came[0:r, :])
        both = unpack(here[r : r + tail, :w]) + unpack(came[r : r + tail, :w])
        gain[...] = jnp.where(c == 0, both[:, : w // 2], both[:, w // 2 :])

    latent_grad, gain = call(finish_kernel, [here, other_core], [((r, h), bf16), ((1, w // 2), f32)], r * h)
    return (noised_out, latent_grad, gain[0])


def solution(mesh):
    positions = mesh.shape["fsdp"]
    on_device = on_tiles if positions in (4, 8) and mesh.shape["mp"] == 2 else on_groups
    return jax.shard_map(
        on_device,
        mesh=mesh,
        in_specs=(
            P(("rep", "fsdp"), "mp"),
            P(("rep", "fsdp"), "mp"),
            P("rep"),
            P("rep"),
            P("fsdp", "mp"),
            P("fsdp", "mp"),
            P("fsdp", "mp"),
            P(),
            P(),
            P(),
            P(),
            P(),
            P(),
        ),
        out_specs=(P(("rep", "fsdp"), "mp"), P(("rep", "fsdp"), "mp"), P(("rep", "fsdp", "mp"))),
        check_vma=False,
    )
```

```python
import math

import jax
import jax.numpy as jnp
from jax import lax
from jax.experimental import pallas as pl
from jax.experimental.pallas import tpu as pltpu
from jax.sharding import PartitionSpec as P

NT = 1000


norm_epsilon = 1e-06


def from_behind(value, axis, by):
    size = lax.axis_size(axis)
    pairs = [(i, i + by) for i in range(size) if 0 <= i + by < size]
    return lax.ppermute(value, axis, pairs)


def shifted(value, axis, by):
    size = lax.axis_size(axis)
    return lax.ppermute(value, axis, [(i, (i + by) % size) for i in range(size)])


def step_features(step_ids, feature_width):
    half_width = feature_width // 2
    frequency = jnp.exp(-math.log(10000.0) * jnp.arange(half_width, dtype=jnp.float32) / half_width)
    angles = step_ids.astype(jnp.float32)[:, None] * frequency[None, :]
    return jnp.concatenate([jnp.cos(angles), jnp.sin(angles)], axis=1).astype(jnp.bfloat16)


def lookup(step_table, block_ids):
    matches = block_ids[:, None] == jnp.arange(step_table.shape[0], dtype=jnp.int32)[None, :]
    return jnp.sum(jnp.where(matches, step_table[None, :], 0), axis=1)


def block_shares(step_ids):
    return ((step_ids.astype(jnp.float32) + 1.0) / (NT + 1.0))[:, None, None]


def modulate(full_rows, gain_vec, modulation):
    blocks = modulation.shape[0]
    values = full_rows.astype(jnp.float32)
    normed = values * lax.rsqrt(jnp.mean(values * values, axis=1, keepdims=True) + norm_epsilon)
    lifted = normed.reshape(blocks, -1, values.shape[1]) * gain_vec * (1.0 + modulation[:, None, :])
    return (normed, lifted.reshape(values.shape).astype(jnp.bfloat16))


def on_groups(
    noise_in,
    renoise,
    gen_step,
    noise_step,
    gen_weight,
    real_weight,
    fake_weight,
    gen_embed,
    real_embed,
    fake_embed,
    gen_gain,
    real_gain,
    fake_gain,
):
    devices = lax.axis_size("fsdp")
    quarter = devices // 4
    half = 2 * quarter
    position = lax.axis_index("fsdp")
    block_rows = noise_in.shape[0]
    half_width = noise_in.shape[1]
    model_width = gen_gain.shape[0]
    feature_width = gen_embed.shape[0]
    slice_rows = 4 * block_rows // devices
    group_role = (position >= quarter).astype(jnp.int32) + (position >= half).astype(jnp.int32)
    in_generator = group_role == 2
    slot_ids = jnp.arange(devices, dtype=jnp.int32)
    slot_role = (
        (slot_ids >= quarter).astype(jnp.int32) + (slot_ids >= half).astype(jnp.int32)
    ).reshape(devices, 1, 1)
    outgoing = jnp.where(
        slot_role == 2,
        gen_weight[None],
        jnp.where(slot_role == 0, real_weight[None], fake_weight[None]),
    )
    received = lax.all_to_all(outgoing, "fsdp", split_axis=0, concat_axis=0, tiled=True)
    weight_mine = received.reshape(model_width, half_width)
    embed_mine = jnp.where(
        group_role == 2, gen_embed, jnp.where(group_role == 0, real_embed, fake_embed)
    )
    gain_mine = jnp.where(
        group_role == 2, gen_gain, jnp.where(group_role == 0, real_gain, fake_gain)
    )
    partner_noise, partner_renoise = from_behind((noise_in, renoise), "fsdp", half)
    gen_ids = jnp.stack([position, (position + half) % devices])
    gen_mod = jnp.dot(
        step_features(lookup(gen_step, gen_ids), feature_width),
        embed_mine,
        preferred_element_type=jnp.float32,
    )
    gen_shares = block_shares(lookup(noise_step, gen_ids))
    gen_rows = jnp.concatenate([noise_in, partner_noise], axis=0)
    gen_noise = jnp.concatenate([renoise, partner_renoise], axis=0)
    gen_full = lax.all_gather(gen_rows, "mp", axis=1, tiled=True)

    def generate(operands):
        full_rows, own_rows, fresh_noise = operands
        normed, lifted = modulate(full_rows, gain_mine, gen_mod)
        latents = own_rows.astype(jnp.float32) + jnp.dot(
            lifted, weight_mine, preferred_element_type=jnp.float32
        )
        blended = (1.0 - gen_shares) * latents.reshape(
            2, block_rows, half_width
        ) + gen_shares * fresh_noise.astype(jnp.float32).reshape(2, block_rows, half_width)
        return (blended.reshape(2 * block_rows, half_width).astype(jnp.bfloat16), normed)

    def skip_generate(operands):
        return (
            jnp.zeros((2 * block_rows, half_width), jnp.bfloat16),
            jnp.zeros((2 * block_rows, model_width), jnp.float32),
        )

    gen_noised, gen_normed = lax.cond(
        in_generator, generate, skip_generate, (gen_full, gen_rows, gen_noise)
    )
    width_now = gen_noised.shape[1]
    pieces = (
        gen_noised.reshape(2, quarter, slice_rows, width_now)
        .transpose(1, 0, 2, 3)
        .reshape(quarter, 2 * slice_rows, width_now)
    )
    send_rows = jnp.concatenate(
        [pieces, pieces, jnp.zeros((half, 2 * slice_rows, width_now), jnp.bfloat16)], axis=0
    )
    arrived = lax.all_to_all(send_rows, "fsdp", split_axis=0, concat_axis=0, tiled=True)
    score_rows = arrived[half:].reshape(2 * half * slice_rows, width_now)
    gen_slots = jnp.arange(half, dtype=jnp.int32)
    score_ids = jnp.stack([gen_slots + half, gen_slots], axis=1).reshape(2 * half)
    score_mod = jnp.dot(
        step_features(lookup(noise_step, score_ids), feature_width),
        embed_mine,
        preferred_element_type=jnp.float32,
    )
    score_full = lax.all_gather(score_rows, "mp", axis=1, tiled=True)

    def assess(full_rows):
        normed, lifted = modulate(full_rows, gain_mine, score_mod)
        return jnp.dot(lifted, weight_mine, preferred_element_type=jnp.float32).astype(jnp.bfloat16)

    def skip_assess(full_rows):
        return jnp.zeros((2 * half * slice_rows, half_width), jnp.bfloat16)

    prediction = lax.cond(in_generator, skip_assess, assess, score_full)
    grouped = prediction.reshape(half, 2, slice_rows, half_width)
    by_owner = jnp.concatenate([grouped[:, 1], grouped[:, 0]], axis=0)
    returned = lax.all_to_all(by_owner, "fsdp", split_axis=0, concat_axis=0, tiled=True)
    real_block = returned[:quarter].reshape(block_rows, half_width).astype(jnp.float32)
    fake_block = returned[quarter:half].reshape(block_rows, half_width).astype(jnp.float32)
    own_share = block_shares(lookup(noise_step, position[None]))[0]
    own_grad = (own_share * (real_block - fake_block)).astype(jnp.bfloat16)
    handed = jnp.where(in_generator, gen_noised[block_rows:], own_grad)
    taken = shifted(handed, "fsdp", half)

    def reverse(operands):
        grad_rows, normed = operands
        backward = lax.dot_general(
            grad_rows, weight_mine, (((1,), (1,)), ((), ())), preferred_element_type=jnp.float32
        )
        scaled = backward.reshape(2, block_rows, model_width) * (1.0 + gen_mod[:, None, :])
        return jnp.sum(scaled.reshape(2 * block_rows, model_width) * normed, axis=0) / block_rows

    def skip_reverse(operands):
        return jnp.zeros((model_width,), jnp.float32)

    grad_rows = jnp.concatenate([own_grad, taken], axis=0)
    gain_term = lax.cond(in_generator, reverse, skip_reverse, (grad_rows, gen_normed))
    gain_grad = lax.psum_scatter(gain_term, ("fsdp", "mp"), scatter_dimension=0, tiled=True)
    noised_out = jnp.where(in_generator, gen_noised[:block_rows], taken)
    return (noised_out, own_grad, gain_grad)


def on_tiles(
    noise_in,
    renoise,
    gen_step,
    noise_step,
    gen_weight,
    real_weight,
    fake_weight,
    gen_embed,
    real_embed,
    fake_embed,
    gen_gain,
    real_gain,
    fake_gain,
):
    g = lax.axis_size("fsdp") // 2
    r, h = noise_in.shape
    d = 2 * h
    w = h // g
    t = g * r
    blocks = gen_step.shape[0]
    f32, bf16 = jnp.float32, jnp.bfloat16
    tail = 16
    span = range(g)

    def place():
        position, c = lax.axis_index("fsdp"), lax.axis_index("mp")
        return lax.div(position, g), lax.rem(position, g), c

    def flat(s_, q_, c_):
        return (s_ * g + q_) * 2 + c_

    every = [(s_, q_, c_) for s_ in (0, 1) for q_ in span for c_ in (0, 1)]

    def in_square(value, k):
        return lax.ppermute(value, "fsdp", [(i, i ^ k) for i in range(2 * g)])

    def across(value):
        return lax.ppermute(value, "fsdp", [(i, i ^ g) for i in range(2 * g)])

    def cores(value):
        return lax.ppermute(value, "mp", [(0, 1), (1, 0)])

    def turned(value):
        return lax.ppermute(value, ("fsdp", "mp"), [(flat(*i), flat(i[2], i[1], i[0])) for i in every])

    whole = pl.BlockSpec(memory_space=pltpu.VMEM)
    scalars = pl.BlockSpec(memory_space=pltpu.SMEM)

    def call(kernel, operands, outs, flops, scratch=(), in_scalars=0):
        moved = sum(o.size * o.dtype.itemsize for o in operands)
        return pl.pallas_call(
            kernel,
            in_specs=[scalars] * in_scalars + [whole] * (len(operands) - in_scalars),
            out_specs=[whole] * len(outs),
            out_shape=[jax.ShapeDtypeStruct(*o) for o in outs],
            scratch_shapes=list(scratch),
            compiler_params=pltpu.CompilerParams(vmem_limit_bytes=40 * 1024 * 1024),
            cost_estimate=pl.CostEstimate(flops=flops, bytes_accessed=moved, transcendentals=0),
        )(*operands)

    def rows_of(columns):
        return jnp.broadcast_to(columns, (t, 128)).T[:8]

    def columns_of(rows):
        return rows.T[:, :1]

    def pack(rows, store):
        high = rows.astype(bf16)
        rest = rows - high.astype(f32)
        middle = rest.astype(bf16)
        low = (rest - middle.astype(f32)).astype(bf16)
        line = lax.broadcasted_iota(jnp.int32, rows.shape, 0)
        mixed = jnp.where(line == 0, high.astype(f32), jnp.where(line == 1, middle.astype(f32), low.astype(f32)))
        mixed = jnp.where(line < 3, mixed, 0.0)
        store(jnp.concatenate([mixed, jnp.zeros_like(mixed)], axis=0).astype(bf16))

    def unpack(block):
        return jnp.sum(block.astype(f32), axis=0, keepdims=True)

    def share(steps, block):
        return (steps[block].astype(f32) + 1.0) / (NT + 1.0)

    def band(j):
        return slice(j * r, (j + 1) * r)

    def lanes(k):
        return pl.ds(pl.multiple_of(k * w, w), w)

    def scales_kernel(features, gen_e, real_e, fake_e, gen_g, real_g, fake_g, out):
        s, _, _ = place()
        mine = pl.ds(pl.multiple_of(s * h, h), h)
        per = h // 128

        def gain(ref):
            return jnp.concatenate([ref[pl.ds(s * per + i, 1), :] for i in range(per)], axis=1)

        for n, (embed, gains) in enumerate(((gen_e, gen_g), (real_e, real_g), (fake_e, fake_g))):
            part = 0 if n == 0 else 1
            mod = 1.0 + jnp.dot(
                features[part], embed[:, mine], preferred_element_type=f32
            )
            if n == 0:
                out[3] = mod
            scale = mod * gain(gains)
            out[n] = -scale if n == 2 else scale

    features = jnp.stack(
        [step_features(gen_step, gen_embed.shape[0]), step_features(noise_step, gen_embed.shape[0])]
    )
    (scales,) = call(
        scales_kernel,
        [features, gen_embed, real_embed, fake_embed]
        + [v.reshape(-1, 128) for v in (gen_gain, real_gain, fake_gain)],
        [((4, blocks, h), f32)],
        2 * 3 * blocks * 128 * h,
    )

    depth = gen_weight.shape[0]
    fold = r // g

    def cut_gen_kernel(weight, *outs):
        _, q, _ = place()
        for k in span:
            outs[k][...] = weight[:, lanes(q ^ k)]

    def cut_score_kernel(real, fake, *outs):
        _, q, _ = place()
        for k in span:
            outs[k][0] = real[:, lanes(q ^ k)]
            outs[k][1] = fake[:, lanes(q ^ k)]

    def cut_rows_kernel(rows, fresh, *outs):
        _, q, _ = place()
        for k in span:
            outs[k][0:r, :] = rows[...]
            for i in span:
                outs[k][r : r + fold, i * w : (i + 1) * w] = fresh[i * fold : (i + 1) * fold, lanes(q ^ k)]

    x_turned, fresh_turned = turned(noise_in), turned(renoise)
    gen_sent = call(cut_gen_kernel, [gen_weight], [((depth, w), bf16)] * g, depth * h)
    gen_mine = [gen_sent[0]] + [in_square(gen_sent[k], k) for k in range(1, g)]
    x_turned, scales = lax.optimization_barrier((x_turned, scales))
    x_sent = call(cut_rows_kernel, [x_turned, fresh_turned], [((r + fold, h), bf16)] * g, r * h)
    x = [x_sent[0]] + [in_square(x_sent[k], k) for k in range(1, g)]
    gen_swap, x[1] = lax.optimization_barrier((gen_mine, x[1]))
    gen_other = [cores(v) for v in gen_swap]
    real_weight, fake_weight, _ = lax.optimization_barrier((real_weight, fake_weight, x_turned))
    score_sent = call(cut_score_kernel, [real_weight, fake_weight], [((2, depth, w), bf16)] * g, 2 * depth * h)
    score_mine = [score_sent[0]] + [in_square(score_sent[k], k) for k in range(1, g)]

    def generate_kernel(steps, *refs):
        xs, scale, own, other = refs[:g], refs[g], refs[g + 1 : 2 * g + 1], refs[2 * g + 1 : 3 * g + 1]
        keep, away, sums, base, lift = refs[3 * g + 1 :]
        s, q, c = place()
        totals = []
        for j in span:
            wide = xs[j][0:r, :].astype(f32)
            totals.append(jnp.sum(wide * wide, axis=1, keepdims=True))
            lift[band(j), :] = (wide * scale[0, pl.ds(c * g + (q ^ j), 1), :]).astype(bf16)
            part = share(steps, c * g + (q ^ j))
            for i in span:
                some = slice(i * fold, (i + 1) * fold)
                base[j * r + i * fold : j * r + (i + 1) * fold, :] = (1.0 - part) * xs[j][some, lanes(q)].astype(
                    f32
                ) + part * xs[j][r : r + fold, i * w : (i + 1) * w].astype(f32)
        here = jnp.zeros((t, w), f32)
        there = jnp.zeros((t, w), f32)
        for k in span:
            part = lift[:, lanes(q ^ k)]
            here = here + jnp.dot(part, own[k][...], preferred_element_type=f32)
            there = there + jnp.dot(part, other[k][...], preferred_element_type=f32)
        stays = s == c
        keep[...] = jnp.where(stays, here, there)
        away[0:t, :] = jnp.where(stays, there, here).astype(bf16)
        rows = rows_of(jnp.concatenate(totals, axis=0))
        sums[...] = rows

        def store(value):
            away[t : t + tail, 0:t] = value

        if w > t:
            away[t : t + tail, t:] = jnp.zeros((tail, w - t), bf16)
        pack(rows, store)

    keep, away, x_sums, base = call(
        generate_kernel,
        [noise_step] + x + [scales] + gen_mine + gen_other,
        [((t, w), f32), ((t + tail, w), bf16), ((8, t), f32), ((t, w), f32)],
        4 * t * h * w,
        [pltpu.VMEM((t, h), bf16)],
        in_scalars=1,
    )

    def inverse_rms(sums, came):
        total = sums[...] + unpack(came[t : t + tail, 0:t])
        return columns_of(lax.rsqrt(total / d + norm_epsilon))

    def blend_kernel(steps, keep, came, sums, base, noised, root):
        _, q, c = place()
        inverse = inverse_rms(sums, came)
        root[...] = jnp.broadcast_to(inverse, (t, 128))
        for j in span:
            stay = 1.0 - share(steps, c * g + (q ^ j))
            made = keep[band(j), :] + came[band(j), :].astype(f32)
            noised[band(j), :] = (base[band(j), :] + (stay * inverse[band(j), :]) * made).astype(bf16)

    noised_mine, x_root = call(
        blend_kernel,
        [noise_step, keep, across(away), x_sums, base],
        [((t, w), bf16), ((t, 128), f32)],
        10 * t * w,
        in_scalars=1,
    )
    noised_owned = turned(noised_mine)
    noised = [noised_mine] + [in_square(noised_mine, k) for k in range(1, g)]
    noised_owned, score_scales = lax.optimization_barrier((noised_owned, scales))

    def score_kernel(*refs):
        ns, scale, own = refs[:g], refs[g], refs[g + 1 : 2 * g + 1]
        gap, away, sums, lifts = refs[2 * g + 1 :]
        _, q, c = place()
        totals = [jnp.zeros((r, 1), f32) for _ in span]
        here = jnp.zeros((t, w), f32)
        for k in span:
            columns = slice(k * w, (k + 1) * w)
            for j in span:
                block = pl.ds(c * g + (q ^ j), 1)
                wide = ns[k][band(j ^ k), :].astype(f32)
                totals[j] = totals[j] + jnp.sum(wide * wide, axis=1, keepdims=True)
                for n in (0, 1):
                    lifts[n, band(j), columns] = (wide * scale[1 + n, block, lanes(q ^ k)]).astype(bf16)
            for n in (0, 1):
                here = here + jnp.dot(lifts[n, :, columns], own[k][n], preferred_element_type=f32)
        gap[...] = here
        away[0:t, :] = here.astype(bf16)
        rows = rows_of(jnp.concatenate(totals, axis=0))
        sums[...] = rows
        if w > t:
            away[t : t + tail, t:] = jnp.zeros((tail, w - t), bf16)

        def store(value):
            away[t : t + tail, 0:t] = value

        pack(rows, store)

    gap_here, away_here, noised_sums, lifts = call(
        score_kernel,
        noised + [score_scales] + score_mine,
        [((t, w), f32), ((t + tail, w), bf16), ((8, t), f32), ((2, t, h), bf16)],
        4 * t * h * w,
    )
    came_here = across(away_here)
    score_mine, away_here = lax.optimization_barrier((score_mine, away_here))
    score_other = [cores(v) for v in score_mine]

    def score_rest_kernel(lifts, *refs):
        other, (gap, away) = refs[:g], refs[g:]
        there = jnp.zeros((t, w), f32)
        for k in span:
            for n in (0, 1):
                there = there + jnp.dot(
                    lifts[n, :, k * w : (k + 1) * w], other[k][n], preferred_element_type=f32
                )
        gap[...] = there
        away[...] = there.astype(bf16)

    gap_there, away_there = call(
        score_rest_kernel, [lifts] + score_other, [((t, w), f32), ((t, w), bf16)], 4 * t * h * w
    )
    came_there = across(away_there)

    def gradient(steps, gap, came, inverse, grad, outs):
        _, q, c = place()
        for j in span:
            part = share(steps, c * g + (q ^ j))
            value = (part * inverse[band(j), :]) * (gap[band(j), :] + came[band(j), :].astype(f32))
            grad[band(j), :] = value.astype(bf16)
            outs[j][0:r, :] = value.astype(bf16)

    def gain_sums(grad, tile, xs, root, scale):
        _, q, c = place()
        sums = []
        for k in span:
            back = lax.dot_general(grad[...], tile[k][...], (((1,), (1,)), ((), ())), preferred_element_type=f32)
            total = jnp.zeros((1, w), f32)
            for j in span:
                normed = xs[j][0:r, lanes(q ^ k)].astype(f32) * root[band(j), :1]
                summed = jnp.sum(back[band(j), :] * normed, axis=0, keepdims=True)
                total = total + summed * scale[3, pl.ds(c * g + (q ^ j), 1), lanes(q ^ k)]
            sums.append(total)
        return sums

    def backward_kernel(steps, gap, came, sums, root, scale, owned, *refs):
        xs, own, outs, (noised_root, partial, grad) = refs[:g], refs[g : 2 * g], refs[2 * g : 3 * g], refs[3 * g :]
        inverse = inverse_rms(sums, came)
        noised_root[...] = jnp.broadcast_to(inverse, (t, 128))
        gradient(steps, gap, came, inverse, grad, outs)
        for k, total in enumerate(gain_sums(grad, own, xs, root, scale)):
            partial[k : k + 1, :] = total
            outs[k][r : 2 * r, :] = owned[band(k), :]

    *sent_here, noised_root, partial = call(
        backward_kernel,
        [noise_step, gap_here, came_here, noised_sums, x_root, scales, noised_owned] + x + gen_mine,
        [((2 * r, w), bf16)] * g + [((t, 128), f32), ((8, w), f32)],
        2 * t * h * w,
        [pltpu.VMEM((t, w), bf16)],
        in_scalars=1,
    )
    arrived_here = [sent_here[0]] + [in_square(sent_here[k], k) for k in range(1, g)]

    def backward_rest_kernel(steps, gap, came, noised_root, partial, root, scale, *refs):
        xs, other, outs, (grad,) = refs[:g], refs[g : 2 * g], refs[2 * g : 3 * g], refs[3 * g :]
        gradient(steps, gap, came, noised_root[:, :1], grad, outs)
        for k, total in enumerate(gain_sums(grad, other, xs, root, scale)):

            def store(value):
                outs[k][r : r + tail, :] = value

            pack(jnp.broadcast_to((total + partial[k : k + 1, :]) / r, (8, w)), store)

    sent_there = call(
        backward_rest_kernel,
        [noise_step, gap_there, came_there, noised_root, partial, x_root, scales] + x + gen_other,
        [((r + tail, w), bf16)] * g,
        2 * t * h * w,
        [pltpu.VMEM((t, w), bf16)],
        in_scalars=1,
    )
    arrived_there = [sent_there[0]] + [in_square(sent_there[k], k) for k in range(1, g)]

    def gather_kernel(*refs):
        a, b, (here, there, gains, noised) = refs[:g], refs[g : 2 * g], refs[2 * g :]
        _, q, _ = place()
        total = jnp.zeros((1, w), f32)
        for k in span:
            here[:, lanes(q ^ k)] = a[k][0:r, :]
            noised[:, lanes(q ^ k)] = a[k][r : 2 * r, :]
            there[0:r, lanes(q ^ k)] = b[k][0:r, :]
            total = total + unpack(b[k][r : r + tail, :])
        gains[...] = total

        def store(value):
            there[r : r + tail, :w] = value

        pack(jnp.broadcast_to(total, (8, w)), store)
        there[r : r + tail, w:] = jnp.zeros((tail, h - w), bf16)

    here, there, gains, noised_out = call(
        gather_kernel,
        arrived_here + arrived_there,
        [((r, h), bf16), ((r + tail, h), bf16), ((1, w), f32), ((r, h), bf16)],
        t * h,
    )
    other_core = cores(there)

    def finish_kernel(here, gains, came, grad, gain):
        s, _, c = place()
        grad[...] = jnp.where(s == c, here[...], came[0:r, :])
        both = gains[...] + unpack(came[r : r + tail, :w])
        gain[...] = jnp.where(c == 0, both[:, : w // 2], both[:, w // 2 :])

    latent_grad, gain = call(
        finish_kernel, [here, gains, other_core], [((r, h), bf16), ((1, w // 2), f32)], r * h
    )
    return (noised_out, latent_grad, gain[0])


def solution(mesh):
    positions = mesh.shape["fsdp"]
    on_device = on_tiles if positions in (4, 8) and mesh.shape["mp"] == 2 else on_groups
    return jax.shard_map(
        on_device,
        mesh=mesh,
        in_specs=(
            P(("rep", "fsdp"), "mp"),
            P(("rep", "fsdp"), "mp"),
            P("rep"),
            P("rep"),
            P("fsdp", "mp"),
            P("fsdp", "mp"),
            P("fsdp", "mp"),
            P(),
            P(),
            P(),
            P(),
            P(),
            P(),
        ),
        out_specs=(P(("rep", "fsdp"), "mp"), P(("rep", "fsdp"), "mp"), P(("rep", "fsdp", "mp"))),
        check_vma=False,
    )
```

```python
import math

import jax
import jax.numpy as jnp
from jax import lax
from jax.experimental import pallas as pl
from jax.experimental.pallas import tpu as pltpu
from jax.sharding import PartitionSpec as P

NT = 1000


norm_epsilon = 1e-06


def from_behind(value, axis, by):
    size = lax.axis_size(axis)
    pairs = [(i, i + by) for i in range(size) if 0 <= i + by < size]
    return lax.ppermute(value, axis, pairs)


def shifted(value, axis, by):
    size = lax.axis_size(axis)
    return lax.ppermute(value, axis, [(i, (i + by) % size) for i in range(size)])


def step_features(step_ids, feature_width):
    half_width = feature_width // 2
    frequency = jnp.exp(-math.log(10000.0) * jnp.arange(half_width, dtype=jnp.float32) / half_width)
    angles = step_ids.astype(jnp.float32)[:, None] * frequency[None, :]
    return jnp.concatenate([jnp.cos(angles), jnp.sin(angles)], axis=1).astype(jnp.bfloat16)


def lookup(step_table, block_ids):
    matches = block_ids[:, None] == jnp.arange(step_table.shape[0], dtype=jnp.int32)[None, :]
    return jnp.sum(jnp.where(matches, step_table[None, :], 0), axis=1)


def block_shares(step_ids):
    return ((step_ids.astype(jnp.float32) + 1.0) / (NT + 1.0))[:, None, None]


def modulate(full_rows, gain_vec, modulation):
    blocks = modulation.shape[0]
    values = full_rows.astype(jnp.float32)
    normed = values * lax.rsqrt(jnp.mean(values * values, axis=1, keepdims=True) + norm_epsilon)
    lifted = normed.reshape(blocks, -1, values.shape[1]) * gain_vec * (1.0 + modulation[:, None, :])
    return (normed, lifted.reshape(values.shape).astype(jnp.bfloat16))


def on_groups(
    noise_in,
    renoise,
    gen_step,
    noise_step,
    gen_weight,
    real_weight,
    fake_weight,
    gen_embed,
    real_embed,
    fake_embed,
    gen_gain,
    real_gain,
    fake_gain,
):
    devices = lax.axis_size("fsdp")
    quarter = devices // 4
    half = 2 * quarter
    position = lax.axis_index("fsdp")
    block_rows = noise_in.shape[0]
    half_width = noise_in.shape[1]
    model_width = gen_gain.shape[0]
    feature_width = gen_embed.shape[0]
    slice_rows = 4 * block_rows // devices
    group_role = (position >= quarter).astype(jnp.int32) + (position >= half).astype(jnp.int32)
    in_generator = group_role == 2
    slot_ids = jnp.arange(devices, dtype=jnp.int32)
    slot_role = (
        (slot_ids >= quarter).astype(jnp.int32) + (slot_ids >= half).astype(jnp.int32)
    ).reshape(devices, 1, 1)
    outgoing = jnp.where(
        slot_role == 2,
        gen_weight[None],
        jnp.where(slot_role == 0, real_weight[None], fake_weight[None]),
    )
    received = lax.all_to_all(outgoing, "fsdp", split_axis=0, concat_axis=0, tiled=True)
    weight_mine = received.reshape(model_width, half_width)
    embed_mine = jnp.where(
        group_role == 2, gen_embed, jnp.where(group_role == 0, real_embed, fake_embed)
    )
    gain_mine = jnp.where(
        group_role == 2, gen_gain, jnp.where(group_role == 0, real_gain, fake_gain)
    )
    partner_noise, partner_renoise = from_behind((noise_in, renoise), "fsdp", half)
    gen_ids = jnp.stack([position, (position + half) % devices])
    gen_mod = jnp.dot(
        step_features(lookup(gen_step, gen_ids), feature_width),
        embed_mine,
        preferred_element_type=jnp.float32,
    )
    gen_shares = block_shares(lookup(noise_step, gen_ids))
    gen_rows = jnp.concatenate([noise_in, partner_noise], axis=0)
    gen_noise = jnp.concatenate([renoise, partner_renoise], axis=0)
    gen_full = lax.all_gather(gen_rows, "mp", axis=1, tiled=True)

    def generate(operands):
        full_rows, own_rows, fresh_noise = operands
        normed, lifted = modulate(full_rows, gain_mine, gen_mod)
        latents = own_rows.astype(jnp.float32) + jnp.dot(
            lifted, weight_mine, preferred_element_type=jnp.float32
        )
        blended = (1.0 - gen_shares) * latents.reshape(
            2, block_rows, half_width
        ) + gen_shares * fresh_noise.astype(jnp.float32).reshape(2, block_rows, half_width)
        return (blended.reshape(2 * block_rows, half_width).astype(jnp.bfloat16), normed)

    def skip_generate(operands):
        return (
            jnp.zeros((2 * block_rows, half_width), jnp.bfloat16),
            jnp.zeros((2 * block_rows, model_width), jnp.float32),
        )

    gen_noised, gen_normed = lax.cond(
        in_generator, generate, skip_generate, (gen_full, gen_rows, gen_noise)
    )
    width_now = gen_noised.shape[1]
    pieces = (
        gen_noised.reshape(2, quarter, slice_rows, width_now)
        .transpose(1, 0, 2, 3)
        .reshape(quarter, 2 * slice_rows, width_now)
    )
    send_rows = jnp.concatenate(
        [pieces, pieces, jnp.zeros((half, 2 * slice_rows, width_now), jnp.bfloat16)], axis=0
    )
    arrived = lax.all_to_all(send_rows, "fsdp", split_axis=0, concat_axis=0, tiled=True)
    score_rows = arrived[half:].reshape(2 * half * slice_rows, width_now)
    gen_slots = jnp.arange(half, dtype=jnp.int32)
    score_ids = jnp.stack([gen_slots + half, gen_slots], axis=1).reshape(2 * half)
    score_mod = jnp.dot(
        step_features(lookup(noise_step, score_ids), feature_width),
        embed_mine,
        preferred_element_type=jnp.float32,
    )
    score_full = lax.all_gather(score_rows, "mp", axis=1, tiled=True)

    def assess(full_rows):
        normed, lifted = modulate(full_rows, gain_mine, score_mod)
        return jnp.dot(lifted, weight_mine, preferred_element_type=jnp.float32).astype(jnp.bfloat16)

    def skip_assess(full_rows):
        return jnp.zeros((2 * half * slice_rows, half_width), jnp.bfloat16)

    prediction = lax.cond(in_generator, skip_assess, assess, score_full)
    grouped = prediction.reshape(half, 2, slice_rows, half_width)
    by_owner = jnp.concatenate([grouped[:, 1], grouped[:, 0]], axis=0)
    returned = lax.all_to_all(by_owner, "fsdp", split_axis=0, concat_axis=0, tiled=True)
    real_block = returned[:quarter].reshape(block_rows, half_width).astype(jnp.float32)
    fake_block = returned[quarter:half].reshape(block_rows, half_width).astype(jnp.float32)
    own_share = block_shares(lookup(noise_step, position[None]))[0]
    own_grad = (own_share * (real_block - fake_block)).astype(jnp.bfloat16)
    handed = jnp.where(in_generator, gen_noised[block_rows:], own_grad)
    taken = shifted(handed, "fsdp", half)

    def reverse(operands):
        grad_rows, normed = operands
        backward = lax.dot_general(
            grad_rows, weight_mine, (((1,), (1,)), ((), ())), preferred_element_type=jnp.float32
        )
        scaled = backward.reshape(2, block_rows, model_width) * (1.0 + gen_mod[:, None, :])
        return jnp.sum(scaled.reshape(2 * block_rows, model_width) * normed, axis=0) / block_rows

    def skip_reverse(operands):
        return jnp.zeros((model_width,), jnp.float32)

    grad_rows = jnp.concatenate([own_grad, taken], axis=0)
    gain_term = lax.cond(in_generator, reverse, skip_reverse, (grad_rows, gen_normed))
    gain_grad = lax.psum_scatter(gain_term, ("fsdp", "mp"), scatter_dimension=0, tiled=True)
    noised_out = jnp.where(in_generator, gen_noised[:block_rows], taken)
    return (noised_out, own_grad, gain_grad)


def on_tiles(
    noise_in,
    renoise,
    gen_step,
    noise_step,
    gen_weight,
    real_weight,
    fake_weight,
    gen_embed,
    real_embed,
    fake_embed,
    gen_gain,
    real_gain,
    fake_gain,
):
    g = lax.axis_size("fsdp") // 2
    r, h = noise_in.shape
    d = 2 * h
    w = h // g
    t = g * r
    blocks = gen_step.shape[0]
    f32, bf16 = jnp.float32, jnp.bfloat16
    tail = 16
    span = range(g)

    def place():
        position, c = lax.axis_index("fsdp"), lax.axis_index("mp")
        return lax.div(position, g), lax.rem(position, g), c

    def flat(s_, q_, c_):
        return (s_ * g + q_) * 2 + c_

    every = [(s_, q_, c_) for s_ in (0, 1) for q_ in span for c_ in (0, 1)]

    def in_square(value, k):
        return lax.ppermute(value, "fsdp", [(i, i ^ k) for i in range(2 * g)])

    def across(value):
        return lax.ppermute(value, "fsdp", [(i, i ^ g) for i in range(2 * g)])

    def cores(value):
        return lax.ppermute(value, "mp", [(0, 1), (1, 0)])

    def turned(value):
        return lax.ppermute(value, ("fsdp", "mp"), [(flat(*i), flat(i[2], i[1], i[0])) for i in every])

    whole = pl.BlockSpec(memory_space=pltpu.VMEM)
    scalars = pl.BlockSpec(memory_space=pltpu.SMEM)

    def call(kernel, operands, outs, flops, scratch=(), in_scalars=0):
        moved = sum(o.size * o.dtype.itemsize for o in operands)
        return pl.pallas_call(
            kernel,
            in_specs=[scalars] * in_scalars + [whole] * (len(operands) - in_scalars),
            out_specs=[whole] * len(outs),
            out_shape=[jax.ShapeDtypeStruct(*o) for o in outs],
            scratch_shapes=list(scratch),
            compiler_params=pltpu.CompilerParams(vmem_limit_bytes=40 * 1024 * 1024),
            cost_estimate=pl.CostEstimate(flops=flops, bytes_accessed=moved, transcendentals=0),
        )(*operands)

    def rows_of(columns):
        return jnp.broadcast_to(columns, (t, 128)).T[:8]

    def columns_of(rows):
        return rows.T[:, :1]

    def pack(rows, store):
        high = rows.astype(bf16)
        rest = rows - high.astype(f32)
        middle = rest.astype(bf16)
        low = (rest - middle.astype(f32)).astype(bf16)
        line = lax.broadcasted_iota(jnp.int32, rows.shape, 0)
        mixed = jnp.where(line == 0, high.astype(f32), jnp.where(line == 1, middle.astype(f32), low.astype(f32)))
        mixed = jnp.where(line < 3, mixed, 0.0)
        store(jnp.concatenate([mixed, jnp.zeros_like(mixed)], axis=0).astype(bf16))

    def unpack(block):
        return jnp.sum(block.astype(f32), axis=0, keepdims=True)

    def share(steps, block):
        return (steps[block].astype(f32) + 1.0) / (NT + 1.0)

    def band(j):
        return slice(j * r, (j + 1) * r)

    def lanes(k):
        return pl.ds(pl.multiple_of(k * w, w), w)

    def scales_kernel(features, gen_e, real_e, fake_e, gen_g, real_g, fake_g, out):
        s, _, _ = place()
        mine = pl.ds(pl.multiple_of(s * h, h), h)
        per = h // 128

        def gain(ref):
            return jnp.concatenate([ref[pl.ds(s * per + i, 1), :] for i in range(per)], axis=1)

        for n, (embed, gains) in enumerate(((gen_e, gen_g), (real_e, real_g), (fake_e, fake_g))):
            part = 0 if n == 0 else 1
            mod = 1.0 + jnp.dot(
                features[part], embed[:, mine], preferred_element_type=f32
            )
            if n == 0:
                out[3] = mod
            scale = mod * gain(gains)
            out[n] = -scale if n == 2 else scale

    features = jnp.stack(
        [step_features(gen_step, gen_embed.shape[0]), step_features(noise_step, gen_embed.shape[0])]
    )
    (scales,) = call(
        scales_kernel,
        [features, gen_embed, real_embed, fake_embed]
        + [v.reshape(-1, 128) for v in (gen_gain, real_gain, fake_gain)],
        [((4, blocks, h), f32)],
        2 * 3 * blocks * 128 * h,
    )

    depth = gen_weight.shape[0]
    fold = r // g
    shared = g // 2

    def cut_gen_kernel(weight, *outs):
        _, q, _ = place()
        for k in span:
            outs[k][...] = weight[:, lanes(q ^ k)]

    def cut_score_kernel(real, fake, *outs):
        _, q, _ = place()
        for k in span:
            if k < shared:
                outs[k][0] = real[:, lanes(q ^ k)]
                outs[k][1] = fake[:, lanes(q ^ k)]
            else:
                for n, weight in enumerate((real, fake)):

                    @pl.when(lax.axis_index("rep") == n)
                    def _():
                        outs[k][...] = weight[:, lanes(q ^ k)]

    def cut_rows_kernel(rows, fresh, *outs):
        _, q, _ = place()
        for k in span:
            outs[k][0:r, :] = rows[...]
            for i in span:
                outs[k][r : r + fold, i * w : (i + 1) * w] = fresh[i * fold : (i + 1) * fold, lanes(q ^ k)]

    def swap_all(tile):
        counts = [v.size // (depth * w) for v in tile]

        def join_kernel(*refs):
            out, at = refs[-1], 0
            for ref, n in zip(refs[:-1], counts):
                for i in range(n):
                    out[at] = ref[i] if n > 1 else ref[...]
                    at += 1

        (joined,) = call(join_kernel, tile, [((sum(counts), depth, w), bf16)], depth * w)
        return cores(joined)

    x_turned, fresh_turned = turned(noise_in), turned(renoise)
    gen_sent = call(cut_gen_kernel, [gen_weight], [((depth, w), bf16)] * g, depth * h)
    gen_mine = [gen_sent[0]] + [in_square(gen_sent[k], k) for k in range(1, g)]
    x_turned, scales = lax.optimization_barrier((x_turned, scales))
    x_sent = call(cut_rows_kernel, [x_turned, fresh_turned], [((r + fold, h), bf16)] * g, r * h)
    x = [x_sent[0]] + [in_square(x_sent[k], k) for k in range(1, g)]
    gen_swap, x[1] = lax.optimization_barrier((gen_mine, x[1]))
    gen_other = [cores(v) for v in gen_swap]
    real_weight, fake_weight, _ = lax.optimization_barrier((real_weight, fake_weight, x_turned))
    score_sent = call(
        cut_score_kernel,
        [real_weight, fake_weight],
        [((2, depth, w), bf16)] * shared + [((depth, w), bf16)] * (g - shared),
        2 * depth * h,
    )
    score_mine = [score_sent[0]] + [in_square(score_sent[k], k) for k in range(1, g)]

    def generate_kernel(steps, *refs):
        xs, scale, own, other = refs[:g], refs[g], refs[g + 1 : 2 * g + 1], refs[2 * g + 1 : 3 * g + 1]
        keep, away, sums, base, lift = refs[3 * g + 1 :]
        s, q, c = place()
        totals = []
        for j in span:
            wide = xs[j][0:r, :].astype(f32)
            totals.append(jnp.sum(wide * wide, axis=1, keepdims=True))
            lift[band(j), :] = (wide * scale[0, pl.ds(c * g + (q ^ j), 1), :]).astype(bf16)
            part = share(steps, c * g + (q ^ j))
            for i in span:
                some = slice(i * fold, (i + 1) * fold)
                base[j * r + i * fold : j * r + (i + 1) * fold, :] = (1.0 - part) * xs[j][some, lanes(q)].astype(
                    f32
                ) + part * xs[j][r : r + fold, i * w : (i + 1) * w].astype(f32)
        here = jnp.zeros((t, w), f32)
        there = jnp.zeros((t, w), f32)
        for k in span:
            part = lift[:, lanes(q ^ k)]
            here = here + jnp.dot(part, own[k][...], preferred_element_type=f32)
            there = there + jnp.dot(part, other[k][...], preferred_element_type=f32)
        stays = s == c
        keep[...] = jnp.where(stays, here, there)
        away[0:t, :] = jnp.where(stays, there, here).astype(bf16)
        rows = rows_of(jnp.concatenate(totals, axis=0))
        sums[...] = rows

        def store(value):
            away[t : t + tail, 0:t] = value

        if w > t:
            away[t : t + tail, t:] = jnp.zeros((tail, w - t), bf16)
        pack(rows, store)

    keep, away, x_sums, base = call(
        generate_kernel,
        [noise_step] + x + [scales] + gen_mine + gen_other,
        [((t, w), f32), ((t + tail, w), bf16), ((8, t), f32), ((t, w), f32)],
        4 * t * h * w,
        [pltpu.VMEM((t, h), bf16)],
        in_scalars=1,
    )

    def inverse_rms(sums, came):
        total = sums[...] + unpack(came[t : t + tail, 0:t])
        return columns_of(lax.rsqrt(total / d + norm_epsilon))

    def blend_kernel(steps, keep, came, sums, base, noised, root):
        _, q, c = place()
        inverse = inverse_rms(sums, came)
        root[...] = jnp.broadcast_to(inverse, (t, 128))
        for j in span:
            stay = 1.0 - share(steps, c * g + (q ^ j))
            made = keep[band(j), :] + came[band(j), :].astype(f32)
            noised[band(j), :] = (base[band(j), :] + (stay * inverse[band(j), :]) * made).astype(bf16)

    came, *fetched = lax.optimization_barrier((across(away), *score_mine[shared:g]))
    score_mine[shared:g] = fetched
    for k in range(shared, g):
        score_mine.append(lax.ppermute(score_mine[k], "rep", [(0, 1), (1, 0)]))
    noised_mine, x_root = call(
        blend_kernel,
        [noise_step, keep, came, x_sums, base],
        [((t, w), bf16), ((t, 128), f32)],
        10 * t * w,
        in_scalars=1,
    )
    noised_last, score_mine[1] = lax.optimization_barrier((noised_mine, score_mine[1]))
    noised = [noised_mine, in_square(noised_last, 1)] + [in_square(noised_mine, k) for k in range(2, g)]

    tiles = len(score_mine)

    def score_product(lifts, tile):
        copy = lax.axis_index("rep")
        total = jnp.zeros((t, w), f32)
        for k in span:
            columns = slice(k * w, (k + 1) * w)
            if k < shared:
                pairs = [(tile[k][0], 0), (tile[k][1], 1)]
            else:
                pairs = [(tile[k][...], copy), (tile[k + g - shared][...], 1 - copy)]
            for part, n in pairs:
                total = total + jnp.dot(lifts[n, :, columns], part, preferred_element_type=f32)
        return total

    def score_kernel(*refs):
        ns, scale, own = refs[:g], refs[g], refs[g + 1 : g + 1 + tiles]
        gap, away, sums, lifts = refs[g + 1 + tiles :]
        _, q, c = place()
        totals = [jnp.zeros((r, 1), f32) for _ in span]
        for k in span:
            columns = slice(k * w, (k + 1) * w)
            for j in span:
                block = pl.ds(c * g + (q ^ j), 1)
                wide = ns[k][band(j ^ k), :].astype(f32)
                totals[j] = totals[j] + jnp.sum(wide * wide, axis=1, keepdims=True)
                for n in (0, 1):
                    lifts[n, band(j), columns] = (wide * scale[1 + n, block, lanes(q ^ k)]).astype(bf16)
        here = score_product(lifts, own)
        gap[...] = here
        away[0:t, :] = here.astype(bf16)
        rows = rows_of(jnp.concatenate(totals, axis=0))
        sums[...] = rows
        if w > t:
            away[t : t + tail, t:] = jnp.zeros((tail, w - t), bf16)

        def store(value):
            away[t : t + tail, 0:t] = value

        pack(rows, store)

    gap_here, away_here, noised_sums, lifts = call(
        score_kernel,
        noised + [scales] + score_mine,
        [((t, w), f32), ((t + tail, w), bf16), ((8, t), f32), ((2, t, h), bf16)],
        4 * t * h * w,
    )
    came_here = across(away_here)
    score_mine, noised_home, away_here = lax.optimization_barrier((score_mine, noised_mine, away_here))
    noised_owned = turned(noised_home)
    score_other = swap_all(score_mine)

    def score_rest_kernel(lifts, other, gap, away):
        there = score_product(
            lifts,
            [(other[2 * k], other[2 * k + 1]) for k in range(shared)]
            + [other[shared + k] for k in range(shared, tiles)],
        )
        gap[...] = there
        away[...] = there.astype(bf16)

    gap_there, away_there = call(
        score_rest_kernel, [lifts, score_other], [((t, w), f32), ((t, w), bf16)], 4 * t * h * w
    )
    came_there = across(away_there)

    def gradient(steps, gap, came, inverse, grad, outs):
        _, q, c = place()
        for j in span:
            part = share(steps, c * g + (q ^ j))
            value = (part * inverse[band(j), :]) * (gap[band(j), :] + came[band(j), :].astype(f32))
            grad[band(j), :] = value.astype(bf16)
            outs[j][0:r, :] = value.astype(bf16)

    def gain_sums(grad, tile, xs, root, scale):
        _, q, c = place()
        sums = []
        for k in span:
            back = lax.dot_general(grad[...], tile[k][...], (((1,), (1,)), ((), ())), preferred_element_type=f32)
            total = jnp.zeros((1, w), f32)
            for j in span:
                normed = xs[j][0:r, lanes(q ^ k)].astype(f32) * root[band(j), :1]
                summed = jnp.sum(back[band(j), :] * normed, axis=0, keepdims=True)
                total = total + summed * scale[3, pl.ds(c * g + (q ^ j), 1), lanes(q ^ k)]
            sums.append(total)
        return sums

    def backward_kernel(steps, gap, came, sums, root, scale, owned, *refs):
        xs, own, outs, (noised_root, partial, grad) = refs[:g], refs[g : 2 * g], refs[2 * g : 3 * g], refs[3 * g :]
        inverse = inverse_rms(sums, came)
        noised_root[...] = jnp.broadcast_to(inverse, (t, 128))
        gradient(steps, gap, came, inverse, grad, outs)
        for k, total in enumerate(gain_sums(grad, own, xs, root, scale)):
            partial[k : k + 1, :] = total
            outs[k][r : 2 * r, :] = owned[band(k), :]

    *sent_here, noised_root, partial = call(
        backward_kernel,
        [noise_step, gap_here, came_here, noised_sums, x_root, scales, noised_owned] + x + gen_mine,
        [((2 * r, w), bf16)] * g + [((t, 128), f32), ((8, w), f32)],
        2 * t * h * w,
        [pltpu.VMEM((t, w), bf16)],
        in_scalars=1,
    )
    arrived_here = [sent_here[0]] + [in_square(sent_here[k], k) for k in range(1, g)]

    def backward_rest_kernel(steps, gap, came, noised_root, partial, root, scale, *refs):
        xs, other, outs, (grad,) = refs[:g], refs[g : 2 * g], refs[2 * g : 3 * g], refs[3 * g :]
        gradient(steps, gap, came, noised_root[:, :1], grad, outs)
        for k, total in enumerate(gain_sums(grad, other, xs, root, scale)):

            def store(value):
                outs[k][r : r + tail, :] = value

            pack(jnp.broadcast_to((total + partial[k : k + 1, :]) / r, (8, w)), store)

    sent_there = call(
        backward_rest_kernel,
        [noise_step, gap_there, came_there, noised_root, partial, x_root, scales] + x + gen_other,
        [((r + tail, w), bf16)] * g,
        2 * t * h * w,
        [pltpu.VMEM((t, w), bf16)],
        in_scalars=1,
    )
    arrived_there = [sent_there[0]] + [in_square(sent_there[k], k) for k in range(1, g)]

    def gather_kernel(*refs):
        a, b, (here, there, gains, noised) = refs[:g], refs[g : 2 * g], refs[2 * g :]
        _, q, _ = place()
        total = jnp.zeros((1, w), f32)
        for k in span:
            here[:, lanes(q ^ k)] = a[k][0:r, :]
            noised[:, lanes(q ^ k)] = a[k][r : 2 * r, :]
            there[0:r, lanes(q ^ k)] = b[k][0:r, :]
            total = total + unpack(b[k][r : r + tail, :])
        gains[...] = total

        def store(value):
            there[r : r + tail, :w] = value

        pack(jnp.broadcast_to(total, (8, w)), store)
        there[r : r + tail, w:] = jnp.zeros((tail, h - w), bf16)

    here, there, gains, noised_out = call(
        gather_kernel,
        arrived_here + arrived_there,
        [((r, h), bf16), ((r + tail, h), bf16), ((1, w), f32), ((r, h), bf16)],
        t * h,
    )
    other_core = cores(there)

    def finish_kernel(here, gains, came, grad, gain):
        s, _, c = place()
        grad[...] = jnp.where(s == c, here[...], came[0:r, :])
        both = gains[...] + unpack(came[r : r + tail, :w])
        gain[...] = jnp.where(c == 0, both[:, : w // 2], both[:, w // 2 :])

    latent_grad, gain = call(
        finish_kernel, [here, gains, other_core], [((r, h), bf16), ((1, w // 2), f32)], r * h
    )
    return (noised_out, latent_grad, gain[0])


def solution(mesh):
    positions = mesh.shape["fsdp"]
    on_device = on_tiles if (positions, mesh.shape["rep"], mesh.shape["mp"]) == (8, 2, 2) else on_groups
    return jax.shard_map(
        on_device,
        mesh=mesh,
        in_specs=(
            P(("rep", "fsdp"), "mp"),
            P(("rep", "fsdp"), "mp"),
            P("rep"),
            P("rep"),
            P("fsdp", "mp"),
            P("fsdp", "mp"),
            P("fsdp", "mp"),
            P(),
            P(),
            P(),
            P(),
            P(),
            P(),
        ),
        out_specs=(P(("rep", "fsdp"), "mp"), P(("rep", "fsdp"), "mp"), P(("rep", "fsdp", "mp"))),
        check_vma=False,
    )
```

```python
import math

import jax
import jax.numpy as jnp
from jax import lax
from jax.experimental import pallas as pl
from jax.experimental.pallas import tpu as pltpu
from jax.sharding import PartitionSpec as P

NT = 1000


norm_epsilon = 1e-06


def from_behind(value, axis, by):
    size = lax.axis_size(axis)
    pairs = [(i, i + by) for i in range(size) if 0 <= i + by < size]
    return lax.ppermute(value, axis, pairs)


def shifted(value, axis, by):
    size = lax.axis_size(axis)
    return lax.ppermute(value, axis, [(i, (i + by) % size) for i in range(size)])


def step_features(step_ids, feature_width):
    half_width = feature_width // 2
    frequency = jnp.exp(-math.log(10000.0) * jnp.arange(half_width, dtype=jnp.float32) / half_width)
    angles = step_ids.astype(jnp.float32)[:, None] * frequency[None, :]
    return jnp.concatenate([jnp.cos(angles), jnp.sin(angles)], axis=1).astype(jnp.bfloat16)


def lookup(step_table, block_ids):
    matches = block_ids[:, None] == jnp.arange(step_table.shape[0], dtype=jnp.int32)[None, :]
    return jnp.sum(jnp.where(matches, step_table[None, :], 0), axis=1)


def block_shares(step_ids):
    return ((step_ids.astype(jnp.float32) + 1.0) / (NT + 1.0))[:, None, None]


def modulate(full_rows, gain_vec, modulation):
    blocks = modulation.shape[0]
    values = full_rows.astype(jnp.float32)
    normed = values * lax.rsqrt(jnp.mean(values * values, axis=1, keepdims=True) + norm_epsilon)
    lifted = normed.reshape(blocks, -1, values.shape[1]) * gain_vec * (1.0 + modulation[:, None, :])
    return (normed, lifted.reshape(values.shape).astype(jnp.bfloat16))


def on_groups(
    noise_in,
    renoise,
    gen_step,
    noise_step,
    gen_weight,
    real_weight,
    fake_weight,
    gen_embed,
    real_embed,
    fake_embed,
    gen_gain,
    real_gain,
    fake_gain,
):
    devices = lax.axis_size("fsdp")
    quarter = devices // 4
    half = 2 * quarter
    position = lax.axis_index("fsdp")
    block_rows = noise_in.shape[0]
    half_width = noise_in.shape[1]
    model_width = gen_gain.shape[0]
    feature_width = gen_embed.shape[0]
    slice_rows = 4 * block_rows // devices
    group_role = (position >= quarter).astype(jnp.int32) + (position >= half).astype(jnp.int32)
    in_generator = group_role == 2
    slot_ids = jnp.arange(devices, dtype=jnp.int32)
    slot_role = (
        (slot_ids >= quarter).astype(jnp.int32) + (slot_ids >= half).astype(jnp.int32)
    ).reshape(devices, 1, 1)
    outgoing = jnp.where(
        slot_role == 2,
        gen_weight[None],
        jnp.where(slot_role == 0, real_weight[None], fake_weight[None]),
    )
    received = lax.all_to_all(outgoing, "fsdp", split_axis=0, concat_axis=0, tiled=True)
    weight_mine = received.reshape(model_width, half_width)
    embed_mine = jnp.where(
        group_role == 2, gen_embed, jnp.where(group_role == 0, real_embed, fake_embed)
    )
    gain_mine = jnp.where(
        group_role == 2, gen_gain, jnp.where(group_role == 0, real_gain, fake_gain)
    )
    partner_noise, partner_renoise = from_behind((noise_in, renoise), "fsdp", half)
    gen_ids = jnp.stack([position, (position + half) % devices])
    gen_mod = jnp.dot(
        step_features(lookup(gen_step, gen_ids), feature_width),
        embed_mine,
        preferred_element_type=jnp.float32,
    )
    gen_shares = block_shares(lookup(noise_step, gen_ids))
    gen_rows = jnp.concatenate([noise_in, partner_noise], axis=0)
    gen_noise = jnp.concatenate([renoise, partner_renoise], axis=0)
    gen_full = lax.all_gather(gen_rows, "mp", axis=1, tiled=True)

    def generate(operands):
        full_rows, own_rows, fresh_noise = operands
        normed, lifted = modulate(full_rows, gain_mine, gen_mod)
        latents = own_rows.astype(jnp.float32) + jnp.dot(
            lifted, weight_mine, preferred_element_type=jnp.float32
        )
        blended = (1.0 - gen_shares) * latents.reshape(
            2, block_rows, half_width
        ) + gen_shares * fresh_noise.astype(jnp.float32).reshape(2, block_rows, half_width)
        return (blended.reshape(2 * block_rows, half_width).astype(jnp.bfloat16), normed)

    def skip_generate(operands):
        return (
            jnp.zeros((2 * block_rows, half_width), jnp.bfloat16),
            jnp.zeros((2 * block_rows, model_width), jnp.float32),
        )

    gen_noised, gen_normed = lax.cond(
        in_generator, generate, skip_generate, (gen_full, gen_rows, gen_noise)
    )
    width_now = gen_noised.shape[1]
    pieces = (
        gen_noised.reshape(2, quarter, slice_rows, width_now)
        .transpose(1, 0, 2, 3)
        .reshape(quarter, 2 * slice_rows, width_now)
    )
    send_rows = jnp.concatenate(
        [pieces, pieces, jnp.zeros((half, 2 * slice_rows, width_now), jnp.bfloat16)], axis=0
    )
    arrived = lax.all_to_all(send_rows, "fsdp", split_axis=0, concat_axis=0, tiled=True)
    score_rows = arrived[half:].reshape(2 * half * slice_rows, width_now)
    gen_slots = jnp.arange(half, dtype=jnp.int32)
    score_ids = jnp.stack([gen_slots + half, gen_slots], axis=1).reshape(2 * half)
    score_mod = jnp.dot(
        step_features(lookup(noise_step, score_ids), feature_width),
        embed_mine,
        preferred_element_type=jnp.float32,
    )
    score_full = lax.all_gather(score_rows, "mp", axis=1, tiled=True)

    def assess(full_rows):
        normed, lifted = modulate(full_rows, gain_mine, score_mod)
        return jnp.dot(lifted, weight_mine, preferred_element_type=jnp.float32).astype(jnp.bfloat16)

    def skip_assess(full_rows):
        return jnp.zeros((2 * half * slice_rows, half_width), jnp.bfloat16)

    prediction = lax.cond(in_generator, skip_assess, assess, score_full)
    grouped = prediction.reshape(half, 2, slice_rows, half_width)
    by_owner = jnp.concatenate([grouped[:, 1], grouped[:, 0]], axis=0)
    returned = lax.all_to_all(by_owner, "fsdp", split_axis=0, concat_axis=0, tiled=True)
    real_block = returned[:quarter].reshape(block_rows, half_width).astype(jnp.float32)
    fake_block = returned[quarter:half].reshape(block_rows, half_width).astype(jnp.float32)
    own_share = block_shares(lookup(noise_step, position[None]))[0]
    own_grad = (own_share * (real_block - fake_block)).astype(jnp.bfloat16)
    handed = jnp.where(in_generator, gen_noised[block_rows:], own_grad)
    taken = shifted(handed, "fsdp", half)

    def reverse(operands):
        grad_rows, normed = operands
        backward = lax.dot_general(
            grad_rows, weight_mine, (((1,), (1,)), ((), ())), preferred_element_type=jnp.float32
        )
        scaled = backward.reshape(2, block_rows, model_width) * (1.0 + gen_mod[:, None, :])
        return jnp.sum(scaled.reshape(2 * block_rows, model_width) * normed, axis=0) / block_rows

    def skip_reverse(operands):
        return jnp.zeros((model_width,), jnp.float32)

    grad_rows = jnp.concatenate([own_grad, taken], axis=0)
    gain_term = lax.cond(in_generator, reverse, skip_reverse, (grad_rows, gen_normed))
    gain_grad = lax.psum_scatter(gain_term, ("fsdp", "mp"), scatter_dimension=0, tiled=True)
    noised_out = jnp.where(in_generator, gen_noised[:block_rows], taken)
    return (noised_out, own_grad, gain_grad)


def on_tiles(
    noise_in,
    renoise,
    gen_step,
    noise_step,
    gen_weight,
    real_weight,
    fake_weight,
    gen_embed,
    real_embed,
    fake_embed,
    gen_gain,
    real_gain,
    fake_gain,
):
    g = lax.axis_size("fsdp") // 2
    r, h = noise_in.shape
    d = 2 * h
    w = h // g
    t = g * r
    blocks = gen_step.shape[0]
    f32, bf16 = jnp.float32, jnp.bfloat16
    tail = 16
    span = range(g)

    def place():
        position, c = lax.axis_index("fsdp"), lax.axis_index("mp")
        return lax.div(position, g), lax.rem(position, g), c

    def flat(s_, q_, c_):
        return (s_ * g + q_) * 2 + c_

    every = [(s_, q_, c_) for s_ in (0, 1) for q_ in span for c_ in (0, 1)]

    def in_square(value, k):
        return lax.ppermute(value, "fsdp", [(i, i ^ k) for i in range(2 * g)])

    def across(value):
        return lax.ppermute(value, "fsdp", [(i, i ^ g) for i in range(2 * g)])

    def cores(value):
        return lax.ppermute(value, "mp", [(0, 1), (1, 0)])

    def turned(value):
        return lax.ppermute(value, ("fsdp", "mp"), [(flat(*i), flat(i[2], i[1], i[0])) for i in every])

    whole = pl.BlockSpec(memory_space=pltpu.VMEM)
    scalars = pl.BlockSpec(memory_space=pltpu.SMEM)

    def call(kernel, operands, outs, flops, scratch=(), in_scalars=0):
        moved = sum(o.size * o.dtype.itemsize for o in operands)
        return pl.pallas_call(
            kernel,
            in_specs=[scalars] * in_scalars + [whole] * (len(operands) - in_scalars),
            out_specs=[whole] * len(outs),
            out_shape=[jax.ShapeDtypeStruct(*o) for o in outs],
            scratch_shapes=list(scratch),
            compiler_params=pltpu.CompilerParams(vmem_limit_bytes=40 * 1024 * 1024),
            cost_estimate=pl.CostEstimate(flops=flops, bytes_accessed=moved, transcendentals=0),
        )(*operands)

    def rows_of(columns):
        return jnp.broadcast_to(columns, (t, 128)).T[:8]

    def columns_of(rows):
        return rows.T[:, :1]

    def pack(rows, store):
        high = rows.astype(bf16)
        rest = rows - high.astype(f32)
        middle = rest.astype(bf16)
        low = (rest - middle.astype(f32)).astype(bf16)
        line = lax.broadcasted_iota(jnp.int32, rows.shape, 0)
        mixed = jnp.where(line == 0, high.astype(f32), jnp.where(line == 1, middle.astype(f32), low.astype(f32)))
        mixed = jnp.where(line < 3, mixed, 0.0)
        store(jnp.concatenate([mixed, jnp.zeros_like(mixed)], axis=0).astype(bf16))

    def unpack(block):
        return jnp.sum(block.astype(f32), axis=0, keepdims=True)

    def share(steps, block):
        return (steps[block].astype(f32) + 1.0) / (NT + 1.0)

    def band(j):
        return slice(j * r, (j + 1) * r)

    def lanes(k):
        return pl.ds(pl.multiple_of(k * w, w), w)

    def scales_kernel(features, *refs):
        sources, out, held, sems = refs[:6], refs[6], refs[7:13], refs[13]
        s, _, _ = place()
        mine = pl.ds(pl.multiple_of(s * h, h), h)
        per = h // 128
        copies = [
            pltpu.make_async_copy(source.at[:, mine] if n < 3 else source, here, sems.at[n])
            for n, (source, here) in enumerate(zip(sources, held))
        ]
        for copy in copies:
            copy.start()
        for copy in copies:
            copy.wait()

        def gain(ref):
            return jnp.concatenate([ref[pl.ds(s * per + i, 1), :] for i in range(per)], axis=1)

        for n in range(3):
            steps = slice(0, blocks) if n == 0 else slice(blocks, 2 * blocks)
            mod = 1.0 + jnp.dot(features[steps, :], held[n][...], preferred_element_type=f32)
            if n == 0:
                out[3] = mod
            scale = mod * gain(held[3 + n])
            out[n] = -scale if n == 2 else scale

    gains = [v.reshape(-1, 128) for v in (gen_gain, real_gain, fake_gain)]
    scales = pl.pallas_call(
        scales_kernel,
        in_specs=[whole] + [pl.BlockSpec(memory_space=pltpu.HBM)] * 6,
        out_specs=whole,
        out_shape=jax.ShapeDtypeStruct((4, blocks, h), f32),
        scratch_shapes=[pltpu.VMEM((gen_embed.shape[0], h), bf16)] * 3
        + [pltpu.VMEM(v.shape, f32) for v in gains]
        + [pltpu.SemaphoreType.DMA((6,))],
        compiler_params=pltpu.CompilerParams(vmem_limit_bytes=40 * 1024 * 1024),
        cost_estimate=pl.CostEstimate(flops=6 * blocks * 128 * h, bytes_accessed=6 * 128 * h, transcendentals=0),
    )(
        step_features(jnp.concatenate([gen_step, noise_step]), gen_embed.shape[0]),
        gen_embed,
        real_embed,
        fake_embed,
        *gains,
    )

    depth = gen_weight.shape[0]
    fold = r // g
    shared = g // 2

    part_rows = depth // 2

    def rows_half(n):
        return pl.ds(pl.multiple_of(n * part_rows, 16), part_rows)

    def cut_gen_kernel(weight, *outs):
        _, q, _ = place()
        copy = lax.axis_index("rep")
        for k in span:
            if k < shared:
                outs[k][...] = weight[:, lanes(q ^ k)]
            else:
                outs[k][...] = weight[rows_half(copy), lanes(q ^ k)]

    def join_gen_kernel(*refs):
        copy = lax.axis_index("rep")
        n = g - shared
        for fetched, given, out in zip(refs[:n], refs[n : 2 * n], refs[2 * n :]):
            out[rows_half(copy), :] = fetched[...]
            out[rows_half(1 - copy), :] = given[...]

    def cut_score_kernel(real, fake, *outs):
        _, q, _ = place()
        for k in span:
            if k < shared:
                outs[k][0] = real[:, lanes(q ^ k)]
                outs[k][1] = fake[:, lanes(q ^ k)]
            else:
                for n, weight in enumerate((real, fake)):

                    @pl.when(lax.axis_index("rep") == n)
                    def _():
                        outs[k][...] = weight[:, lanes(q ^ k)]

    def cut_rows_kernel(rows, fresh, *outs):
        _, q, _ = place()
        for k in span:
            outs[k][0:r, :] = rows[...]
            for i in span:
                outs[k][r : r + fold, i * w : (i + 1) * w] = fresh[i * fold : (i + 1) * fold, lanes(q ^ k)]

    def swap_all(tile):
        counts = [v.size // (depth * w) for v in tile]

        def join_kernel(*refs):
            out, at = refs[-1], 0
            for ref, n in zip(refs[:-1], counts):
                for i in range(n):
                    out[at] = ref[i] if n > 1 else ref[...]
                    at += 1

        (joined,) = call(join_kernel, tile, [((sum(counts), depth, w), bf16)], depth * w)
        return cores(joined)

    x_turned, fresh_turned = turned(noise_in), turned(renoise)
    gen_sent = call(cut_gen_kernel, [gen_weight], [((depth, w), bf16)] * shared + [((part_rows, w), bf16)] * (g - shared), depth * h)
    gen_mine = [gen_sent[0]] + [in_square(gen_sent[k], k) for k in range(1, g)]
    fetched = gen_mine[shared:]
    given = [lax.ppermute(v, "rep", [(0, 1), (1, 0)]) for v in fetched]
    gen_mine[shared:] = call(join_gen_kernel, fetched + given, [((depth, w), bf16)] * (g - shared), depth * w)
    x_sent = call(cut_rows_kernel, [x_turned, fresh_turned], [((r + fold, h), bf16)] * g, r * h)
    x = [x_sent[0]] + [in_square(x_sent[k], k) for k in range(1, g)]
    gen_swap, x[1], scales = lax.optimization_barrier((gen_mine, x[1], scales))
    gen_other = [cores(v) for v in gen_swap]
    real_weight, fake_weight, _ = lax.optimization_barrier((real_weight, fake_weight, x_turned))
    score_sent = call(
        cut_score_kernel,
        [real_weight, fake_weight],
        [((2, depth, w), bf16)] * shared + [((depth, w), bf16)] * (g - shared),
        2 * depth * h,
    )
    score_mine = [score_sent[0]] + [in_square(score_sent[k], k) for k in range(1, g)]

    def generate_kernel(steps, *refs):
        xs, scale, own, other = refs[:g], refs[g], refs[g + 1 : 2 * g + 1], refs[2 * g + 1 : 3 * g + 1]
        keep, away, sums, base, lift = refs[3 * g + 1 :]
        s, q, c = place()
        totals = []
        for j in span:
            wide = xs[j][0:r, :].astype(f32)
            totals.append(jnp.sum(wide * wide, axis=1, keepdims=True))
            lift[band(j), :] = (wide * scale[0, pl.ds(c * g + (q ^ j), 1), :]).astype(bf16)
            part = share(steps, c * g + (q ^ j))
            for i in span:
                some = slice(i * fold, (i + 1) * fold)
                base[j * r + i * fold : j * r + (i + 1) * fold, :] = (1.0 - part) * xs[j][some, lanes(q)].astype(
                    f32
                ) + part * xs[j][r : r + fold, i * w : (i + 1) * w].astype(f32)
        here = jnp.zeros((t, w), f32)
        there = jnp.zeros((t, w), f32)
        for k in span:
            part = lift[:, lanes(q ^ k)]
            here = here + jnp.dot(part, own[k][...], preferred_element_type=f32)
            there = there + jnp.dot(part, other[k][...], preferred_element_type=f32)
        stays = s == c
        keep[...] = jnp.where(stays, here, there)
        away[0:t, :] = jnp.where(stays, there, here).astype(bf16)
        rows = rows_of(jnp.concatenate(totals, axis=0))
        sums[...] = rows

        def store(value):
            away[t : t + tail, 0:t] = value

        if w > t:
            away[t : t + tail, t:] = jnp.zeros((tail, w - t), bf16)
        pack(rows, store)

    keep, away, x_sums, base = call(
        generate_kernel,
        [noise_step] + x + [scales] + gen_mine + gen_other,
        [((t, w), f32), ((t + tail, w), bf16), ((8, t), f32), ((t, w), f32)],
        4 * t * h * w,
        [pltpu.VMEM((t, h), bf16)],
        in_scalars=1,
    )

    def inverse_rms(sums, came):
        total = sums[...] + unpack(came[t : t + tail, 0:t])
        return columns_of(lax.rsqrt(total / d + norm_epsilon))

    def blend_kernel(steps, keep, came, sums, base, noised, root):
        _, q, c = place()
        inverse = inverse_rms(sums, came)
        root[...] = jnp.broadcast_to(inverse, (t, 128))
        for j in span:
            stay = 1.0 - share(steps, c * g + (q ^ j))
            made = keep[band(j), :] + came[band(j), :].astype(f32)
            noised[band(j), :] = (base[band(j), :] + (stay * inverse[band(j), :]) * made).astype(bf16)

    came, *fetched = lax.optimization_barrier((across(away), *score_mine[shared:g]))
    score_mine[shared:g] = fetched
    for k in range(shared, g):
        score_mine.append(lax.ppermute(score_mine[k], "rep", [(0, 1), (1, 0)]))
    noised_mine, x_root = call(
        blend_kernel,
        [noise_step, keep, came, x_sums, base],
        [((t, w), bf16), ((t, 128), f32)],
        10 * t * w,
        in_scalars=1,
    )
    noised_last, score_mine[1] = lax.optimization_barrier((noised_mine, score_mine[1]))
    noised = [noised_mine, in_square(noised_last, 1)] + [in_square(noised_mine, k) for k in range(2, g)]

    tiles = len(score_mine)

    def score_product(lifts, tile):
        copy = lax.axis_index("rep")
        total = jnp.zeros((t, w), f32)
        for k in span:
            columns = slice(k * w, (k + 1) * w)
            if k < shared:
                pairs = [(tile[k][0], 0), (tile[k][1], 1)]
            else:
                pairs = [(tile[k][...], copy), (tile[k + g - shared][...], 1 - copy)]
            for part, n in pairs:
                total = total + jnp.dot(lifts[n, :, columns], part, preferred_element_type=f32)
        return total

    def score_kernel(*refs):
        ns, scale, own = refs[:g], refs[g], refs[g + 1 : g + 1 + tiles]
        gap, away, sums, lifts = refs[g + 1 + tiles :]
        _, q, c = place()
        totals = [jnp.zeros((r, 1), f32) for _ in span]
        for k in span:
            columns = slice(k * w, (k + 1) * w)
            for j in span:
                block = pl.ds(c * g + (q ^ j), 1)
                wide = ns[k][band(j ^ k), :].astype(f32)
                totals[j] = totals[j] + jnp.sum(wide * wide, axis=1, keepdims=True)
                for n in (0, 1):
                    lifts[n, band(j), columns] = (wide * scale[1 + n, block, lanes(q ^ k)]).astype(bf16)
        here = score_product(lifts, own)
        gap[...] = here
        away[0:t, :] = here.astype(bf16)
        rows = rows_of(jnp.concatenate(totals, axis=0))
        sums[...] = rows
        if w > t:
            away[t : t + tail, t:] = jnp.zeros((tail, w - t), bf16)

        def store(value):
            away[t : t + tail, 0:t] = value

        pack(rows, store)

    gap_here, away_here, noised_sums, lifts = call(
        score_kernel,
        noised + [scales] + score_mine,
        [((t, w), f32), ((t + tail, w), bf16), ((8, t), f32), ((2, t, h), bf16)],
        4 * t * h * w,
    )
    came_here = across(away_here)
    score_mine, noised_home, away_here = lax.optimization_barrier((score_mine, noised_mine, away_here))
    noised_owned = turned(noised_home)
    score_other = swap_all(score_mine)

    def score_rest_kernel(lifts, other, gap, away):
        there = score_product(
            lifts,
            [(other[2 * k], other[2 * k + 1]) for k in range(shared)]
            + [other[shared + k] for k in range(shared, tiles)],
        )
        gap[...] = there
        away[...] = there.astype(bf16)

    gap_there, away_there = call(
        score_rest_kernel, [lifts, score_other], [((t, w), f32), ((t, w), bf16)], 4 * t * h * w
    )
    came_there = across(away_there)

    def gradient(steps, gap, came, inverse, grad, outs):
        _, q, c = place()
        for j in span:
            part = share(steps, c * g + (q ^ j))
            value = (part * inverse[band(j), :]) * (gap[band(j), :] + came[band(j), :].astype(f32))
            grad[band(j), :] = value.astype(bf16)
            outs[j][0:r, :] = value.astype(bf16)

    def gain_sums(grad, tile, xs, root, scale):
        _, q, c = place()
        sums = []
        for k in span:
            back = lax.dot_general(grad[...], tile[k][...], (((1,), (1,)), ((), ())), preferred_element_type=f32)
            total = jnp.zeros((1, w), f32)
            for j in span:
                normed = xs[j][0:r, lanes(q ^ k)].astype(f32) * root[band(j), :1]
                summed = jnp.sum(back[band(j), :] * normed, axis=0, keepdims=True)
                total = total + summed * scale[3, pl.ds(c * g + (q ^ j), 1), lanes(q ^ k)]
            sums.append(total)
        return sums

    def backward_kernel(steps, gap, came, sums, root, scale, owned, *refs):
        xs, own, outs, (noised_root, partial, grad) = refs[:g], refs[g : 2 * g], refs[2 * g : 3 * g], refs[3 * g :]
        inverse = inverse_rms(sums, came)
        noised_root[...] = jnp.broadcast_to(inverse, (t, 128))
        gradient(steps, gap, came, inverse, grad, outs)
        for k, total in enumerate(gain_sums(grad, own, xs, root, scale)):
            partial[k : k + 1, :] = total
            outs[k][r : 2 * r, :] = owned[band(k), :]

    *sent_here, noised_root, partial = call(
        backward_kernel,
        [noise_step, gap_here, came_here, noised_sums, x_root, scales, noised_owned] + x + gen_mine,
        [((2 * r, w), bf16)] * g + [((t, 128), f32), ((8, w), f32)],
        2 * t * h * w,
        [pltpu.VMEM((t, w), bf16)],
        in_scalars=1,
    )
    arrived_here = [sent_here[0]] + [in_square(sent_here[k], k) for k in range(1, g)]

    def backward_rest_kernel(steps, gap, came, noised_root, partial, root, scale, *refs):
        xs, other, outs, (grad,) = refs[:g], refs[g : 2 * g], refs[2 * g : 3 * g], refs[3 * g :]
        gradient(steps, gap, came, noised_root[:, :1], grad, outs)
        for k, total in enumerate(gain_sums(grad, other, xs, root, scale)):

            def store(value):
                outs[k][r : r + tail, :] = value

            pack(jnp.broadcast_to((total + partial[k : k + 1, :]) / r, (8, w)), store)

    sent_there = call(
        backward_rest_kernel,
        [noise_step, gap_there, came_there, noised_root, partial, x_root, scales] + x + gen_other,
        [((r + tail, w), bf16)] * g,
        2 * t * h * w,
        [pltpu.VMEM((t, w), bf16)],
        in_scalars=1,
    )
    arrived_there = [sent_there[0]] + [in_square(sent_there[k], k) for k in range(1, g)]

    def gather_kernel(*refs):
        a, b, (here, there, gains, noised) = refs[:g], refs[g : 2 * g], refs[2 * g :]
        _, q, _ = place()
        total = jnp.zeros((1, w), f32)
        for k in span:
            here[:, lanes(q ^ k)] = a[k][0:r, :]
            noised[:, lanes(q ^ k)] = a[k][r : 2 * r, :]
            there[0:r, lanes(q ^ k)] = b[k][0:r, :]
            total = total + unpack(b[k][r : r + tail, :])
        gains[...] = total

        def store(value):
            there[r : r + tail, :w] = value

        pack(jnp.broadcast_to(total, (8, w)), store)
        there[r : r + tail, w:] = jnp.zeros((tail, h - w), bf16)

    here, there, gains, noised_out = call(
        gather_kernel,
        arrived_here + arrived_there,
        [((r, h), bf16), ((r + tail, h), bf16), ((1, w), f32), ((r, h), bf16)],
        t * h,
    )
    other_core = cores(there)

    def finish_kernel(here, gains, came, grad, gain):
        s, _, c = place()
        grad[...] = jnp.where(s == c, here[...], came[0:r, :])
        both = gains[...] + unpack(came[r : r + tail, :w])
        gain[...] = jnp.where(c == 0, both[:, : w // 2], both[:, w // 2 :])

    latent_grad, gain = call(
        finish_kernel, [here, gains, other_core], [((r, h), bf16), ((1, w // 2), f32)], r * h
    )
    return (noised_out, latent_grad, gain[0])


def solution(mesh):
    positions = mesh.shape["fsdp"]
    on_device = on_tiles if (positions, mesh.shape["rep"], mesh.shape["mp"]) == (8, 2, 2) else on_groups
    return jax.shard_map(
        on_device,
        mesh=mesh,
        in_specs=(
            P(("rep", "fsdp"), "mp"),
            P(("rep", "fsdp"), "mp"),
            P("rep"),
            P("rep"),
            P("fsdp", "mp"),
            P("fsdp", "mp"),
            P("fsdp", "mp"),
            P(),
            P(),
            P(),
            P(),
            P(),
            P(),
        ),
        out_specs=(P(("rep", "fsdp"), "mp"), P(("rep", "fsdp"), "mp"), P(("rep", "fsdp", "mp"))),
        check_vma=False,
    )
```

```python
import math

import jax
import jax.numpy as jnp
from jax import lax
from jax.experimental import pallas as pl
from jax.experimental.pallas import tpu as pltpu
from jax.sharding import PartitionSpec as P

NT = 1000


norm_epsilon = 1e-06


def from_behind(value, axis, by):
    size = lax.axis_size(axis)
    pairs = [(i, i + by) for i in range(size) if 0 <= i + by < size]
    return lax.ppermute(value, axis, pairs)


def shifted(value, axis, by):
    size = lax.axis_size(axis)
    return lax.ppermute(value, axis, [(i, (i + by) % size) for i in range(size)])


def step_features(step_ids, feature_width):
    half_width = feature_width // 2
    frequency = jnp.exp(-math.log(10000.0) * jnp.arange(half_width, dtype=jnp.float32) / half_width)
    angles = step_ids.astype(jnp.float32)[:, None] * frequency[None, :]
    return jnp.concatenate([jnp.cos(angles), jnp.sin(angles)], axis=1).astype(jnp.bfloat16)


def lookup(step_table, block_ids):
    matches = block_ids[:, None] == jnp.arange(step_table.shape[0], dtype=jnp.int32)[None, :]
    return jnp.sum(jnp.where(matches, step_table[None, :], 0), axis=1)


def block_shares(step_ids):
    return ((step_ids.astype(jnp.float32) + 1.0) / (NT + 1.0))[:, None, None]


def modulate(full_rows, gain_vec, modulation):
    blocks = modulation.shape[0]
    values = full_rows.astype(jnp.float32)
    normed = values * lax.rsqrt(jnp.mean(values * values, axis=1, keepdims=True) + norm_epsilon)
    lifted = normed.reshape(blocks, -1, values.shape[1]) * gain_vec * (1.0 + modulation[:, None, :])
    return (normed, lifted.reshape(values.shape).astype(jnp.bfloat16))


def on_groups(
    noise_in,
    renoise,
    gen_step,
    noise_step,
    gen_weight,
    real_weight,
    fake_weight,
    gen_embed,
    real_embed,
    fake_embed,
    gen_gain,
    real_gain,
    fake_gain,
):
    devices = lax.axis_size("fsdp")
    quarter = devices // 4
    half = 2 * quarter
    position = lax.axis_index("fsdp")
    block_rows = noise_in.shape[0]
    half_width = noise_in.shape[1]
    model_width = gen_gain.shape[0]
    feature_width = gen_embed.shape[0]
    slice_rows = 4 * block_rows // devices
    group_role = (position >= quarter).astype(jnp.int32) + (position >= half).astype(jnp.int32)
    in_generator = group_role == 2
    slot_ids = jnp.arange(devices, dtype=jnp.int32)
    slot_role = (
        (slot_ids >= quarter).astype(jnp.int32) + (slot_ids >= half).astype(jnp.int32)
    ).reshape(devices, 1, 1)
    outgoing = jnp.where(
        slot_role == 2,
        gen_weight[None],
        jnp.where(slot_role == 0, real_weight[None], fake_weight[None]),
    )
    received = lax.all_to_all(outgoing, "fsdp", split_axis=0, concat_axis=0, tiled=True)
    weight_mine = received.reshape(model_width, half_width)
    embed_mine = jnp.where(
        group_role == 2, gen_embed, jnp.where(group_role == 0, real_embed, fake_embed)
    )
    gain_mine = jnp.where(
        group_role == 2, gen_gain, jnp.where(group_role == 0, real_gain, fake_gain)
    )
    partner_noise, partner_renoise = from_behind((noise_in, renoise), "fsdp", half)
    gen_ids = jnp.stack([position, (position + half) % devices])
    gen_mod = jnp.dot(
        step_features(lookup(gen_step, gen_ids), feature_width),
        embed_mine,
        preferred_element_type=jnp.float32,
    )
    gen_shares = block_shares(lookup(noise_step, gen_ids))
    gen_rows = jnp.concatenate([noise_in, partner_noise], axis=0)
    gen_noise = jnp.concatenate([renoise, partner_renoise], axis=0)
    gen_full = lax.all_gather(gen_rows, "mp", axis=1, tiled=True)

    def generate(operands):
        full_rows, own_rows, fresh_noise = operands
        normed, lifted = modulate(full_rows, gain_mine, gen_mod)
        latents = own_rows.astype(jnp.float32) + jnp.dot(
            lifted, weight_mine, preferred_element_type=jnp.float32
        )
        blended = (1.0 - gen_shares) * latents.reshape(
            2, block_rows, half_width
        ) + gen_shares * fresh_noise.astype(jnp.float32).reshape(2, block_rows, half_width)
        return (blended.reshape(2 * block_rows, half_width).astype(jnp.bfloat16), normed)

    def skip_generate(operands):
        return (
            jnp.zeros((2 * block_rows, half_width), jnp.bfloat16),
            jnp.zeros((2 * block_rows, model_width), jnp.float32),
        )

    gen_noised, gen_normed = lax.cond(
        in_generator, generate, skip_generate, (gen_full, gen_rows, gen_noise)
    )
    width_now = gen_noised.shape[1]
    pieces = (
        gen_noised.reshape(2, quarter, slice_rows, width_now)
        .transpose(1, 0, 2, 3)
        .reshape(quarter, 2 * slice_rows, width_now)
    )
    send_rows = jnp.concatenate(
        [pieces, pieces, jnp.zeros((half, 2 * slice_rows, width_now), jnp.bfloat16)], axis=0
    )
    arrived = lax.all_to_all(send_rows, "fsdp", split_axis=0, concat_axis=0, tiled=True)
    score_rows = arrived[half:].reshape(2 * half * slice_rows, width_now)
    gen_slots = jnp.arange(half, dtype=jnp.int32)
    score_ids = jnp.stack([gen_slots + half, gen_slots], axis=1).reshape(2 * half)
    score_mod = jnp.dot(
        step_features(lookup(noise_step, score_ids), feature_width),
        embed_mine,
        preferred_element_type=jnp.float32,
    )
    score_full = lax.all_gather(score_rows, "mp", axis=1, tiled=True)

    def assess(full_rows):
        normed, lifted = modulate(full_rows, gain_mine, score_mod)
        return jnp.dot(lifted, weight_mine, preferred_element_type=jnp.float32).astype(jnp.bfloat16)

    def skip_assess(full_rows):
        return jnp.zeros((2 * half * slice_rows, half_width), jnp.bfloat16)

    prediction = lax.cond(in_generator, skip_assess, assess, score_full)
    grouped = prediction.reshape(half, 2, slice_rows, half_width)
    by_owner = jnp.concatenate([grouped[:, 1], grouped[:, 0]], axis=0)
    returned = lax.all_to_all(by_owner, "fsdp", split_axis=0, concat_axis=0, tiled=True)
    real_block = returned[:quarter].reshape(block_rows, half_width).astype(jnp.float32)
    fake_block = returned[quarter:half].reshape(block_rows, half_width).astype(jnp.float32)
    own_share = block_shares(lookup(noise_step, position[None]))[0]
    own_grad = (own_share * (real_block - fake_block)).astype(jnp.bfloat16)
    handed = jnp.where(in_generator, gen_noised[block_rows:], own_grad)
    taken = shifted(handed, "fsdp", half)

    def reverse(operands):
        grad_rows, normed = operands
        backward = lax.dot_general(
            grad_rows, weight_mine, (((1,), (1,)), ((), ())), preferred_element_type=jnp.float32
        )
        scaled = backward.reshape(2, block_rows, model_width) * (1.0 + gen_mod[:, None, :])
        return jnp.sum(scaled.reshape(2 * block_rows, model_width) * normed, axis=0) / block_rows

    def skip_reverse(operands):
        return jnp.zeros((model_width,), jnp.float32)

    grad_rows = jnp.concatenate([own_grad, taken], axis=0)
    gain_term = lax.cond(in_generator, reverse, skip_reverse, (grad_rows, gen_normed))
    gain_grad = lax.psum_scatter(gain_term, ("fsdp", "mp"), scatter_dimension=0, tiled=True)
    noised_out = jnp.where(in_generator, gen_noised[:block_rows], taken)
    return (noised_out, own_grad, gain_grad)


def on_tiles(
    noise_in,
    renoise,
    gen_step,
    noise_step,
    gen_weight,
    real_weight,
    fake_weight,
    gen_embed,
    real_embed,
    fake_embed,
    gen_gain,
    real_gain,
    fake_gain,
):
    g = lax.axis_size("fsdp") // 2
    r, h = noise_in.shape
    d = 2 * h
    w = h // g
    t = g * r
    blocks = gen_step.shape[0]
    f32, bf16 = jnp.float32, jnp.bfloat16
    tail = 16
    span = range(g)

    def place():
        position, c = lax.axis_index("fsdp"), lax.axis_index("mp")
        return lax.div(position, g), lax.rem(position, g), c

    def flat(s_, q_, c_):
        return (s_ * g + q_) * 2 + c_

    every = [(s_, q_, c_) for s_ in (0, 1) for q_ in span for c_ in (0, 1)]

    def in_square(value, k):
        return lax.ppermute(value, "fsdp", [(i, i ^ k) for i in range(2 * g)])

    def across(value):
        return lax.ppermute(value, "fsdp", [(i, i ^ g) for i in range(2 * g)])

    def cores(value):
        return lax.ppermute(value, "mp", [(0, 1), (1, 0)])

    def turned(value):
        return lax.ppermute(value, ("fsdp", "mp"), [(flat(*i), flat(i[2], i[1], i[0])) for i in every])

    whole = pl.BlockSpec(memory_space=pltpu.VMEM)
    scalars = pl.BlockSpec(memory_space=pltpu.SMEM)

    def call(kernel, operands, outs, flops, scratch=(), in_scalars=0):
        moved = sum(o.size * o.dtype.itemsize for o in operands)
        return pl.pallas_call(
            kernel,
            in_specs=[scalars] * in_scalars + [whole] * (len(operands) - in_scalars),
            out_specs=[whole] * len(outs),
            out_shape=[jax.ShapeDtypeStruct(*o) for o in outs],
            scratch_shapes=list(scratch),
            compiler_params=pltpu.CompilerParams(vmem_limit_bytes=40 * 1024 * 1024),
            cost_estimate=pl.CostEstimate(flops=flops, bytes_accessed=moved, transcendentals=0),
        )(*operands)

    def rows_of(columns):
        return jnp.broadcast_to(columns, (t, 128)).T[:8]

    def columns_of(rows):
        return rows.T[:, :1]

    def pack(rows, store):
        high = rows.astype(bf16)
        rest = rows - high.astype(f32)
        middle = rest.astype(bf16)
        low = (rest - middle.astype(f32)).astype(bf16)
        line = lax.broadcasted_iota(jnp.int32, rows.shape, 0)
        mixed = jnp.where(line == 0, high.astype(f32), jnp.where(line == 1, middle.astype(f32), low.astype(f32)))
        mixed = jnp.where(line < 3, mixed, 0.0)
        store(jnp.concatenate([mixed, jnp.zeros_like(mixed)], axis=0).astype(bf16))

    def unpack(block):
        return jnp.sum(block.astype(f32), axis=0, keepdims=True)

    def share(steps, block):
        return (steps[block].astype(f32) + 1.0) / (NT + 1.0)

    def band(j):
        return slice(j * r, (j + 1) * r)

    def lanes(k):
        return pl.ds(pl.multiple_of(k * w, w), w)

    def scales_kernel(features, *refs):
        sources, out, held, sems = refs[:6], refs[6], refs[7:13], refs[13]
        s, _, _ = place()
        mine = pl.ds(pl.multiple_of(s * h, h), h)
        per = h // 128
        copies = [
            pltpu.make_async_copy(source.at[:, mine] if n < 3 else source, here, sems.at[n])
            for n, (source, here) in enumerate(zip(sources, held))
        ]
        for copy in copies:
            copy.start()
        for copy in copies:
            copy.wait()

        def gain(ref):
            return jnp.concatenate([ref[pl.ds(s * per + i, 1), :] for i in range(per)], axis=1)

        for n in range(3):
            steps = slice(0, blocks) if n == 0 else slice(blocks, 2 * blocks)
            mod = 1.0 + jnp.dot(features[steps, :], held[n][...], preferred_element_type=f32)
            if n == 0:
                out[3] = mod
            scale = mod * gain(held[3 + n])
            out[n] = -scale if n == 2 else scale

    gains = [v.reshape(-1, 128) for v in (gen_gain, real_gain, fake_gain)]
    scales = pl.pallas_call(
        scales_kernel,
        in_specs=[whole] + [pl.BlockSpec(memory_space=pltpu.HBM)] * 6,
        out_specs=whole,
        out_shape=jax.ShapeDtypeStruct((4, blocks, h), f32),
        scratch_shapes=[pltpu.VMEM((gen_embed.shape[0], h), bf16)] * 3
        + [pltpu.VMEM(v.shape, f32) for v in gains]
        + [pltpu.SemaphoreType.DMA((6,))],
        compiler_params=pltpu.CompilerParams(vmem_limit_bytes=40 * 1024 * 1024),
        cost_estimate=pl.CostEstimate(flops=6 * blocks * 128 * h, bytes_accessed=6 * 128 * h, transcendentals=0),
    )(
        step_features(jnp.concatenate([gen_step, noise_step]), gen_embed.shape[0]),
        gen_embed,
        real_embed,
        fake_embed,
        *gains,
    )

    depth = gen_weight.shape[0]
    fold = r // g
    shared = g // 2

    part_rows = depth // 2

    def rows_half(n):
        return pl.ds(pl.multiple_of(n * part_rows, 16), part_rows)

    def cut_gen_kernel(weight, *outs):
        _, q, _ = place()
        copy = lax.axis_index("rep")
        for k in span:
            if k < shared:
                outs[k][...] = weight[:, lanes(q ^ k)]
            else:
                outs[k][...] = weight[rows_half(copy), lanes(q ^ k)]

    def join_gen_kernel(*refs):
        copy = lax.axis_index("rep")
        n = g - shared
        for fetched, given, out in zip(refs[:n], refs[n : 2 * n], refs[2 * n :]):
            out[rows_half(copy), :] = fetched[...]
            out[rows_half(1 - copy), :] = given[...]

    def cut_score_kernel(real, fake, *outs):
        _, q, _ = place()
        for k in span:
            if k < shared:
                outs[k][0] = real[:, lanes(q ^ k)]
                outs[k][1] = fake[:, lanes(q ^ k)]
            else:
                for n, weight in enumerate((real, fake)):

                    @pl.when(lax.axis_index("rep") == n)
                    def _():
                        outs[k][...] = weight[:, lanes(q ^ k)]

    def cut_rows_kernel(rows, fresh, *outs):
        _, q, _ = place()
        for k in span:
            outs[k][0:r, :] = rows[...]
            for i in span:
                outs[k][r : r + fold, i * w : (i + 1) * w] = fresh[i * fold : (i + 1) * fold, lanes(q ^ k)]

    def swap_all(tile):
        counts = [v.size // (depth * w) for v in tile]

        def join_kernel(*refs):
            out, at = refs[-1], 0
            for ref, n in zip(refs[:-1], counts):
                for i in range(n):
                    out[at] = ref[i] if n > 1 else ref[...]
                    at += 1

        (joined,) = call(join_kernel, tile, [((sum(counts), depth, w), bf16)], depth * w)
        return cores(joined)

    x_turned, fresh_turned = turned(noise_in), turned(renoise)
    gen_sent = call(cut_gen_kernel, [gen_weight], [((depth, w), bf16)] * shared + [((part_rows, w), bf16)] * (g - shared), depth * h)
    gen_mine = [gen_sent[0]] + [in_square(gen_sent[k], k) for k in range(1, g)]
    x_sent = call(cut_rows_kernel, [x_turned, fresh_turned], [((r + fold, h), bf16)] * g, r * h)
    x_sent = list(x_sent)
    *fetched, x_sent[0] = lax.optimization_barrier((*gen_mine[shared:], x_sent[0]))
    given = [lax.ppermute(v, "rep", [(0, 1), (1, 0)]) for v in fetched]
    gen_mine[shared:] = call(join_gen_kernel, fetched + given, [((depth, w), bf16)] * (g - shared), depth * w)
    x = [x_sent[0]] + [in_square(x_sent[k], k) for k in range(1, g)]
    gen_swap, x[1], scales = lax.optimization_barrier((gen_mine, x[1], scales))
    gen_other = [cores(v) for v in gen_swap]
    real_weight, fake_weight, _ = lax.optimization_barrier((real_weight, fake_weight, x_turned))
    score_sent = call(
        cut_score_kernel,
        [real_weight, fake_weight],
        [((2, depth, w), bf16)] * shared + [((depth, w), bf16)] * (g - shared),
        2 * depth * h,
    )
    score_mine = [score_sent[0]] + [in_square(score_sent[k], k) for k in range(1, g)]

    def generate_kernel(steps, *refs):
        xs, scale, own, other = refs[:g], refs[g], refs[g + 1 : 2 * g + 1], refs[2 * g + 1 : 3 * g + 1]
        keep, away, sums, base, lift = refs[3 * g + 1 :]
        s, q, c = place()
        totals = []
        for j in span:
            wide = xs[j][0:r, :].astype(f32)
            totals.append(jnp.sum(wide * wide, axis=1, keepdims=True))
            lift[band(j), :] = (wide * scale[0, pl.ds(c * g + (q ^ j), 1), :]).astype(bf16)
            part = share(steps, c * g + (q ^ j))
            for i in span:
                some = slice(i * fold, (i + 1) * fold)
                base[j * r + i * fold : j * r + (i + 1) * fold, :] = (1.0 - part) * xs[j][some, lanes(q)].astype(
                    f32
                ) + part * xs[j][r : r + fold, i * w : (i + 1) * w].astype(f32)
        here = jnp.zeros((t, w), f32)
        there = jnp.zeros((t, w), f32)
        for k in span:
            part = lift[:, lanes(q ^ k)]
            here = here + jnp.dot(part, own[k][...], preferred_element_type=f32)
            there = there + jnp.dot(part, other[k][...], preferred_element_type=f32)
        stays = s == c
        keep[...] = jnp.where(stays, here, there)
        away[0:t, :] = jnp.where(stays, there, here).astype(bf16)
        rows = rows_of(jnp.concatenate(totals, axis=0))
        sums[...] = rows

        def store(value):
            away[t : t + tail, 0:t] = value

        if w > t:
            away[t : t + tail, t:] = jnp.zeros((tail, w - t), bf16)
        pack(rows, store)

    keep, away, x_sums, base = call(
        generate_kernel,
        [noise_step] + x + [scales] + gen_mine + gen_other,
        [((t, w), f32), ((t + tail, w), bf16), ((8, t), f32), ((t, w), f32)],
        4 * t * h * w,
        [pltpu.VMEM((t, h), bf16)],
        in_scalars=1,
    )

    def inverse_rms(sums, came):
        total = sums[...] + unpack(came[t : t + tail, 0:t])
        return columns_of(lax.rsqrt(total / d + norm_epsilon))

    def blend_kernel(steps, keep, came, sums, base, noised, root):
        _, q, c = place()
        inverse = inverse_rms(sums, came)
        root[...] = jnp.broadcast_to(inverse, (t, 128))
        for j in span:
            stay = 1.0 - share(steps, c * g + (q ^ j))
            made = keep[band(j), :] + came[band(j), :].astype(f32)
            noised[band(j), :] = (base[band(j), :] + (stay * inverse[band(j), :]) * made).astype(bf16)

    came, *fetched = lax.optimization_barrier((across(away), *score_mine[shared:g]))
    score_mine[shared:g] = fetched
    for k in range(shared, g):
        score_mine.append(lax.ppermute(score_mine[k], "rep", [(0, 1), (1, 0)]))
    noised_mine, x_root = call(
        blend_kernel,
        [noise_step, keep, came, x_sums, base],
        [((t, w), bf16), ((t, 128), f32)],
        10 * t * w,
        in_scalars=1,
    )
    noised_last, score_mine[1] = lax.optimization_barrier((noised_mine, score_mine[1]))
    noised = [noised_mine, in_square(noised_last, 1)] + [in_square(noised_mine, k) for k in range(2, g)]

    tiles = len(score_mine)

    def score_product(lifts, tile):
        copy = lax.axis_index("rep")
        total = jnp.zeros((t, w), f32)
        for k in span:
            columns = slice(k * w, (k + 1) * w)
            if k < shared:
                pairs = [(tile[k][0], 0), (tile[k][1], 1)]
            else:
                pairs = [(tile[k][...], copy), (tile[k + g - shared][...], 1 - copy)]
            for part, n in pairs:
                total = total + jnp.dot(lifts[n, :, columns], part, preferred_element_type=f32)
        return total

    def score_kernel(*refs):
        ns, scale, own = refs[:g], refs[g], refs[g + 1 : g + 1 + tiles]
        gap, away, sums, lifts = refs[g + 1 + tiles :]
        _, q, c = place()
        totals = [jnp.zeros((r, 1), f32) for _ in span]
        for k in span:
            columns = slice(k * w, (k + 1) * w)
            for j in span:
                block = pl.ds(c * g + (q ^ j), 1)
                wide = ns[k][band(j ^ k), :].astype(f32)
                totals[j] = totals[j] + jnp.sum(wide * wide, axis=1, keepdims=True)
                for n in (0, 1):
                    lifts[n, band(j), columns] = (wide * scale[1 + n, block, lanes(q ^ k)]).astype(bf16)
        here = score_product(lifts, own)
        gap[...] = here
        away[0:t, :] = here.astype(bf16)
        rows = rows_of(jnp.concatenate(totals, axis=0))
        sums[...] = rows
        if w > t:
            away[t : t + tail, t:] = jnp.zeros((tail, w - t), bf16)

        def store(value):
            away[t : t + tail, 0:t] = value

        pack(rows, store)

    noised_home, noised[3] = lax.optimization_barrier((noised_mine, noised[3]))
    gap_here, away_here, noised_sums, lifts = call(
        score_kernel,
        noised + [scales] + score_mine,
        [((t, w), f32), ((t + tail, w), bf16), ((8, t), f32), ((2, t, h), bf16)],
        4 * t * h * w,
    )
    came_here = across(away_here)
    noised_owned, score_mine, gap_here = lax.optimization_barrier((turned(noised_home), score_mine, gap_here))
    score_mine, _ = lax.optimization_barrier((score_mine, cores(noised_sums)))
    score_other = swap_all(score_mine)

    def score_rest_kernel(lifts, other, gap, away):
        there = score_product(
            lifts,
            [(other[2 * k], other[2 * k + 1]) for k in range(shared)]
            + [other[shared + k] for k in range(shared, tiles)],
        )
        gap[...] = there
        away[...] = there.astype(bf16)

    gap_there, away_there = call(
        score_rest_kernel, [lifts, score_other], [((t, w), f32), ((t, w), bf16)], 4 * t * h * w
    )
    came_there = across(away_there)

    def gradient(steps, gap, came, inverse, grad, outs):
        _, q, c = place()
        for j in span:
            part = share(steps, c * g + (q ^ j))
            value = (part * inverse[band(j), :]) * (gap[band(j), :] + came[band(j), :].astype(f32))
            grad[band(j), :] = value.astype(bf16)
            outs[j][0:r, :] = value.astype(bf16)

    def gain_sums(grad, tile, xs, root, scale):
        _, q, c = place()
        sums = []
        for k in span:
            back = lax.dot_general(grad[...], tile[k][...], (((1,), (1,)), ((), ())), preferred_element_type=f32)
            total = jnp.zeros((1, w), f32)
            for j in span:
                normed = xs[j][0:r, lanes(q ^ k)].astype(f32) * root[band(j), :1]
                summed = jnp.sum(back[band(j), :] * normed, axis=0, keepdims=True)
                total = total + summed * scale[3, pl.ds(c * g + (q ^ j), 1), lanes(q ^ k)]
            sums.append(total)
        return sums

    def backward_kernel(steps, gap, came, sums, root, scale, owned, *refs):
        xs, own, outs, (noised_root, partial, grad) = refs[:g], refs[g : 2 * g], refs[2 * g : 3 * g], refs[3 * g :]
        inverse = inverse_rms(sums, came)
        noised_root[...] = jnp.broadcast_to(inverse, (t, 128))
        gradient(steps, gap, came, inverse, grad, outs)
        for k, total in enumerate(gain_sums(grad, own, xs, root, scale)):
            partial[k : k + 1, :] = total
            outs[k][r : 2 * r, :] = owned[band(k), :]

    *sent_here, noised_root, partial = call(
        backward_kernel,
        [noise_step, gap_here, came_here, noised_sums, x_root, scales, noised_owned] + x + gen_mine,
        [((2 * r, w), bf16)] * g + [((t, 128), f32), ((8, w), f32)],
        2 * t * h * w,
        [pltpu.VMEM((t, w), bf16)],
        in_scalars=1,
    )
    arrived_here = [sent_here[0]] + [in_square(sent_here[k], k) for k in range(1, g)]

    def backward_rest_kernel(steps, gap, came, noised_root, partial, root, scale, *refs):
        xs, other, outs, (grad,) = refs[:g], refs[g : 2 * g], refs[2 * g : 3 * g], refs[3 * g :]
        gradient(steps, gap, came, noised_root[:, :1], grad, outs)
        for k, total in enumerate(gain_sums(grad, other, xs, root, scale)):

            def store(value):
                outs[k][r : r + tail, :] = value

            pack(jnp.broadcast_to((total + partial[k : k + 1, :]) / r, (8, w)), store)

    sent_there = call(
        backward_rest_kernel,
        [noise_step, gap_there, came_there, noised_root, partial, x_root, scales] + x + gen_other,
        [((r + tail, w), bf16)] * g,
        2 * t * h * w,
        [pltpu.VMEM((t, w), bf16)],
        in_scalars=1,
    )
    arrived_there = [sent_there[0]] + [in_square(sent_there[k], k) for k in range(1, g)]

    def gather_kernel(*refs):
        a, b, (here, there, gains, noised) = refs[:g], refs[g : 2 * g], refs[2 * g :]
        _, q, _ = place()
        total = jnp.zeros((1, w), f32)
        for k in span:
            here[:, lanes(q ^ k)] = a[k][0:r, :]
            noised[:, lanes(q ^ k)] = a[k][r : 2 * r, :]
            there[0:r, lanes(q ^ k)] = b[k][0:r, :]
            total = total + unpack(b[k][r : r + tail, :])
        gains[...] = total

        def store(value):
            there[r : r + tail, :w] = value

        pack(jnp.broadcast_to(total, (8, w)), store)
        there[r : r + tail, w:] = jnp.zeros((tail, h - w), bf16)

    here, there, gains, noised_out = call(
        gather_kernel,
        arrived_here + arrived_there,
        [((r, h), bf16), ((r + tail, h), bf16), ((1, w), f32), ((r, h), bf16)],
        t * h,
    )
    other_core = cores(there)

    def finish_kernel(here, gains, came, grad, gain):
        s, _, c = place()
        grad[...] = jnp.where(s == c, here[...], came[0:r, :])
        both = gains[...] + unpack(came[r : r + tail, :w])
        gain[...] = jnp.where(c == 0, both[:, : w // 2], both[:, w // 2 :])

    latent_grad, gain = call(
        finish_kernel, [here, gains, other_core], [((r, h), bf16), ((1, w // 2), f32)], r * h
    )
    return (noised_out, latent_grad, gain[0])


def solution(mesh):
    positions = mesh.shape["fsdp"]
    on_device = on_tiles if (positions, mesh.shape["rep"], mesh.shape["mp"]) == (8, 2, 2) else on_groups
    return jax.shard_map(
        on_device,
        mesh=mesh,
        in_specs=(
            P(("rep", "fsdp"), "mp"),
            P(("rep", "fsdp"), "mp"),
            P("rep"),
            P("rep"),
            P("fsdp", "mp"),
            P("fsdp", "mp"),
            P("fsdp", "mp"),
            P(),
            P(),
            P(),
            P(),
            P(),
            P(),
        ),
        out_specs=(P(("rep", "fsdp"), "mp"), P(("rep", "fsdp"), "mp"), P(("rep", "fsdp", "mp"))),
        check_vma=False,
    )
```

```python
import math

import jax
import jax.numpy as jnp
from jax import lax
from jax.experimental import pallas as pl
from jax.experimental.pallas import tpu as pltpu
from jax.sharding import PartitionSpec as P

NT = 1000


norm_epsilon = 1e-06


def from_behind(value, axis, by):
    size = lax.axis_size(axis)
    pairs = [(i, i + by) for i in range(size) if 0 <= i + by < size]
    return lax.ppermute(value, axis, pairs)


def shifted(value, axis, by):
    size = lax.axis_size(axis)
    return lax.ppermute(value, axis, [(i, (i + by) % size) for i in range(size)])


def step_features(step_ids, feature_width):
    half_width = feature_width // 2
    frequency = jnp.exp(-math.log(10000.0) * jnp.arange(half_width, dtype=jnp.float32) / half_width)
    angles = step_ids.astype(jnp.float32)[:, None] * frequency[None, :]
    return jnp.concatenate([jnp.cos(angles), jnp.sin(angles)], axis=1).astype(jnp.bfloat16)


def lookup(step_table, block_ids):
    matches = block_ids[:, None] == jnp.arange(step_table.shape[0], dtype=jnp.int32)[None, :]
    return jnp.sum(jnp.where(matches, step_table[None, :], 0), axis=1)


def block_shares(step_ids):
    return ((step_ids.astype(jnp.float32) + 1.0) / (NT + 1.0))[:, None, None]


def modulate(full_rows, gain_vec, modulation):
    blocks = modulation.shape[0]
    values = full_rows.astype(jnp.float32)
    normed = values * lax.rsqrt(jnp.mean(values * values, axis=1, keepdims=True) + norm_epsilon)
    lifted = normed.reshape(blocks, -1, values.shape[1]) * gain_vec * (1.0 + modulation[:, None, :])
    return (normed, lifted.reshape(values.shape).astype(jnp.bfloat16))


def on_groups(
    noise_in,
    renoise,
    gen_step,
    noise_step,
    gen_weight,
    real_weight,
    fake_weight,
    gen_embed,
    real_embed,
    fake_embed,
    gen_gain,
    real_gain,
    fake_gain,
):
    devices = lax.axis_size("fsdp")
    quarter = devices // 4
    half = 2 * quarter
    position = lax.axis_index("fsdp")
    block_rows = noise_in.shape[0]
    half_width = noise_in.shape[1]
    model_width = gen_gain.shape[0]
    feature_width = gen_embed.shape[0]
    slice_rows = 4 * block_rows // devices
    group_role = (position >= quarter).astype(jnp.int32) + (position >= half).astype(jnp.int32)
    in_generator = group_role == 2
    slot_ids = jnp.arange(devices, dtype=jnp.int32)
    slot_role = (
        (slot_ids >= quarter).astype(jnp.int32) + (slot_ids >= half).astype(jnp.int32)
    ).reshape(devices, 1, 1)
    outgoing = jnp.where(
        slot_role == 2,
        gen_weight[None],
        jnp.where(slot_role == 0, real_weight[None], fake_weight[None]),
    )
    received = lax.all_to_all(outgoing, "fsdp", split_axis=0, concat_axis=0, tiled=True)
    weight_mine = received.reshape(model_width, half_width)
    embed_mine = jnp.where(
        group_role == 2, gen_embed, jnp.where(group_role == 0, real_embed, fake_embed)
    )
    gain_mine = jnp.where(
        group_role == 2, gen_gain, jnp.where(group_role == 0, real_gain, fake_gain)
    )
    partner_noise, partner_renoise = from_behind((noise_in, renoise), "fsdp", half)
    gen_ids = jnp.stack([position, (position + half) % devices])
    gen_mod = jnp.dot(
        step_features(lookup(gen_step, gen_ids), feature_width),
        embed_mine,
        preferred_element_type=jnp.float32,
    )
    gen_shares = block_shares(lookup(noise_step, gen_ids))
    gen_rows = jnp.concatenate([noise_in, partner_noise], axis=0)
    gen_noise = jnp.concatenate([renoise, partner_renoise], axis=0)
    gen_full = lax.all_gather(gen_rows, "mp", axis=1, tiled=True)

    def generate(operands):
        full_rows, own_rows, fresh_noise = operands
        normed, lifted = modulate(full_rows, gain_mine, gen_mod)
        latents = own_rows.astype(jnp.float32) + jnp.dot(
            lifted, weight_mine, preferred_element_type=jnp.float32
        )
        blended = (1.0 - gen_shares) * latents.reshape(
            2, block_rows, half_width
        ) + gen_shares * fresh_noise.astype(jnp.float32).reshape(2, block_rows, half_width)
        return (blended.reshape(2 * block_rows, half_width).astype(jnp.bfloat16), normed)

    def skip_generate(operands):
        return (
            jnp.zeros((2 * block_rows, half_width), jnp.bfloat16),
            jnp.zeros((2 * block_rows, model_width), jnp.float32),
        )

    gen_noised, gen_normed = lax.cond(
        in_generator, generate, skip_generate, (gen_full, gen_rows, gen_noise)
    )
    width_now = gen_noised.shape[1]
    pieces = (
        gen_noised.reshape(2, quarter, slice_rows, width_now)
        .transpose(1, 0, 2, 3)
        .reshape(quarter, 2 * slice_rows, width_now)
    )
    send_rows = jnp.concatenate(
        [pieces, pieces, jnp.zeros((half, 2 * slice_rows, width_now), jnp.bfloat16)], axis=0
    )
    arrived = lax.all_to_all(send_rows, "fsdp", split_axis=0, concat_axis=0, tiled=True)
    score_rows = arrived[half:].reshape(2 * half * slice_rows, width_now)
    gen_slots = jnp.arange(half, dtype=jnp.int32)
    score_ids = jnp.stack([gen_slots + half, gen_slots], axis=1).reshape(2 * half)
    score_mod = jnp.dot(
        step_features(lookup(noise_step, score_ids), feature_width),
        embed_mine,
        preferred_element_type=jnp.float32,
    )
    score_full = lax.all_gather(score_rows, "mp", axis=1, tiled=True)

    def assess(full_rows):
        normed, lifted = modulate(full_rows, gain_mine, score_mod)
        return jnp.dot(lifted, weight_mine, preferred_element_type=jnp.float32).astype(jnp.bfloat16)

    def skip_assess(full_rows):
        return jnp.zeros((2 * half * slice_rows, half_width), jnp.bfloat16)

    prediction = lax.cond(in_generator, skip_assess, assess, score_full)
    grouped = prediction.reshape(half, 2, slice_rows, half_width)
    by_owner = jnp.concatenate([grouped[:, 1], grouped[:, 0]], axis=0)
    returned = lax.all_to_all(by_owner, "fsdp", split_axis=0, concat_axis=0, tiled=True)
    real_block = returned[:quarter].reshape(block_rows, half_width).astype(jnp.float32)
    fake_block = returned[quarter:half].reshape(block_rows, half_width).astype(jnp.float32)
    own_share = block_shares(lookup(noise_step, position[None]))[0]
    own_grad = (own_share * (real_block - fake_block)).astype(jnp.bfloat16)
    handed = jnp.where(in_generator, gen_noised[block_rows:], own_grad)
    taken = shifted(handed, "fsdp", half)

    def reverse(operands):
        grad_rows, normed = operands
        backward = lax.dot_general(
            grad_rows, weight_mine, (((1,), (1,)), ((), ())), preferred_element_type=jnp.float32
        )
        scaled = backward.reshape(2, block_rows, model_width) * (1.0 + gen_mod[:, None, :])
        return jnp.sum(scaled.reshape(2 * block_rows, model_width) * normed, axis=0) / block_rows

    def skip_reverse(operands):
        return jnp.zeros((model_width,), jnp.float32)

    grad_rows = jnp.concatenate([own_grad, taken], axis=0)
    gain_term = lax.cond(in_generator, reverse, skip_reverse, (grad_rows, gen_normed))
    gain_grad = lax.psum_scatter(gain_term, ("fsdp", "mp"), scatter_dimension=0, tiled=True)
    noised_out = jnp.where(in_generator, gen_noised[:block_rows], taken)
    return (noised_out, own_grad, gain_grad)


def on_tiles(
    noise_in,
    renoise,
    gen_step,
    noise_step,
    gen_weight,
    real_weight,
    fake_weight,
    gen_embed,
    real_embed,
    fake_embed,
    gen_gain,
    real_gain,
    fake_gain,
):
    g = lax.axis_size("fsdp") // 2
    r, h = noise_in.shape
    d = 2 * h
    w = h // g
    t = g * r
    blocks = gen_step.shape[0]
    f32, bf16 = jnp.float32, jnp.bfloat16
    tail = 16
    span = range(g)

    def place():
        position, c = lax.axis_index("fsdp"), lax.axis_index("mp")
        return lax.div(position, g), lax.rem(position, g), c

    def flat(s_, q_, c_):
        return (s_ * g + q_) * 2 + c_

    every = [(s_, q_, c_) for s_ in (0, 1) for q_ in span for c_ in (0, 1)]

    def in_square(value, k):
        return lax.ppermute(value, "fsdp", [(i, i ^ k) for i in range(2 * g)])

    def across(value):
        return lax.ppermute(value, "fsdp", [(i, i ^ g) for i in range(2 * g)])

    def cores(value):
        return lax.ppermute(value, "mp", [(0, 1), (1, 0)])

    def turned(value):
        return lax.ppermute(value, ("fsdp", "mp"), [(flat(*i), flat(i[2], i[1], i[0])) for i in every])

    whole = pl.BlockSpec(memory_space=pltpu.VMEM)
    scalars = pl.BlockSpec(memory_space=pltpu.SMEM)

    def call(kernel, operands, outs, flops, scratch=(), in_scalars=0):
        moved = sum(o.size * o.dtype.itemsize for o in operands)
        return pl.pallas_call(
            kernel,
            in_specs=[scalars] * in_scalars + [whole] * (len(operands) - in_scalars),
            out_specs=[whole] * len(outs),
            out_shape=[jax.ShapeDtypeStruct(*o) for o in outs],
            scratch_shapes=list(scratch),
            compiler_params=pltpu.CompilerParams(vmem_limit_bytes=40 * 1024 * 1024),
            cost_estimate=pl.CostEstimate(flops=flops, bytes_accessed=moved, transcendentals=0),
        )(*operands)

    def rows_of(columns):
        return jnp.broadcast_to(columns, (t, 128)).T[:8]

    def columns_of(rows):
        return rows.T[:, :1]

    def pack(rows, store):
        high = rows.astype(bf16)
        rest = rows - high.astype(f32)
        middle = rest.astype(bf16)
        low = (rest - middle.astype(f32)).astype(bf16)
        line = lax.broadcasted_iota(jnp.int32, rows.shape, 0)
        mixed = jnp.where(line == 0, high.astype(f32), jnp.where(line == 1, middle.astype(f32), low.astype(f32)))
        mixed = jnp.where(line < 3, mixed, 0.0)
        store(jnp.concatenate([mixed, jnp.zeros_like(mixed)], axis=0).astype(bf16))

    def unpack(block):
        return jnp.sum(block.astype(f32), axis=0, keepdims=True)

    def share(steps, block):
        return (steps[block].astype(f32) + 1.0) / (NT + 1.0)

    def band(j):
        return slice(j * r, (j + 1) * r)

    def lanes(k):
        return pl.ds(pl.multiple_of(k * w, w), w)

    def scales_kernel(features, *refs):
        sources, out, held, sems = refs[:6], refs[6], refs[7:13], refs[13]
        s, _, _ = place()
        mine = pl.ds(pl.multiple_of(s * h, h), h)
        per = h // 128
        copies = [
            pltpu.make_async_copy(source.at[:, mine] if n < 3 else source, here, sems.at[n])
            for n, (source, here) in enumerate(zip(sources, held))
        ]
        for copy in copies:
            copy.start()
        for copy in copies:
            copy.wait()

        def gain(ref):
            return jnp.concatenate([ref[pl.ds(s * per + i, 1), :] for i in range(per)], axis=1)

        for n in range(3):
            steps = slice(0, blocks) if n == 0 else slice(blocks, 2 * blocks)
            mod = 1.0 + jnp.dot(features[steps, :], held[n][...], preferred_element_type=f32)
            if n == 0:
                out[3] = mod
            scale = mod * gain(held[3 + n])
            out[n] = -scale if n == 2 else scale

    gains = [v.reshape(-1, 128) for v in (gen_gain, real_gain, fake_gain)]
    scales = pl.pallas_call(
        scales_kernel,
        in_specs=[whole] + [pl.BlockSpec(memory_space=pltpu.HBM)] * 6,
        out_specs=whole,
        out_shape=jax.ShapeDtypeStruct((4, blocks, h), f32),
        scratch_shapes=[pltpu.VMEM((gen_embed.shape[0], h), bf16)] * 3
        + [pltpu.VMEM(v.shape, f32) for v in gains]
        + [pltpu.SemaphoreType.DMA((6,))],
        compiler_params=pltpu.CompilerParams(vmem_limit_bytes=40 * 1024 * 1024),
        cost_estimate=pl.CostEstimate(flops=6 * blocks * 128 * h, bytes_accessed=6 * 128 * h, transcendentals=0),
    )(
        step_features(jnp.concatenate([gen_step, noise_step]), gen_embed.shape[0]),
        gen_embed,
        real_embed,
        fake_embed,
        *gains,
    )

    depth = gen_weight.shape[0]
    fold = r // g
    shared = g // 2

    part_rows = depth // 2

    def rows_half(n):
        return pl.ds(pl.multiple_of(n * part_rows, 16), part_rows)

    def cut_gen_kernel(weight, *outs):
        _, q, _ = place()
        copy = lax.axis_index("rep")
        for k in span:
            if k < shared:
                outs[k][...] = weight[:, lanes(q ^ k)]
            else:
                outs[k][...] = weight[rows_half(copy), lanes(q ^ k)]

    def join_gen_kernel(*refs):
        copy = lax.axis_index("rep")
        n = g - shared
        for fetched, given, out in zip(refs[:n], refs[n : 2 * n], refs[2 * n :]):
            out[rows_half(copy), :] = fetched[...]
            out[rows_half(1 - copy), :] = given[...]

    def cut_score_kernel(real, fake, *outs):
        _, q, _ = place()
        for k in span:
            if k < shared:
                outs[k][0] = real[:, lanes(q ^ k)]
                outs[k][1] = fake[:, lanes(q ^ k)]
            else:
                for n, weight in enumerate((real, fake)):

                    @pl.when(lax.axis_index("rep") == n)
                    def _():
                        outs[k][...] = weight[:, lanes(q ^ k)]

    def cut_rows_kernel(rows, fresh, *outs):
        _, q, _ = place()
        for k in span:
            outs[k][0:r, :] = rows[...]
            for i in span:
                outs[k][r : r + fold, i * w : (i + 1) * w] = fresh[i * fold : (i + 1) * fold, lanes(q ^ k)]

    def swap_all(tile):
        counts = [v.size // (depth * w) for v in tile]

        def join_kernel(*refs):
            out, at = refs[-1], 0
            for ref, n in zip(refs[:-1], counts):
                for i in range(n):
                    out[at] = ref[i] if n > 1 else ref[...]
                    at += 1

        (joined,) = call(join_kernel, tile, [((sum(counts), depth, w), bf16)], depth * w)
        return cores(joined)

    x_turned, fresh_turned = turned(noise_in), turned(renoise)
    gen_sent = call(cut_gen_kernel, [gen_weight], [((depth, w), bf16)] * shared + [((part_rows, w), bf16)] * (g - shared), depth * h)
    gen_mine = [gen_sent[0]] + [in_square(gen_sent[k], k) for k in range(1, g)]
    x_sent = call(cut_rows_kernel, [x_turned, fresh_turned], [((r + fold, h), bf16)] * g, r * h)
    x_sent = list(x_sent)
    *fetched, x_sent[0] = lax.optimization_barrier((*gen_mine[shared:], x_sent[0]))
    given = [lax.ppermute(v, "rep", [(0, 1), (1, 0)]) for v in fetched]
    gen_mine[shared:] = call(join_gen_kernel, fetched + given, [((depth, w), bf16)] * (g - shared), depth * w)
    x = [x_sent[0]] + [in_square(x_sent[k], k) for k in range(1, g)]
    gen_swap, x[1], scales = lax.optimization_barrier((gen_mine, x[1], scales))
    gen_other = [cores(v) for v in gen_swap]
    real_weight, fake_weight, _ = lax.optimization_barrier((real_weight, fake_weight, x_turned))
    score_sent = call(
        cut_score_kernel,
        [real_weight, fake_weight],
        [((2, depth, w), bf16)] * shared + [((depth, w), bf16)] * (g - shared),
        2 * depth * h,
    )
    score_mine = [score_sent[0]] + [in_square(score_sent[k], k) for k in range(1, g)]

    def generate_kernel(steps, *refs):
        xs, scale, own, other = refs[:g], refs[g], refs[g + 1 : 2 * g + 1], refs[2 * g + 1 : 3 * g + 1]
        keep, away, sums, base, lift = refs[3 * g + 1 :]
        s, q, c = place()
        totals = []
        for j in span:
            wide = xs[j][0:r, :].astype(f32)
            totals.append(jnp.sum(wide * wide, axis=1, keepdims=True))
            lift[band(j), :] = (wide * scale[0, pl.ds(c * g + (q ^ j), 1), :]).astype(bf16)
            part = share(steps, c * g + (q ^ j))
            for i in span:
                some = slice(i * fold, (i + 1) * fold)
                base[j * r + i * fold : j * r + (i + 1) * fold, :] = (1.0 - part) * xs[j][some, lanes(q)].astype(
                    f32
                ) + part * xs[j][r : r + fold, i * w : (i + 1) * w].astype(f32)
        here = jnp.zeros((t, w), f32)
        there = jnp.zeros((t, w), f32)
        for k in span:
            part = lift[:, lanes(q ^ k)]
            here = here + jnp.dot(part, own[k][...], preferred_element_type=f32)
            there = there + jnp.dot(part, other[k][...], preferred_element_type=f32)
        stays = s == c
        keep[...] = jnp.where(stays, here, there)
        away[0:t, :] = jnp.where(stays, there, here).astype(bf16)
        rows = rows_of(jnp.concatenate(totals, axis=0))
        sums[...] = rows

        def store(value):
            away[t : t + tail, 0:t] = value

        if w > t:
            away[t : t + tail, t:] = jnp.zeros((tail, w - t), bf16)
        pack(rows, store)

    keep, away, x_sums, base = call(
        generate_kernel,
        [noise_step] + x + [scales] + gen_mine + gen_other,
        [((t, w), f32), ((t + tail, w), bf16), ((8, t), f32), ((t, w), f32)],
        4 * t * h * w,
        [pltpu.VMEM((t, h), bf16)],
        in_scalars=1,
    )

    def inverse_rms(sums, came):
        total = sums[...] + unpack(came[t : t + tail, 0:t])
        return columns_of(lax.rsqrt(total / d + norm_epsilon))

    def blend_kernel(steps, keep, came, sums, base, noised, root):
        _, q, c = place()
        inverse = inverse_rms(sums, came)
        root[...] = jnp.broadcast_to(inverse, (t, 128))
        for j in span:
            stay = 1.0 - share(steps, c * g + (q ^ j))
            made = keep[band(j), :] + came[band(j), :].astype(f32)
            noised[band(j), :] = (base[band(j), :] + (stay * inverse[band(j), :]) * made).astype(bf16)

    came, *fetched = lax.optimization_barrier((across(away), *score_mine[shared : g - 1]))
    score_mine[shared : g - 1] = fetched
    for k in range(shared, g):
        score_mine.append(lax.ppermute(score_mine[k], "rep", [(0, 1), (1, 0)]))
    noised_mine, x_root = call(
        blend_kernel,
        [noise_step, keep, came, x_sums, base],
        [((t, w), bf16), ((t, 128), f32)],
        10 * t * w,
        in_scalars=1,
    )
    noised_last, score_mine[1] = lax.optimization_barrier((noised_mine, score_mine[1]))
    noised = [noised_mine, in_square(noised_last, 1)] + [in_square(noised_mine, k) for k in range(2, g)]

    tiles = len(score_mine)

    def score_product(lifts, tile):
        copy = lax.axis_index("rep")
        total = jnp.zeros((t, w), f32)
        for k in span:
            columns = slice(k * w, (k + 1) * w)
            if k < shared:
                pairs = [(tile[k][0], 0), (tile[k][1], 1)]
            else:
                pairs = [(tile[k][...], copy), (tile[k + g - shared][...], 1 - copy)]
            for part, n in pairs:
                total = total + jnp.dot(lifts[n, :, columns], part, preferred_element_type=f32)
        return total

    def score_kernel(*refs):
        ns, scale, own = refs[:g], refs[g], refs[g + 1 : g + 1 + tiles]
        gap, away, sums, lifts = refs[g + 1 + tiles :]
        _, q, c = place()
        totals = [jnp.zeros((r, 1), f32) for _ in span]
        for k in span:
            columns = slice(k * w, (k + 1) * w)
            for j in span:
                block = pl.ds(c * g + (q ^ j), 1)
                wide = ns[k][band(j ^ k), :].astype(f32)
                totals[j] = totals[j] + jnp.sum(wide * wide, axis=1, keepdims=True)
                for n in (0, 1):
                    lifts[n, band(j), columns] = (wide * scale[1 + n, block, lanes(q ^ k)]).astype(bf16)
        here = score_product(lifts, own)
        gap[...] = here
        away[0:t, :] = here.astype(bf16)
        rows = rows_of(jnp.concatenate(totals, axis=0))
        sums[...] = rows
        if w > t:
            away[t : t + tail, t:] = jnp.zeros((tail, w - t), bf16)

        def store(value):
            away[t : t + tail, 0:t] = value

        pack(rows, store)

    noised_home, noised[2] = lax.optimization_barrier((noised_mine, noised[2]))
    gap_here, away_here, noised_sums, lifts = call(
        score_kernel,
        noised + [scales] + score_mine,
        [((t, w), f32), ((t + tail, w), bf16), ((8, t), f32), ((2, t, h), bf16)],
        4 * t * h * w,
    )
    came_here = across(away_here)
    noised_owned, score_mine, gap_here = lax.optimization_barrier((turned(noised_home), score_mine, gap_here))
    score_mine, _ = lax.optimization_barrier((score_mine, cores(noised_sums)))
    score_other = swap_all(score_mine)

    def score_rest_kernel(lifts, other, gap, away):
        there = score_product(
            lifts,
            [(other[2 * k], other[2 * k + 1]) for k in range(shared)]
            + [other[shared + k] for k in range(shared, tiles)],
        )
        gap[...] = there
        away[...] = there.astype(bf16)

    gap_there, away_there = call(
        score_rest_kernel, [lifts, score_other], [((t, w), f32), ((t, w), bf16)], 4 * t * h * w
    )
    came_there = across(away_there)

    def gradient(steps, gap, came, inverse, grad, outs):
        _, q, c = place()
        for j in span:
            part = share(steps, c * g + (q ^ j))
            value = (part * inverse[band(j), :]) * (gap[band(j), :] + came[band(j), :].astype(f32))
            grad[band(j), :] = value.astype(bf16)
            outs[j][0:r, :] = value.astype(bf16)

    def gain_sums(grad, tile, xs, root, scale):
        _, q, c = place()
        sums = []
        for k in span:
            back = lax.dot_general(grad[...], tile[k][...], (((1,), (1,)), ((), ())), preferred_element_type=f32)
            total = jnp.zeros((1, w), f32)
            for j in span:
                normed = xs[j][0:r, lanes(q ^ k)].astype(f32) * root[band(j), :1]
                summed = jnp.sum(back[band(j), :] * normed, axis=0, keepdims=True)
                total = total + summed * scale[3, pl.ds(c * g + (q ^ j), 1), lanes(q ^ k)]
            sums.append(total)
        return sums

    def backward_kernel(steps, gap, came, sums, root, scale, owned, *refs):
        xs, own, outs, (noised_root, partial, grad) = refs[:g], refs[g : 2 * g], refs[2 * g : 3 * g], refs[3 * g :]
        inverse = inverse_rms(sums, came)
        noised_root[...] = jnp.broadcast_to(inverse, (t, 128))
        gradient(steps, gap, came, inverse, grad, outs)
        for k, total in enumerate(gain_sums(grad, own, xs, root, scale)):
            partial[k : k + 1, :] = total
            outs[k][r : 2 * r, :] = owned[band(k), :]

    *sent_here, noised_root, partial = call(
        backward_kernel,
        [noise_step, gap_here, came_here, noised_sums, x_root, scales, noised_owned] + x + gen_mine,
        [((2 * r, w), bf16)] * g + [((t, 128), f32), ((8, w), f32)],
        2 * t * h * w,
        [pltpu.VMEM((t, w), bf16)],
        in_scalars=1,
    )
    arrived_here = [sent_here[0]] + [in_square(sent_here[k], k) for k in range(1, g)]

    def backward_rest_kernel(steps, gap, came, noised_root, partial, root, scale, *refs):
        xs, other, outs, (grad,) = refs[:g], refs[g : 2 * g], refs[2 * g : 3 * g], refs[3 * g :]
        gradient(steps, gap, came, noised_root[:, :1], grad, outs)
        for k, total in enumerate(gain_sums(grad, other, xs, root, scale)):

            def store(value):
                outs[k][r : r + tail, :] = value

            pack(jnp.broadcast_to((total + partial[k : k + 1, :]) / r, (8, w)), store)

    sent_there = call(
        backward_rest_kernel,
        [noise_step, gap_there, came_there, noised_root, partial, x_root, scales] + x + gen_other,
        [((r + tail, w), bf16)] * g,
        2 * t * h * w,
        [pltpu.VMEM((t, w), bf16)],
        in_scalars=1,
    )
    arrived_there = [sent_there[0]] + [in_square(sent_there[k], k) for k in range(1, g)]

    def gather_kernel(*refs):
        a, b, (here, there, gains, noised) = refs[:g], refs[g : 2 * g], refs[2 * g :]
        _, q, _ = place()
        total = jnp.zeros((1, w), f32)
        for k in span:
            here[:, lanes(q ^ k)] = a[k][0:r, :]
            noised[:, lanes(q ^ k)] = a[k][r : 2 * r, :]
            there[0:r, lanes(q ^ k)] = b[k][0:r, :]
            total = total + unpack(b[k][r : r + tail, :])
        gains[...] = total

        def store(value):
            there[r : r + tail, :w] = value

        pack(jnp.broadcast_to(total, (8, w)), store)
        there[r : r + tail, w:] = jnp.zeros((tail, h - w), bf16)

    here, there, gains, noised_out = call(
        gather_kernel,
        arrived_here + arrived_there,
        [((r, h), bf16), ((r + tail, h), bf16), ((1, w), f32), ((r, h), bf16)],
        t * h,
    )
    other_core = cores(there)

    def finish_kernel(here, gains, came, grad, gain):
        s, _, c = place()
        grad[...] = jnp.where(s == c, here[...], came[0:r, :])
        both = gains[...] + unpack(came[r : r + tail, :w])
        gain[...] = jnp.where(c == 0, both[:, : w // 2], both[:, w // 2 :])

    latent_grad, gain = call(
        finish_kernel, [here, gains, other_core], [((r, h), bf16), ((1, w // 2), f32)], r * h
    )
    return (noised_out, latent_grad, gain[0])


def solution(mesh):
    positions = mesh.shape["fsdp"]
    on_device = on_tiles if (positions, mesh.shape["rep"], mesh.shape["mp"]) == (8, 2, 2) else on_groups
    return jax.shard_map(
        on_device,
        mesh=mesh,
        in_specs=(
            P(("rep", "fsdp"), "mp"),
            P(("rep", "fsdp"), "mp"),
            P("rep"),
            P("rep"),
            P("fsdp", "mp"),
            P("fsdp", "mp"),
            P("fsdp", "mp"),
            P(),
            P(),
            P(),
            P(),
            P(),
            P(),
        ),
        out_specs=(P(("rep", "fsdp"), "mp"), P(("rep", "fsdp"), "mp"), P(("rep", "fsdp", "mp"))),
        check_vma=False,
    )
```

```python
import math

import jax
import jax.numpy as jnp
from jax import lax
from jax.experimental import pallas as pl
from jax.experimental.pallas import tpu as pltpu
from jax.sharding import PartitionSpec as P

NT = 1000


norm_epsilon = 1e-06


def from_behind(value, axis, by):
    size = lax.axis_size(axis)
    pairs = [(i, i + by) for i in range(size) if 0 <= i + by < size]
    return lax.ppermute(value, axis, pairs)


def shifted(value, axis, by):
    size = lax.axis_size(axis)
    return lax.ppermute(value, axis, [(i, (i + by) % size) for i in range(size)])


def step_features(step_ids, feature_width):
    half_width = feature_width // 2
    frequency = jnp.exp(-math.log(10000.0) * jnp.arange(half_width, dtype=jnp.float32) / half_width)
    angles = step_ids.astype(jnp.float32)[:, None] * frequency[None, :]
    return jnp.concatenate([jnp.cos(angles), jnp.sin(angles)], axis=1).astype(jnp.bfloat16)


def lookup(step_table, block_ids):
    matches = block_ids[:, None] == jnp.arange(step_table.shape[0], dtype=jnp.int32)[None, :]
    return jnp.sum(jnp.where(matches, step_table[None, :], 0), axis=1)


def block_shares(step_ids):
    return ((step_ids.astype(jnp.float32) + 1.0) / (NT + 1.0))[:, None, None]


def modulate(full_rows, gain_vec, modulation):
    blocks = modulation.shape[0]
    values = full_rows.astype(jnp.float32)
    normed = values * lax.rsqrt(jnp.mean(values * values, axis=1, keepdims=True) + norm_epsilon)
    lifted = normed.reshape(blocks, -1, values.shape[1]) * gain_vec * (1.0 + modulation[:, None, :])
    return (normed, lifted.reshape(values.shape).astype(jnp.bfloat16))


def on_groups(
    noise_in,
    renoise,
    gen_step,
    noise_step,
    gen_weight,
    real_weight,
    fake_weight,
    gen_embed,
    real_embed,
    fake_embed,
    gen_gain,
    real_gain,
    fake_gain,
):
    devices = lax.axis_size("fsdp")
    quarter = devices // 4
    half = 2 * quarter
    position = lax.axis_index("fsdp")
    block_rows = noise_in.shape[0]
    half_width = noise_in.shape[1]
    model_width = gen_gain.shape[0]
    feature_width = gen_embed.shape[0]
    slice_rows = 4 * block_rows // devices
    group_role = (position >= quarter).astype(jnp.int32) + (position >= half).astype(jnp.int32)
    in_generator = group_role == 2
    slot_ids = jnp.arange(devices, dtype=jnp.int32)
    slot_role = (
        (slot_ids >= quarter).astype(jnp.int32) + (slot_ids >= half).astype(jnp.int32)
    ).reshape(devices, 1, 1)
    outgoing = jnp.where(
        slot_role == 2,
        gen_weight[None],
        jnp.where(slot_role == 0, real_weight[None], fake_weight[None]),
    )
    received = lax.all_to_all(outgoing, "fsdp", split_axis=0, concat_axis=0, tiled=True)
    weight_mine = received.reshape(model_width, half_width)
    embed_mine = jnp.where(
        group_role == 2, gen_embed, jnp.where(group_role == 0, real_embed, fake_embed)
    )
    gain_mine = jnp.where(
        group_role == 2, gen_gain, jnp.where(group_role == 0, real_gain, fake_gain)
    )
    partner_noise, partner_renoise = from_behind((noise_in, renoise), "fsdp", half)
    gen_ids = jnp.stack([position, (position + half) % devices])
    gen_mod = jnp.dot(
        step_features(lookup(gen_step, gen_ids), feature_width),
        embed_mine,
        preferred_element_type=jnp.float32,
    )
    gen_shares = block_shares(lookup(noise_step, gen_ids))
    gen_rows = jnp.concatenate([noise_in, partner_noise], axis=0)
    gen_noise = jnp.concatenate([renoise, partner_renoise], axis=0)
    gen_full = lax.all_gather(gen_rows, "mp", axis=1, tiled=True)

    def generate(operands):
        full_rows, own_rows, fresh_noise = operands
        normed, lifted = modulate(full_rows, gain_mine, gen_mod)
        latents = own_rows.astype(jnp.float32) + jnp.dot(
            lifted, weight_mine, preferred_element_type=jnp.float32
        )
        blended = (1.0 - gen_shares) * latents.reshape(
            2, block_rows, half_width
        ) + gen_shares * fresh_noise.astype(jnp.float32).reshape(2, block_rows, half_width)
        return (blended.reshape(2 * block_rows, half_width).astype(jnp.bfloat16), normed)

    def skip_generate(operands):
        return (
            jnp.zeros((2 * block_rows, half_width), jnp.bfloat16),
            jnp.zeros((2 * block_rows, model_width), jnp.float32),
        )

    gen_noised, gen_normed = lax.cond(
        in_generator, generate, skip_generate, (gen_full, gen_rows, gen_noise)
    )
    width_now = gen_noised.shape[1]
    pieces = (
        gen_noised.reshape(2, quarter, slice_rows, width_now)
        .transpose(1, 0, 2, 3)
        .reshape(quarter, 2 * slice_rows, width_now)
    )
    send_rows = jnp.concatenate(
        [pieces, pieces, jnp.zeros((half, 2 * slice_rows, width_now), jnp.bfloat16)], axis=0
    )
    arrived = lax.all_to_all(send_rows, "fsdp", split_axis=0, concat_axis=0, tiled=True)
    score_rows = arrived[half:].reshape(2 * half * slice_rows, width_now)
    gen_slots = jnp.arange(half, dtype=jnp.int32)
    score_ids = jnp.stack([gen_slots + half, gen_slots], axis=1).reshape(2 * half)
    score_mod = jnp.dot(
        step_features(lookup(noise_step, score_ids), feature_width),
        embed_mine,
        preferred_element_type=jnp.float32,
    )
    score_full = lax.all_gather(score_rows, "mp", axis=1, tiled=True)

    def assess(full_rows):
        normed, lifted = modulate(full_rows, gain_mine, score_mod)
        return jnp.dot(lifted, weight_mine, preferred_element_type=jnp.float32).astype(jnp.bfloat16)

    def skip_assess(full_rows):
        return jnp.zeros((2 * half * slice_rows, half_width), jnp.bfloat16)

    prediction = lax.cond(in_generator, skip_assess, assess, score_full)
    grouped = prediction.reshape(half, 2, slice_rows, half_width)
    by_owner = jnp.concatenate([grouped[:, 1], grouped[:, 0]], axis=0)
    returned = lax.all_to_all(by_owner, "fsdp", split_axis=0, concat_axis=0, tiled=True)
    real_block = returned[:quarter].reshape(block_rows, half_width).astype(jnp.float32)
    fake_block = returned[quarter:half].reshape(block_rows, half_width).astype(jnp.float32)
    own_share = block_shares(lookup(noise_step, position[None]))[0]
    own_grad = (own_share * (real_block - fake_block)).astype(jnp.bfloat16)
    handed = jnp.where(in_generator, gen_noised[block_rows:], own_grad)
    taken = shifted(handed, "fsdp", half)

    def reverse(operands):
        grad_rows, normed = operands
        backward = lax.dot_general(
            grad_rows, weight_mine, (((1,), (1,)), ((), ())), preferred_element_type=jnp.float32
        )
        scaled = backward.reshape(2, block_rows, model_width) * (1.0 + gen_mod[:, None, :])
        return jnp.sum(scaled.reshape(2 * block_rows, model_width) * normed, axis=0) / block_rows

    def skip_reverse(operands):
        return jnp.zeros((model_width,), jnp.float32)

    grad_rows = jnp.concatenate([own_grad, taken], axis=0)
    gain_term = lax.cond(in_generator, reverse, skip_reverse, (grad_rows, gen_normed))
    gain_grad = lax.psum_scatter(gain_term, ("fsdp", "mp"), scatter_dimension=0, tiled=True)
    noised_out = jnp.where(in_generator, gen_noised[:block_rows], taken)
    return (noised_out, own_grad, gain_grad)


def on_tiles(
    noise_in,
    renoise,
    gen_step,
    noise_step,
    gen_weight,
    real_weight,
    fake_weight,
    gen_embed,
    real_embed,
    fake_embed,
    gen_gain,
    real_gain,
    fake_gain,
):
    g = lax.axis_size("fsdp") // 2
    r, h = noise_in.shape
    d = 2 * h
    w = h // g
    t = g * r
    blocks = gen_step.shape[0]
    f32, bf16 = jnp.float32, jnp.bfloat16
    tail = 16
    span = range(g)

    def place():
        position, c = lax.axis_index("fsdp"), lax.axis_index("mp")
        return lax.div(position, g), lax.rem(position, g), c

    def flat(s_, q_, c_):
        return (s_ * g + q_) * 2 + c_

    every = [(s_, q_, c_) for s_ in (0, 1) for q_ in span for c_ in (0, 1)]

    def in_square(value, k):
        return lax.ppermute(value, "fsdp", [(i, i ^ k) for i in range(2 * g)])

    def across(value):
        return lax.ppermute(value, "fsdp", [(i, i ^ g) for i in range(2 * g)])

    def cores(value):
        return lax.ppermute(value, "mp", [(0, 1), (1, 0)])

    def turned(value):
        return lax.ppermute(value, ("fsdp", "mp"), [(flat(*i), flat(i[2], i[1], i[0])) for i in every])

    whole = pl.BlockSpec(memory_space=pltpu.VMEM)
    scalars = pl.BlockSpec(memory_space=pltpu.SMEM)

    def call(kernel, operands, outs, flops, scratch=(), in_scalars=0):
        moved = sum(o.size * o.dtype.itemsize for o in operands)
        return pl.pallas_call(
            kernel,
            in_specs=[scalars] * in_scalars + [whole] * (len(operands) - in_scalars),
            out_specs=[whole] * len(outs),
            out_shape=[jax.ShapeDtypeStruct(*o) for o in outs],
            scratch_shapes=list(scratch),
            compiler_params=pltpu.CompilerParams(vmem_limit_bytes=40 * 1024 * 1024),
            cost_estimate=pl.CostEstimate(flops=flops, bytes_accessed=moved, transcendentals=0),
        )(*operands)

    def rows_of(columns):
        return jnp.broadcast_to(columns, (t, 128)).T[:8]

    def columns_of(rows):
        return rows.T[:, :1]

    def pack(rows, store):
        high = rows.astype(bf16)
        rest = rows - high.astype(f32)
        middle = rest.astype(bf16)
        low = (rest - middle.astype(f32)).astype(bf16)
        line = lax.broadcasted_iota(jnp.int32, rows.shape, 0)
        mixed = jnp.where(line == 0, high.astype(f32), jnp.where(line == 1, middle.astype(f32), low.astype(f32)))
        mixed = jnp.where(line < 3, mixed, 0.0)
        store(jnp.concatenate([mixed, jnp.zeros_like(mixed)], axis=0).astype(bf16))

    def unpack(block):
        return jnp.sum(block.astype(f32), axis=0, keepdims=True)

    def share(steps, block):
        return (steps[block].astype(f32) + 1.0) / (NT + 1.0)

    def band(j):
        return slice(j * r, (j + 1) * r)

    def lanes(k):
        return pl.ds(pl.multiple_of(k * w, w), w)

    def scales_kernel(features, *refs):
        sources, out, held, sems = refs[:6], refs[6], refs[7:13], refs[13]
        s, _, _ = place()
        mine = pl.ds(pl.multiple_of(s * h, h), h)
        per = h // 128
        copies = [
            pltpu.make_async_copy(source.at[:, mine] if n < 3 else source, here, sems.at[n])
            for n, (source, here) in enumerate(zip(sources, held))
        ]
        for copy in copies:
            copy.start()
        for copy in copies:
            copy.wait()

        def gain(ref):
            return jnp.concatenate([ref[pl.ds(s * per + i, 1), :] for i in range(per)], axis=1)

        for n in range(3):
            steps = slice(0, blocks) if n == 0 else slice(blocks, 2 * blocks)
            mod = 1.0 + jnp.dot(features[steps, :], held[n][...], preferred_element_type=f32)
            if n == 0:
                out[3] = mod
            scale = mod * gain(held[3 + n])
            out[n] = -scale if n == 2 else scale

    gains = [v.reshape(-1, 128) for v in (gen_gain, real_gain, fake_gain)]
    scales = pl.pallas_call(
        scales_kernel,
        in_specs=[whole] + [pl.BlockSpec(memory_space=pltpu.HBM)] * 6,
        out_specs=whole,
        out_shape=jax.ShapeDtypeStruct((4, blocks, h), f32),
        scratch_shapes=[pltpu.VMEM((gen_embed.shape[0], h), bf16)] * 3
        + [pltpu.VMEM(v.shape, f32) for v in gains]
        + [pltpu.SemaphoreType.DMA((6,))],
        compiler_params=pltpu.CompilerParams(vmem_limit_bytes=40 * 1024 * 1024),
        cost_estimate=pl.CostEstimate(flops=6 * blocks * 128 * h, bytes_accessed=6 * 128 * h, transcendentals=0),
    )(
        step_features(jnp.concatenate([gen_step, noise_step]), gen_embed.shape[0]),
        gen_embed,
        real_embed,
        fake_embed,
        *gains,
    )

    depth = gen_weight.shape[0]
    fold = r // g
    shared = g // 2

    part_rows = depth // 2

    def rows_half(n):
        return pl.ds(pl.multiple_of(n * part_rows, 16), part_rows)

    def cut_gen_kernel(weight, *outs):
        _, q, _ = place()
        copy = lax.axis_index("rep")
        for k in span:
            if k < shared:
                outs[k][...] = weight[:, lanes(q ^ k)]
            else:
                outs[k][...] = weight[rows_half(copy), lanes(q ^ k)]

    def join_gen_kernel(*refs):
        copy = lax.axis_index("rep")
        n = g - shared
        for fetched, given, out in zip(refs[:n], refs[n : 2 * n], refs[2 * n :]):
            out[rows_half(copy), :] = fetched[...]
            out[rows_half(1 - copy), :] = given[...]

    def cut_score_kernel(real, fake, *outs):
        _, q, _ = place()
        for k in span:
            if k < shared:
                outs[k][0] = real[:, lanes(q ^ k)]
                outs[k][1] = fake[:, lanes(q ^ k)]
            else:
                for n, weight in enumerate((real, fake)):

                    @pl.when(lax.axis_index("rep") == n)
                    def _():
                        outs[k][...] = weight[:, lanes(q ^ k)]

    def cut_rows_kernel(rows, fresh, *outs):
        _, q, _ = place()
        for k in span:
            outs[k][0:r, :] = rows[...]
            for i in span:
                outs[k][r : r + fold, i * w : (i + 1) * w] = fresh[i * fold : (i + 1) * fold, lanes(q ^ k)]

    def swap_all(tile):
        counts = [v.size // (depth * w) for v in tile]

        def join_kernel(*refs):
            out, at = refs[-1], 0
            for ref, n in zip(refs[:-1], counts):
                for i in range(n):
                    out[at] = ref[i] if n > 1 else ref[...]
                    at += 1

        (joined,) = call(join_kernel, tile, [((sum(counts), depth, w), bf16)], depth * w)
        return cores(joined)

    x_turned, fresh_turned = turned(noise_in), turned(renoise)
    gen_sent = call(cut_gen_kernel, [gen_weight], [((depth, w), bf16)] * shared + [((part_rows, w), bf16)] * (g - shared), depth * h)
    gen_mine = [gen_sent[0]] + [in_square(gen_sent[k], k) for k in range(1, g)]
    x_sent = call(cut_rows_kernel, [x_turned, fresh_turned], [((r + fold, h), bf16)] * g, r * h)
    x_sent = list(x_sent)
    *fetched, x_sent[0] = lax.optimization_barrier((*gen_mine[shared:], x_sent[0]))
    given = [lax.ppermute(v, "rep", [(0, 1), (1, 0)]) for v in fetched]
    gen_mine[shared:] = call(join_gen_kernel, fetched + given, [((depth, w), bf16)] * (g - shared), depth * w)
    x = [x_sent[0]] + [in_square(x_sent[k], k) for k in range(1, g)]
    gen_swap, x[1], scales = lax.optimization_barrier((gen_mine, x[1], scales))
    gen_other = [cores(v) for v in gen_swap]
    real_weight, fake_weight, _ = lax.optimization_barrier((real_weight, fake_weight, x_turned))
    score_sent = call(
        cut_score_kernel,
        [real_weight, fake_weight],
        [((2, depth, w), bf16)] * shared + [((depth, w), bf16)] * (g - shared),
        2 * depth * h,
    )
    score_mine = [score_sent[0]] + [in_square(score_sent[k], k) for k in range(1, g)]

    def generate_kernel(steps, *refs):
        xs, scale, own, other = refs[:g], refs[g], refs[g + 1 : 2 * g + 1], refs[2 * g + 1 : 3 * g + 1]
        keep, away, sums, base, lift = refs[3 * g + 1 :]
        s, q, c = place()
        totals = []
        for j in span:
            wide = xs[j][0:r, :].astype(f32)
            totals.append(jnp.sum(wide * wide, axis=1, keepdims=True))
            lift[band(j), :] = (wide * scale[0, pl.ds(c * g + (q ^ j), 1), :]).astype(bf16)
            part = share(steps, c * g + (q ^ j))
            for i in span:
                some = slice(i * fold, (i + 1) * fold)
                base[j * r + i * fold : j * r + (i + 1) * fold, :] = (1.0 - part) * xs[j][some, lanes(q)].astype(
                    f32
                ) + part * xs[j][r : r + fold, i * w : (i + 1) * w].astype(f32)
        here = jnp.zeros((t, w), f32)
        there = jnp.zeros((t, w), f32)
        for k in span:
            part = lift[:, lanes(q ^ k)]
            here = here + jnp.dot(part, own[k][...], preferred_element_type=f32)
            there = there + jnp.dot(part, other[k][...], preferred_element_type=f32)
        stays = s == c
        keep[...] = jnp.where(stays, here, there)
        away[0:t, :] = jnp.where(stays, there, here).astype(bf16)
        rows = rows_of(jnp.concatenate(totals, axis=0))
        sums[...] = rows

        def store(value):
            away[t : t + tail, 0:t] = value

        if w > t:
            away[t : t + tail, t:] = jnp.zeros((tail, w - t), bf16)
        pack(rows, store)

    keep, away, x_sums, base = call(
        generate_kernel,
        [noise_step] + x + [scales] + gen_mine + gen_other,
        [((t, w), f32), ((t + tail, w), bf16), ((8, t), f32), ((t, w), f32)],
        4 * t * h * w,
        [pltpu.VMEM((t, h), bf16)],
        in_scalars=1,
    )

    def inverse_rms(sums, came):
        total = sums[...] + unpack(came[t : t + tail, 0:t])
        return columns_of(lax.rsqrt(total / d + norm_epsilon))

    def blend_kernel(steps, keep, came, sums, base, noised, root):
        _, q, c = place()
        inverse = inverse_rms(sums, came)
        root[...] = jnp.broadcast_to(inverse, (t, 128))
        for j in span:
            stay = 1.0 - share(steps, c * g + (q ^ j))
            made = keep[band(j), :] + came[band(j), :].astype(f32)
            noised[band(j), :] = (base[band(j), :] + (stay * inverse[band(j), :]) * made).astype(bf16)

    score_mine += [lax.ppermute(v, "rep", [(0, 1), (1, 0)]) for v in score_mine[shared:g]]
    came, score_mine[shared] = lax.optimization_barrier((across(away), score_mine[shared]))
    noised_mine, x_root = call(
        blend_kernel,
        [noise_step, keep, came, x_sums, base],
        [((t, w), bf16), ((t, 128), f32)],
        10 * t * w,
        in_scalars=1,
    )
    noised_last, score_mine[1] = lax.optimization_barrier((noised_mine, score_mine[1]))
    noised = [noised_mine, in_square(noised_last, 1)] + [in_square(noised_mine, k) for k in range(2, g)]

    tiles = len(score_mine)

    def score_product(lifts, tile):
        copy = lax.axis_index("rep")
        total = jnp.zeros((t, w), f32)
        for k in span:
            columns = slice(k * w, (k + 1) * w)
            if k < shared:
                pairs = [(tile[k][0], 0), (tile[k][1], 1)]
            else:
                pairs = [(tile[k][...], copy), (tile[k + g - shared][...], 1 - copy)]
            for part, n in pairs:
                total = total + jnp.dot(lifts[n, :, columns], part, preferred_element_type=f32)
        return total

    def score_kernel(*refs):
        ns, scale, own = refs[:g], refs[g], refs[g + 1 : g + 1 + tiles]
        gap, away, sums, lifts = refs[g + 1 + tiles :]
        _, q, c = place()
        totals = [jnp.zeros((r, 1), f32) for _ in span]
        for k in span:
            columns = slice(k * w, (k + 1) * w)
            for j in span:
                block = pl.ds(c * g + (q ^ j), 1)
                wide = ns[k][band(j ^ k), :].astype(f32)
                totals[j] = totals[j] + jnp.sum(wide * wide, axis=1, keepdims=True)
                for n in (0, 1):
                    lifts[n, band(j), columns] = (wide * scale[1 + n, block, lanes(q ^ k)]).astype(bf16)
        here = score_product(lifts, own)
        gap[...] = here
        away[0:t, :] = here.astype(bf16)
        rows = rows_of(jnp.concatenate(totals, axis=0))
        sums[...] = rows
        if w > t:
            away[t : t + tail, t:] = jnp.zeros((tail, w - t), bf16)

        def store(value):
            away[t : t + tail, 0:t] = value

        pack(rows, store)

    noised_home, noised[2] = lax.optimization_barrier((noised_mine, noised[2]))
    gap_here, away_here, noised_sums, lifts = call(
        score_kernel,
        noised + [scales] + score_mine,
        [((t, w), f32), ((t + tail, w), bf16), ((8, t), f32), ((2, t, h), bf16)],
        4 * t * h * w,
    )
    came_here = across(away_here)
    noised_owned, score_mine, gap_here = lax.optimization_barrier((turned(noised_home), score_mine, gap_here))
    score_mine, _ = lax.optimization_barrier((score_mine, cores(noised_sums)))
    score_other = swap_all(score_mine)

    def score_rest_kernel(lifts, other, gap, away):
        there = score_product(
            lifts,
            [(other[2 * k], other[2 * k + 1]) for k in range(shared)]
            + [other[shared + k] for k in range(shared, tiles)],
        )
        gap[...] = there
        away[...] = there.astype(bf16)

    gap_there, away_there = call(
        score_rest_kernel, [lifts, score_other], [((t, w), f32), ((t, w), bf16)], 4 * t * h * w
    )
    came_there = across(away_there)

    def gradient(steps, gap, came, inverse, grad, outs):
        _, q, c = place()
        for j in span:
            part = share(steps, c * g + (q ^ j))
            value = (part * inverse[band(j), :]) * (gap[band(j), :] + came[band(j), :].astype(f32))
            grad[band(j), :] = value.astype(bf16)
            outs[j][0:r, :] = value.astype(bf16)

    def gain_sums(grad, tile, xs, root, scale):
        _, q, c = place()
        sums = []
        for k in span:
            back = lax.dot_general(grad[...], tile[k][...], (((1,), (1,)), ((), ())), preferred_element_type=f32)
            total = jnp.zeros((1, w), f32)
            for j in span:
                normed = xs[j][0:r, lanes(q ^ k)].astype(f32) * root[band(j), :1]
                summed = jnp.sum(back[band(j), :] * normed, axis=0, keepdims=True)
                total = total + summed * scale[3, pl.ds(c * g + (q ^ j), 1), lanes(q ^ k)]
            sums.append(total)
        return sums

    def backward_kernel(steps, gap, came, sums, root, scale, owned, *refs):
        xs, own, outs, (noised_root, partial, grad) = refs[:g], refs[g : 2 * g], refs[2 * g : 3 * g], refs[3 * g :]
        inverse = inverse_rms(sums, came)
        noised_root[...] = jnp.broadcast_to(inverse, (t, 128))
        gradient(steps, gap, came, inverse, grad, outs)
        for k, total in enumerate(gain_sums(grad, own, xs, root, scale)):
            partial[k : k + 1, :] = total
            outs[k][r : 2 * r, :] = owned[band(k), :]

    *sent_here, noised_root, partial = call(
        backward_kernel,
        [noise_step, gap_here, came_here, noised_sums, x_root, scales, noised_owned] + x + gen_mine,
        [((2 * r, w), bf16)] * g + [((t, 128), f32), ((8, w), f32)],
        2 * t * h * w,
        [pltpu.VMEM((t, w), bf16)],
        in_scalars=1,
    )
    arrived_here = [sent_here[0]] + [in_square(sent_here[k], k) for k in range(1, g)]

    def backward_rest_kernel(steps, gap, came, noised_root, partial, root, scale, *refs):
        xs, other, outs, (grad,) = refs[:g], refs[g : 2 * g], refs[2 * g : 3 * g], refs[3 * g :]
        gradient(steps, gap, came, noised_root[:, :1], grad, outs)
        for k, total in enumerate(gain_sums(grad, other, xs, root, scale)):

            def store(value):
                outs[k][r : r + tail, :] = value

            pack(jnp.broadcast_to((total + partial[k : k + 1, :]) / r, (8, w)), store)

    sent_there = call(
        backward_rest_kernel,
        [noise_step, gap_there, came_there, noised_root, partial, x_root, scales] + x + gen_other,
        [((r + tail, w), bf16)] * g,
        2 * t * h * w,
        [pltpu.VMEM((t, w), bf16)],
        in_scalars=1,
    )
    arrived_there = [sent_there[0]] + [in_square(sent_there[k], k) for k in range(1, g)]

    def gather_kernel(*refs):
        a, b, (here, there, gains, noised) = refs[:g], refs[g : 2 * g], refs[2 * g :]
        _, q, _ = place()
        total = jnp.zeros((1, w), f32)
        for k in span:
            here[:, lanes(q ^ k)] = a[k][0:r, :]
            noised[:, lanes(q ^ k)] = a[k][r : 2 * r, :]
            there[0:r, lanes(q ^ k)] = b[k][0:r, :]
            total = total + unpack(b[k][r : r + tail, :])
        gains[...] = total

        def store(value):
            there[r : r + tail, :w] = value

        pack(jnp.broadcast_to(total, (8, w)), store)
        there[r : r + tail, w:] = jnp.zeros((tail, h - w), bf16)

    here, there, gains, noised_out = call(
        gather_kernel,
        arrived_here + arrived_there,
        [((r, h), bf16), ((r + tail, h), bf16), ((1, w), f32), ((r, h), bf16)],
        t * h,
    )
    other_core = cores(there)

    def finish_kernel(here, gains, came, grad, gain):
        s, _, c = place()
        grad[...] = jnp.where(s == c, here[...], came[0:r, :])
        both = gains[...] + unpack(came[r : r + tail, :w])
        gain[...] = jnp.where(c == 0, both[:, : w // 2], both[:, w // 2 :])

    latent_grad, gain = call(
        finish_kernel, [here, gains, other_core], [((r, h), bf16), ((1, w // 2), f32)], r * h
    )
    return (noised_out, latent_grad, gain[0])


def solution(mesh):
    positions = mesh.shape["fsdp"]
    on_device = on_tiles if (positions, mesh.shape["rep"], mesh.shape["mp"]) == (8, 2, 2) else on_groups
    return jax.shard_map(
        on_device,
        mesh=mesh,
        in_specs=(
            P(("rep", "fsdp"), "mp"),
            P(("rep", "fsdp"), "mp"),
            P("rep"),
            P("rep"),
            P("fsdp", "mp"),
            P("fsdp", "mp"),
            P("fsdp", "mp"),
            P(),
            P(),
            P(),
            P(),
            P(),
            P(),
        ),
        out_specs=(P(("rep", "fsdp"), "mp"), P(("rep", "fsdp"), "mp"), P(("rep", "fsdp", "mp"))),
        check_vma=False,
    )
```

```python
import math

import jax
import jax.numpy as jnp
from jax import lax
from jax.experimental import pallas as pl
from jax.experimental.pallas import tpu as pltpu
from jax.sharding import PartitionSpec as P

NT = 1000


norm_epsilon = 1e-06


def from_behind(value, axis, by):
    size = lax.axis_size(axis)
    pairs = [(i, i + by) for i in range(size) if 0 <= i + by < size]
    return lax.ppermute(value, axis, pairs)


def shifted(value, axis, by):
    size = lax.axis_size(axis)
    return lax.ppermute(value, axis, [(i, (i + by) % size) for i in range(size)])


def step_features(step_ids, feature_width):
    half_width = feature_width // 2
    frequency = jnp.exp(-math.log(10000.0) * jnp.arange(half_width, dtype=jnp.float32) / half_width)
    angles = step_ids.astype(jnp.float32)[:, None] * frequency[None, :]
    return jnp.concatenate([jnp.cos(angles), jnp.sin(angles)], axis=1).astype(jnp.bfloat16)


def lookup(step_table, block_ids):
    matches = block_ids[:, None] == jnp.arange(step_table.shape[0], dtype=jnp.int32)[None, :]
    return jnp.sum(jnp.where(matches, step_table[None, :], 0), axis=1)


def block_shares(step_ids):
    return ((step_ids.astype(jnp.float32) + 1.0) / (NT + 1.0))[:, None, None]


def modulate(full_rows, gain_vec, modulation):
    blocks = modulation.shape[0]
    values = full_rows.astype(jnp.float32)
    normed = values * lax.rsqrt(jnp.mean(values * values, axis=1, keepdims=True) + norm_epsilon)
    lifted = normed.reshape(blocks, -1, values.shape[1]) * gain_vec * (1.0 + modulation[:, None, :])
    return (normed, lifted.reshape(values.shape).astype(jnp.bfloat16))


def on_groups(
    noise_in,
    renoise,
    gen_step,
    noise_step,
    gen_weight,
    real_weight,
    fake_weight,
    gen_embed,
    real_embed,
    fake_embed,
    gen_gain,
    real_gain,
    fake_gain,
):
    devices = lax.axis_size("fsdp")
    quarter = devices // 4
    half = 2 * quarter
    position = lax.axis_index("fsdp")
    block_rows = noise_in.shape[0]
    half_width = noise_in.shape[1]
    model_width = gen_gain.shape[0]
    feature_width = gen_embed.shape[0]
    slice_rows = 4 * block_rows // devices
    group_role = (position >= quarter).astype(jnp.int32) + (position >= half).astype(jnp.int32)
    in_generator = group_role == 2
    slot_ids = jnp.arange(devices, dtype=jnp.int32)
    slot_role = (
        (slot_ids >= quarter).astype(jnp.int32) + (slot_ids >= half).astype(jnp.int32)
    ).reshape(devices, 1, 1)
    outgoing = jnp.where(
        slot_role == 2,
        gen_weight[None],
        jnp.where(slot_role == 0, real_weight[None], fake_weight[None]),
    )
    received = lax.all_to_all(outgoing, "fsdp", split_axis=0, concat_axis=0, tiled=True)
    weight_mine = received.reshape(model_width, half_width)
    embed_mine = jnp.where(
        group_role == 2, gen_embed, jnp.where(group_role == 0, real_embed, fake_embed)
    )
    gain_mine = jnp.where(
        group_role == 2, gen_gain, jnp.where(group_role == 0, real_gain, fake_gain)
    )
    partner_noise, partner_renoise = from_behind((noise_in, renoise), "fsdp", half)
    gen_ids = jnp.stack([position, (position + half) % devices])
    gen_mod = jnp.dot(
        step_features(lookup(gen_step, gen_ids), feature_width),
        embed_mine,
        preferred_element_type=jnp.float32,
    )
    gen_shares = block_shares(lookup(noise_step, gen_ids))
    gen_rows = jnp.concatenate([noise_in, partner_noise], axis=0)
    gen_noise = jnp.concatenate([renoise, partner_renoise], axis=0)
    gen_full = lax.all_gather(gen_rows, "mp", axis=1, tiled=True)

    def generate(operands):
        full_rows, own_rows, fresh_noise = operands
        normed, lifted = modulate(full_rows, gain_mine, gen_mod)
        latents = own_rows.astype(jnp.float32) + jnp.dot(
            lifted, weight_mine, preferred_element_type=jnp.float32
        )
        blended = (1.0 - gen_shares) * latents.reshape(
            2, block_rows, half_width
        ) + gen_shares * fresh_noise.astype(jnp.float32).reshape(2, block_rows, half_width)
        return (blended.reshape(2 * block_rows, half_width).astype(jnp.bfloat16), normed)

    def skip_generate(operands):
        return (
            jnp.zeros((2 * block_rows, half_width), jnp.bfloat16),
            jnp.zeros((2 * block_rows, model_width), jnp.float32),
        )

    gen_noised, gen_normed = lax.cond(
        in_generator, generate, skip_generate, (gen_full, gen_rows, gen_noise)
    )
    width_now = gen_noised.shape[1]
    pieces = (
        gen_noised.reshape(2, quarter, slice_rows, width_now)
        .transpose(1, 0, 2, 3)
        .reshape(quarter, 2 * slice_rows, width_now)
    )
    send_rows = jnp.concatenate(
        [pieces, pieces, jnp.zeros((half, 2 * slice_rows, width_now), jnp.bfloat16)], axis=0
    )
    arrived = lax.all_to_all(send_rows, "fsdp", split_axis=0, concat_axis=0, tiled=True)
    score_rows = arrived[half:].reshape(2 * half * slice_rows, width_now)
    gen_slots = jnp.arange(half, dtype=jnp.int32)
    score_ids = jnp.stack([gen_slots + half, gen_slots], axis=1).reshape(2 * half)
    score_mod = jnp.dot(
        step_features(lookup(noise_step, score_ids), feature_width),
        embed_mine,
        preferred_element_type=jnp.float32,
    )
    score_full = lax.all_gather(score_rows, "mp", axis=1, tiled=True)

    def assess(full_rows):
        normed, lifted = modulate(full_rows, gain_mine, score_mod)
        return jnp.dot(lifted, weight_mine, preferred_element_type=jnp.float32).astype(jnp.bfloat16)

    def skip_assess(full_rows):
        return jnp.zeros((2 * half * slice_rows, half_width), jnp.bfloat16)

    prediction = lax.cond(in_generator, skip_assess, assess, score_full)
    grouped = prediction.reshape(half, 2, slice_rows, half_width)
    by_owner = jnp.concatenate([grouped[:, 1], grouped[:, 0]], axis=0)
    returned = lax.all_to_all(by_owner, "fsdp", split_axis=0, concat_axis=0, tiled=True)
    real_block = returned[:quarter].reshape(block_rows, half_width).astype(jnp.float32)
    fake_block = returned[quarter:half].reshape(block_rows, half_width).astype(jnp.float32)
    own_share = block_shares(lookup(noise_step, position[None]))[0]
    own_grad = (own_share * (real_block - fake_block)).astype(jnp.bfloat16)
    handed = jnp.where(in_generator, gen_noised[block_rows:], own_grad)
    taken = shifted(handed, "fsdp", half)

    def reverse(operands):
        grad_rows, normed = operands
        backward = lax.dot_general(
            grad_rows, weight_mine, (((1,), (1,)), ((), ())), preferred_element_type=jnp.float32
        )
        scaled = backward.reshape(2, block_rows, model_width) * (1.0 + gen_mod[:, None, :])
        return jnp.sum(scaled.reshape(2 * block_rows, model_width) * normed, axis=0) / block_rows

    def skip_reverse(operands):
        return jnp.zeros((model_width,), jnp.float32)

    grad_rows = jnp.concatenate([own_grad, taken], axis=0)
    gain_term = lax.cond(in_generator, reverse, skip_reverse, (grad_rows, gen_normed))
    gain_grad = lax.psum_scatter(gain_term, ("fsdp", "mp"), scatter_dimension=0, tiled=True)
    noised_out = jnp.where(in_generator, gen_noised[:block_rows], taken)
    return (noised_out, own_grad, gain_grad)


def on_tiles(
    noise_in,
    renoise,
    gen_step,
    noise_step,
    gen_weight,
    real_weight,
    fake_weight,
    gen_embed,
    real_embed,
    fake_embed,
    gen_gain,
    real_gain,
    fake_gain,
):
    g = lax.axis_size("fsdp") // 2
    r, h = noise_in.shape
    d = 2 * h
    w = h // g
    t = g * r
    blocks = gen_step.shape[0]
    f32, bf16 = jnp.float32, jnp.bfloat16
    tail = 16
    span = range(g)

    def place():
        position, c = lax.axis_index("fsdp"), lax.axis_index("mp")
        return lax.div(position, g), lax.rem(position, g), c

    def flat(s_, q_, c_):
        return (s_ * g + q_) * 2 + c_

    every = [(s_, q_, c_) for s_ in (0, 1) for q_ in span for c_ in (0, 1)]

    def in_square(value, k):
        return lax.ppermute(value, "fsdp", [(i, i ^ k) for i in range(2 * g)])

    def across(value):
        return lax.ppermute(value, "fsdp", [(i, i ^ g) for i in range(2 * g)])

    def cores(value):
        return lax.ppermute(value, "mp", [(0, 1), (1, 0)])

    def turned(value):
        return lax.ppermute(value, ("fsdp", "mp"), [(flat(*i), flat(i[2], i[1], i[0])) for i in every])

    whole = pl.BlockSpec(memory_space=pltpu.VMEM)
    scalars = pl.BlockSpec(memory_space=pltpu.SMEM)

    def call(kernel, operands, outs, flops, scratch=(), in_scalars=0):
        moved = sum(o.size * o.dtype.itemsize for o in operands)
        return pl.pallas_call(
            kernel,
            in_specs=[scalars] * in_scalars + [whole] * (len(operands) - in_scalars),
            out_specs=[whole] * len(outs),
            out_shape=[jax.ShapeDtypeStruct(*o) for o in outs],
            scratch_shapes=list(scratch),
            compiler_params=pltpu.CompilerParams(vmem_limit_bytes=40 * 1024 * 1024),
            cost_estimate=pl.CostEstimate(flops=flops, bytes_accessed=moved, transcendentals=0),
        )(*operands)

    def rows_of(columns):
        return jnp.broadcast_to(columns, (t, 128)).T[:8]

    def columns_of(rows):
        return rows.T[:, :1]

    def pack(rows, store):
        high = rows.astype(bf16)
        rest = rows - high.astype(f32)
        middle = rest.astype(bf16)
        low = (rest - middle.astype(f32)).astype(bf16)
        line = lax.broadcasted_iota(jnp.int32, rows.shape, 0)
        mixed = jnp.where(line == 0, high.astype(f32), jnp.where(line == 1, middle.astype(f32), low.astype(f32)))
        mixed = jnp.where(line < 3, mixed, 0.0)
        store(jnp.concatenate([mixed, jnp.zeros_like(mixed)], axis=0).astype(bf16))

    def unpack(block):
        return jnp.sum(block.astype(f32), axis=0, keepdims=True)

    def share(steps, block):
        return (steps[block].astype(f32) + 1.0) / (NT + 1.0)

    def band(j):
        return slice(j * r, (j + 1) * r)

    def lanes(k):
        return pl.ds(pl.multiple_of(k * w, w), w)

    def scales_kernel(features, *refs):
        sources, out, held, sems = refs[:6], refs[6], refs[7:13], refs[13]
        s, _, _ = place()
        mine = pl.ds(pl.multiple_of(s * h, h), h)
        per = h // 128
        copies = [
            pltpu.make_async_copy(source.at[:, mine] if n < 3 else source, here, sems.at[n])
            for n, (source, here) in enumerate(zip(sources, held))
        ]
        for copy in copies:
            copy.start()
        for copy in copies:
            copy.wait()

        def gain(ref):
            return jnp.concatenate([ref[pl.ds(s * per + i, 1), :] for i in range(per)], axis=1)

        for n in range(3):
            steps = slice(0, blocks) if n == 0 else slice(blocks, 2 * blocks)
            mod = 1.0 + jnp.dot(features[steps, :], held[n][...], preferred_element_type=f32)
            if n == 0:
                out[3] = mod
            scale = mod * gain(held[3 + n])
            out[n] = -scale if n == 2 else scale

    gains = [v.reshape(-1, 128) for v in (gen_gain, real_gain, fake_gain)]
    scales = pl.pallas_call(
        scales_kernel,
        in_specs=[whole] + [pl.BlockSpec(memory_space=pltpu.HBM)] * 6,
        out_specs=whole,
        out_shape=jax.ShapeDtypeStruct((4, blocks, h), f32),
        scratch_shapes=[pltpu.VMEM((gen_embed.shape[0], h), bf16)] * 3
        + [pltpu.VMEM(v.shape, f32) for v in gains]
        + [pltpu.SemaphoreType.DMA((6,))],
        compiler_params=pltpu.CompilerParams(vmem_limit_bytes=40 * 1024 * 1024),
        cost_estimate=pl.CostEstimate(flops=6 * blocks * 128 * h, bytes_accessed=6 * 128 * h, transcendentals=0),
    )(
        step_features(jnp.concatenate([gen_step, noise_step]), gen_embed.shape[0]),
        gen_embed,
        real_embed,
        fake_embed,
        *gains,
    )

    depth = gen_weight.shape[0]
    fold = r // g
    shared = g // 2

    part_rows = depth // 2

    def rows_half(n):
        return pl.ds(pl.multiple_of(n * part_rows, 16), part_rows)

    def cut_gen_kernel(weight, *outs):
        _, q, _ = place()
        copy = lax.axis_index("rep")
        for k in span:
            if k < shared:
                outs[k][...] = weight[:, lanes(q ^ k)]
            else:
                outs[k][...] = weight[rows_half(copy), lanes(q ^ k)]

    def join_gen_kernel(*refs):
        copy = lax.axis_index("rep")
        n = g - shared
        for fetched, given, out in zip(refs[:n], refs[n : 2 * n], refs[2 * n :]):
            out[rows_half(copy), :] = fetched[...]
            out[rows_half(1 - copy), :] = given[...]

    def cut_score_kernel(real, fake, *outs):
        _, q, _ = place()
        for k in span:
            if k < shared:
                outs[k][0] = real[:, lanes(q ^ k)]
                outs[k][1] = fake[:, lanes(q ^ k)]
            else:
                for n, weight in enumerate((real, fake)):

                    @pl.when(lax.axis_index("rep") == n)
                    def _():
                        outs[k][...] = weight[:, lanes(q ^ k)]

    def cut_rows_kernel(rows, fresh, *outs):
        _, q, _ = place()
        for k in span:
            outs[k][0:r, :] = rows[...]
            for i in span:
                outs[k][r : r + fold, i * w : (i + 1) * w] = fresh[i * fold : (i + 1) * fold, lanes(q ^ k)]

    def swap_all(tile):
        counts = [v.size // (depth * w) for v in tile]

        def join_kernel(*refs):
            out, at = refs[-1], 0
            for ref, n in zip(refs[:-1], counts):
                for i in range(n):
                    out[at] = ref[i] if n > 1 else ref[...]
                    at += 1

        (joined,) = call(join_kernel, tile, [((sum(counts), depth, w), bf16)], depth * w)
        return cores(joined)

    x_turned, fresh_turned = turned(noise_in), turned(renoise)
    gen_sent = call(cut_gen_kernel, [gen_weight], [((depth, w), bf16)] * shared + [((part_rows, w), bf16)] * (g - shared), depth * h)
    gen_mine = [gen_sent[0]] + [in_square(gen_sent[k], k) for k in range(g - 1, 0, -1)][::-1]
    x_sent = call(cut_rows_kernel, [x_turned, fresh_turned], [((r + fold, h), bf16)] * g, r * h)
    x_sent = list(x_sent)
    *fetched, x_sent[0] = lax.optimization_barrier((*gen_mine[shared:], x_sent[0]))
    given = [lax.ppermute(v, "rep", [(0, 1), (1, 0)]) for v in fetched]
    gen_mine[shared:] = call(join_gen_kernel, fetched + given, [((depth, w), bf16)] * (g - shared), depth * w)
    x = [x_sent[0]] + [in_square(x_sent[k], k) for k in range(g - 1, 0, -1)][::-1]
    gen_swap, x[1], scales = lax.optimization_barrier((gen_mine, x[1], scales))
    gen_other = [cores(v) for v in gen_swap]
    real_weight, fake_weight, _ = lax.optimization_barrier((real_weight, fake_weight, x_turned))
    score_sent = call(
        cut_score_kernel,
        [real_weight, fake_weight],
        [((2, depth, w), bf16)] * shared + [((depth, w), bf16)] * (g - shared),
        2 * depth * h,
    )
    score_mine = [score_sent[0]] + [in_square(score_sent[k], k) for k in range(1, g)]

    def generate_kernel(steps, *refs):
        xs, scale, own, other = refs[:g], refs[g], refs[g + 1 : 2 * g + 1], refs[2 * g + 1 : 3 * g + 1]
        keep, away, sums, base, lift = refs[3 * g + 1 :]
        s, q, c = place()
        totals = []
        for j in span:
            wide = xs[j][0:r, :].astype(f32)
            totals.append(jnp.sum(wide * wide, axis=1, keepdims=True))
            lift[band(j), :] = (wide * scale[0, pl.ds(c * g + (q ^ j), 1), :]).astype(bf16)
            part = share(steps, c * g + (q ^ j))
            for i in span:
                some = slice(i * fold, (i + 1) * fold)
                base[j * r + i * fold : j * r + (i + 1) * fold, :] = (1.0 - part) * xs[j][some, lanes(q)].astype(
                    f32
                ) + part * xs[j][r : r + fold, i * w : (i + 1) * w].astype(f32)
        here = jnp.zeros((t, w), f32)
        there = jnp.zeros((t, w), f32)
        for k in span:
            part = lift[:, lanes(q ^ k)]
            here = here + jnp.dot(part, own[k][...], preferred_element_type=f32)
            there = there + jnp.dot(part, other[k][...], preferred_element_type=f32)
        stays = s == c
        keep[...] = jnp.where(stays, here, there)
        away[0:t, :] = jnp.where(stays, there, here).astype(bf16)
        rows = rows_of(jnp.concatenate(totals, axis=0))
        sums[...] = rows

        def store(value):
            away[t : t + tail, 0:t] = value

        if w > t:
            away[t : t + tail, t:] = jnp.zeros((tail, w - t), bf16)
        pack(rows, store)

    keep, away, x_sums, base = call(
        generate_kernel,
        [noise_step] + x + [scales] + gen_mine + gen_other,
        [((t, w), f32), ((t + tail, w), bf16), ((8, t), f32), ((t, w), f32)],
        4 * t * h * w,
        [pltpu.VMEM((t, h), bf16)],
        in_scalars=1,
    )

    def inverse_rms(sums, came):
        total = sums[...] + unpack(came[t : t + tail, 0:t])
        return columns_of(lax.rsqrt(total / d + norm_epsilon))

    def blend_kernel(steps, keep, came, sums, base, noised, root):
        _, q, c = place()
        inverse = inverse_rms(sums, came)
        root[...] = jnp.broadcast_to(inverse, (t, 128))
        for j in span:
            stay = 1.0 - share(steps, c * g + (q ^ j))
            made = keep[band(j), :] + came[band(j), :].astype(f32)
            noised[band(j), :] = (base[band(j), :] + (stay * inverse[band(j), :]) * made).astype(bf16)

    score_mine += [lax.ppermute(v, "rep", [(0, 1), (1, 0)]) for v in score_mine[shared:g]]
    came, score_mine[shared] = lax.optimization_barrier((across(away), score_mine[shared]))
    noised_mine, x_root = call(
        blend_kernel,
        [noise_step, keep, came, x_sums, base],
        [((t, w), bf16), ((t, 128), f32)],
        10 * t * w,
        in_scalars=1,
    )
    noised_last, score_mine[1] = lax.optimization_barrier((noised_mine, score_mine[1]))
    noised = [noised_mine, in_square(noised_last, 1)] + [in_square(noised_mine, k) for k in range(2, g)]

    tiles = len(score_mine)

    def score_product(lifts, tile):
        copy = lax.axis_index("rep")
        total = jnp.zeros((t, w), f32)
        for k in span:
            columns = slice(k * w, (k + 1) * w)
            if k < shared:
                pairs = [(tile[k][0], 0), (tile[k][1], 1)]
            else:
                pairs = [(tile[k][...], copy), (tile[k + g - shared][...], 1 - copy)]
            for part, n in pairs:
                total = total + jnp.dot(lifts[n, :, columns], part, preferred_element_type=f32)
        return total

    def score_kernel(*refs):
        ns, scale, own = refs[:g], refs[g], refs[g + 1 : g + 1 + tiles]
        gap, away, sums, lifts = refs[g + 1 + tiles :]
        _, q, c = place()
        totals = [jnp.zeros((r, 1), f32) for _ in span]
        for k in span:
            columns = slice(k * w, (k + 1) * w)
            for j in span:
                block = pl.ds(c * g + (q ^ j), 1)
                wide = ns[k][band(j ^ k), :].astype(f32)
                totals[j] = totals[j] + jnp.sum(wide * wide, axis=1, keepdims=True)
                for n in (0, 1):
                    lifts[n, band(j), columns] = (wide * scale[1 + n, block, lanes(q ^ k)]).astype(bf16)
        here = score_product(lifts, own)
        gap[...] = here
        away[0:t, :] = here.astype(bf16)
        rows = rows_of(jnp.concatenate(totals, axis=0))
        sums[...] = rows
        if w > t:
            away[t : t + tail, t:] = jnp.zeros((tail, w - t), bf16)

        def store(value):
            away[t : t + tail, 0:t] = value

        pack(rows, store)

    noised_home, noised[2] = lax.optimization_barrier((noised_mine, noised[2]))
    gap_here, away_here, noised_sums, lifts = call(
        score_kernel,
        noised + [scales] + score_mine,
        [((t, w), f32), ((t + tail, w), bf16), ((8, t), f32), ((2, t, h), bf16)],
        4 * t * h * w,
    )
    came_here = across(away_here)
    noised_owned, score_mine, gap_here = lax.optimization_barrier((turned(noised_home), score_mine, gap_here))
    score_mine, _ = lax.optimization_barrier((score_mine, cores(noised_sums)))
    score_other = swap_all(score_mine)

    def score_rest_kernel(lifts, other, gap, away):
        there = score_product(
            lifts,
            [(other[2 * k], other[2 * k + 1]) for k in range(shared)]
            + [other[shared + k] for k in range(shared, tiles)],
        )
        gap[...] = there
        away[...] = there.astype(bf16)

    gap_there, away_there = call(
        score_rest_kernel, [lifts, score_other], [((t, w), f32), ((t, w), bf16)], 4 * t * h * w
    )
    came_there = across(away_there)

    def gradient(steps, gap, came, inverse, grad, outs):
        _, q, c = place()
        for j in span:
            part = share(steps, c * g + (q ^ j))
            value = (part * inverse[band(j), :]) * (gap[band(j), :] + came[band(j), :].astype(f32))
            grad[band(j), :] = value.astype(bf16)
            outs[j][0:r, :] = value.astype(bf16)

    def gain_sums(grad, tile, xs, root, scale):
        _, q, c = place()
        sums = []
        for k in span:
            back = lax.dot_general(grad[...], tile[k][...], (((1,), (1,)), ((), ())), preferred_element_type=f32)
            total = jnp.zeros((1, w), f32)
            for j in span:
                normed = xs[j][0:r, lanes(q ^ k)].astype(f32) * root[band(j), :1]
                summed = jnp.sum(back[band(j), :] * normed, axis=0, keepdims=True)
                total = total + summed * scale[3, pl.ds(c * g + (q ^ j), 1), lanes(q ^ k)]
            sums.append(total)
        return sums

    def backward_kernel(steps, gap, came, sums, root, scale, owned, *refs):
        xs, own, outs, (noised_root, partial, grad) = refs[:g], refs[g : 2 * g], refs[2 * g : 3 * g], refs[3 * g :]
        inverse = inverse_rms(sums, came)
        noised_root[...] = jnp.broadcast_to(inverse, (t, 128))
        gradient(steps, gap, came, inverse, grad, outs)
        for k, total in enumerate(gain_sums(grad, own, xs, root, scale)):
            partial[k : k + 1, :] = total
            outs[k][r : 2 * r, :] = owned[band(k), :]

    *sent_here, noised_root, partial = call(
        backward_kernel,
        [noise_step, gap_here, came_here, noised_sums, x_root, scales, noised_owned] + x + gen_mine,
        [((2 * r, w), bf16)] * g + [((t, 128), f32), ((8, w), f32)],
        2 * t * h * w,
        [pltpu.VMEM((t, w), bf16)],
        in_scalars=1,
    )
    arrived_here = [sent_here[0]] + [in_square(sent_here[k], k) for k in range(1, g)]

    def backward_rest_kernel(steps, gap, came, noised_root, partial, root, scale, *refs):
        xs, other, outs, (grad,) = refs[:g], refs[g : 2 * g], refs[2 * g : 3 * g], refs[3 * g :]
        gradient(steps, gap, came, noised_root[:, :1], grad, outs)
        for k, total in enumerate(gain_sums(grad, other, xs, root, scale)):

            def store(value):
                outs[k][r : r + tail, :] = value

            pack(jnp.broadcast_to((total + partial[k : k + 1, :]) / r, (8, w)), store)

    sent_there = call(
        backward_rest_kernel,
        [noise_step, gap_there, came_there, noised_root, partial, x_root, scales] + x + gen_other,
        [((r + tail, w), bf16)] * g,
        2 * t * h * w,
        [pltpu.VMEM((t, w), bf16)],
        in_scalars=1,
    )
    arrived_there = [sent_there[0]] + [in_square(sent_there[k], k) for k in range(1, g)]

    def gather_kernel(*refs):
        a, b, (here, there, gains, noised) = refs[:g], refs[g : 2 * g], refs[2 * g :]
        _, q, _ = place()
        total = jnp.zeros((1, w), f32)
        for k in span:
            here[:, lanes(q ^ k)] = a[k][0:r, :]
            noised[:, lanes(q ^ k)] = a[k][r : 2 * r, :]
            there[0:r, lanes(q ^ k)] = b[k][0:r, :]
            total = total + unpack(b[k][r : r + tail, :])
        gains[...] = total

        def store(value):
            there[r : r + tail, :w] = value

        pack(jnp.broadcast_to(total, (8, w)), store)
        there[r : r + tail, w:] = jnp.zeros((tail, h - w), bf16)

    here, there, gains, noised_out = call(
        gather_kernel,
        arrived_here + arrived_there,
        [((r, h), bf16), ((r + tail, h), bf16), ((1, w), f32), ((r, h), bf16)],
        t * h,
    )
    other_core = cores(there)

    def finish_kernel(here, gains, came, grad, gain):
        s, _, c = place()
        grad[...] = jnp.where(s == c, here[...], came[0:r, :])
        both = gains[...] + unpack(came[r : r + tail, :w])
        gain[...] = jnp.where(c == 0, both[:, : w // 2], both[:, w // 2 :])

    latent_grad, gain = call(
        finish_kernel, [here, gains, other_core], [((r, h), bf16), ((1, w // 2), f32)], r * h
    )
    return (noised_out, latent_grad, gain[0])


def solution(mesh):
    positions = mesh.shape["fsdp"]
    on_device = on_tiles if (positions, mesh.shape["rep"], mesh.shape["mp"]) == (8, 2, 2) else on_groups
    return jax.shard_map(
        on_device,
        mesh=mesh,
        in_specs=(
            P(("rep", "fsdp"), "mp"),
            P(("rep", "fsdp"), "mp"),
            P("rep"),
            P("rep"),
            P("fsdp", "mp"),
            P("fsdp", "mp"),
            P("fsdp", "mp"),
            P(),
            P(),
            P(),
            P(),
            P(),
            P(),
        ),
        out_specs=(P(("rep", "fsdp"), "mp"), P(("rep", "fsdp"), "mp"), P(("rep", "fsdp", "mp"))),
        check_vma=False,
    )
```
